32 devices in a mesh: seq: 8 (over z, core), tp: 4 (over y, x).
Axes of the slice: x: 2, y: 2, z: 4, core: 2. Of those that a mesh axis runs over, the one named last changes fastest.
Arguments:
- tokens: bfloat16 [24, 1024, 1600], P('seq', 'tp'), may hold values from -6 to 6
- positions: int32 [24, 1024], P('seq'), may hold values from 0 to 1023, as said below
- ln1_gain: bfloat16 [1600], replicated, may hold values from 0.25 to 1.75
- ln1_bias: bfloat16 [1600], replicated, may hold values from -1.5 to 1.5
- query_key_value_weight: bfloat16 [1600, 4800], P('seq', 'tp'), may hold values from -0.15625 to 0.15625
- qv_bias: bfloat16 [2, 1600], replicated, may hold values from -3 to 3
- attention_output_weight: bfloat16 [1600, 1600], P('seq', 'tp'), may hold values from -0.625 to 0.625
- attention_output_bias: bfloat16 [1600], replicated, may hold values from -1.5 to 1.5
- ln2_gain: bfloat16 [1600], replicated, may hold values from 0.25 to 1.75
- ln2_bias: bfloat16 [1600], replicated, may hold values from -1.5 to 1.5
- expand_weight: bfloat16 [1600, 6400], P('seq', 'tp'), may hold values from -0.15625 to 0.15625
- expand_bias: bfloat16 [6400], replicated, may hold values from -3 to 3
- contract_weight: bfloat16 [6400, 1600], P('tp', 'seq'), may hold values from -0.078125 to 0.078125
- contract_bias: bfloat16 [1600], replicated, may hold values from -1.5 to 1.5
- cotangent: bfloat16 [24, 1024, 1600], P('seq', 'tp'), may hold values from -6 to 6
Outputs:
- layer_out: bfloat16 [24, 1024, 1600], P('seq', 'tp')
- input_grad: bfloat16 [24, 1024, 1600], P('seq', 'tp')
- ln1_gain_grad: float32 [1600], replicated
- ln1_bias_grad: float32 [1600], replicated
- qkv_weight_grad: float32 [1600, 4800], P('seq', 'tp')
- qv_bias_grad: float32 [2, 1600], replicated
- out_weight_grad: float32 [1600, 1600], P('seq', 'tp')
- out_bias_grad: float32 [1600], replicated
- ln2_gain_grad: float32 [1600], replicated
- ln2_bias_grad: float32 [1600], replicated
- fc_weight_grad: float32 [1600, 6400], P('seq', 'tp')
- fc_bias_grad: float32 [6400], replicated
- proj_weight_grad: float32 [6400, 1600], P('tp', 'seq')
- proj_bias_grad: float32 [1600], replicated
The draws below stay inside these ranges and needn't reach their ends.
Inputs may be any that keep to these rules, and one draw needn't show every extreme that they name: `positions`: each row is a permutation of the places 0 to 1023. With n the devices of tp, the places fall into 2 n blocks of 128; the 1024 / n stored tokens that tp index t holds are, in order, all of some block b and then all of block 2 n - 1 - b, ascending within each; b differs between the indices of tp and is drawn for each sequence.
All inputs are finite; a program needn't handle non-finite values.
Results may differ from the reference program's by a relative error of at most 0.0095.
Values may be sent and summed in bfloat16 or wider, within the bound.
A program may use at most 384 MiB of HBM per device.

```python
from functools import partial
import jax
import jax.numpy as jnp
from jax import lax

D = 1600
HEADS = 25
HEAD = 64
FF = 6400
LEN = 1024
SEQ_DEV = 3
NSEQ = 24
SPAN = 128
N_SEQ = 8


def draw_positions(key, part):
    key = jax.random.fold_in(key, 7)
    device_count = LEN // (2 * SPAN)
    seq_keys = jax.random.split(key, NSEQ)
    order = jax.vmap(lambda single: jax.random.permutation(single, device_count))(seq_keys).astype(jnp.int32)
    blocks = jnp.stack([order, 2 * device_count - 1 - order], axis=2)
    within = jnp.arange(SPAN, dtype=jnp.int32)
    placed = blocks[..., None] * SPAN + within
    return placed.reshape(NSEQ, LEN).astype(jnp.int32)


def block_levels(own_key, dims, cuts, least, largest):
    loudness, own = 1.0, jax.random.fold_in(own_key, 6)
    for dim, blocks in cuts:
        heights = jnp.exp(jax.random.uniform(jax.random.fold_in(own, dim), (blocks,), jnp.float32, least / len(cuts), largest / len(cuts)))
        loudness = loudness * jnp.repeat(heights, dims[dim] // blocks).reshape([-1 if axis == dim else 1 for axis in range(len(dims))])
    return loudness


def normal_values(own_key, extent, scale, most, cuts=(), kind=jnp.bfloat16):
    factor_of = block_levels(own_key, extent, cuts, -0.22, 0.18) if cuts else 1.0
    values = jax.random.normal(own_key, extent, jnp.float32) * scale * factor_of
    return jnp.minimum(jnp.maximum(values, -most), most).astype(kind)


def setup_inputs(seed: int = 0) -> dict:
    arg_keys = jax.random.split(jax.random.key(seed), 16)
    return {
        "tokens": normal_values(arg_keys[0], (NSEQ, LEN, D), 1.0, 6.0, ((0, 8), (1, 4))),
        "positions": draw_positions(jax.random.fold_in(arg_keys[15], 71), 0),
        "ln1_gain": jnp.clip(1.0 + 0.15 * jax.random.normal(arg_keys[2], (D,), jnp.float32), 0.25, 1.75).astype(jnp.bfloat16),
        "ln1_bias": normal_values(arg_keys[3], (D,), 0.3, 1.5),
        "query_key_value_weight": normal_values(arg_keys[4], (D, 3 * D), D ** -0.5, 0.15625, ((0, 8), (1, 4))),
        "qv_bias": normal_values(arg_keys[5], (2, D), 0.5, 3.0),
        "attention_output_weight": normal_values(arg_keys[6], (D, D), (D // 16) ** -0.5, 0.625, ((0, 8), (1, 4))),
        "attention_output_bias": normal_values(arg_keys[7], (D,), 0.3, 1.5),
        "ln2_gain": jnp.clip(1.0 + 0.15 * jax.random.normal(arg_keys[8], (D,), jnp.float32), 0.25, 1.75).astype(jnp.bfloat16),
        "ln2_bias": normal_values(arg_keys[9], (D,), 0.3, 1.5),
        "expand_weight": normal_values(arg_keys[10], (D, FF), D ** -0.5, 0.15625, ((0, 8), (1, 4))),
        "expand_bias": normal_values(arg_keys[11], (FF,), 0.5, 3.0),
        "contract_weight": normal_values(arg_keys[12], (FF, D), FF ** -0.5, 0.078125, ((0, 4), (1, 8))),
        "contract_bias": normal_values(arg_keys[13], (D,), 0.3, 1.5),
        "cotangent": normal_values(arg_keys[14], (NSEQ, LEN, D), 1.0, 6.0, ((0, 8), (1, 4))),
    }


highest_precision = lax.Precision.HIGHEST
epsilon = 1e-05

@jax.custom_vjp
def low(v):
    return lax.optimization_barrier(v.astype(jnp.bfloat16)).astype(jnp.float32)

@jax.custom_vjp
def lower_precision_backward(v):
    return v

def low_keep(v):
    return (low(v), None)

def low_pass(kept, grad):
    return (grad,)

def back_keep(v):
    return (v, None)

def back_low(kept, grad):
    return (low(grad),)
low.defvjp(low_keep, low_pass)
lower_precision_backward.defvjp(back_keep, back_low)

def layer_norm(values, norm_gain, norm_shift):
    centred = values - lax.optimization_barrier(jnp.mean(values, -1, keepdims=True))
    spread = lax.optimization_barrier(jnp.mean(centred * centred, -1, keepdims=True))
    return centred * lax.rsqrt(spread + epsilon) * norm_gain + norm_shift

def attend(inputs):
    queries, keys_in, values_in, places = inputs
    row_count = queries.shape[0]
    q_heads = queries.reshape(row_count, HEADS, HEAD)
    k_heads = keys_in.reshape(row_count, HEADS, HEAD)
    v_heads = values_in.reshape(row_count, HEADS, HEAD)
    scores = lower_precision_backward(jnp.einsum('qhe,khe->hqk', q_heads, k_heads, precision=highest_precision) * HEAD ** (-0.5))
    visible = places[None, None, :] <= places[None, :, None]
    scores = jnp.where(visible, scores, -1e+30)
    row_max = lax.optimization_barrier(jnp.max(scores, -1, keepdims=True))
    exponent = jnp.exp(scores - row_max)
    weights = low(exponent / lax.optimization_barrier(jnp.sum(exponent, -1, keepdims=True)))
    mixed = jnp.einsum('hqk,khe->qhe', weights, v_heads, precision=highest_precision)
    return mixed.reshape(row_count, HEADS * HEAD)

def group_block(params, batch):
    inputs, places = batch
    ln1_gain, ln1_bias, query_key_value_weight, qv_bias, attention_output_weight, attention_output_bias, ln2_gain, ln2_bias, expand_weight, expand_bias, contract_weight, contract_bias = params
    normalized_rows = low(layer_norm(inputs, ln1_gain, ln1_bias))
    contracted_output = jnp.einsum('wjv,vp->wjp', normalized_rows, query_key_value_weight, precision=highest_precision)
    queries = low(lower_precision_backward(contracted_output[..., :D] + qv_bias[0]))
    keys_in = low(lower_precision_backward(contracted_output[..., D:2 * D]))
    values_in = low(lower_precision_backward(contracted_output[..., 2 * D:] + qv_bias[1]))
    mixed = lax.map(jax.checkpoint(attend), (queries, keys_in, values_in, places))
    head_outputs = low(lower_precision_backward(mixed))
    branch_output = jnp.einsum('wjv,vp->wjp', head_outputs, attention_output_weight, precision=highest_precision) + attention_output_bias
    residual = inputs + lower_precision_backward(branch_output)
    second_normalized = low(layer_norm(residual, ln2_gain, ln2_bias))
    preactivation = lower_precision_backward(jnp.einsum('iyg,gn->iyn', second_normalized, expand_weight, precision=highest_precision) + expand_bias)
    activated_hidden = low(jax.nn.gelu(preactivation, approximate=True))
    feedforward_output = jnp.einsum('btj,jn->btn', activated_hidden, contract_weight, precision=highest_precision) + contract_bias
    return residual + lower_precision_backward(feedforward_output)

def reference(tokens, positions, ln1_gain, ln1_bias, query_key_value_weight, qv_bias, attention_output_weight, attention_output_bias, ln2_gain, ln2_bias, expand_weight, expand_bias, contract_weight, contract_bias, cotangent):
    params = tuple((argument.astype(jnp.float32) for argument in (ln1_gain, ln1_bias, query_key_value_weight, qv_bias, attention_output_weight, attention_output_bias, ln2_gain, ln2_bias, expand_weight, expand_bias, contract_weight, contract_bias)))

    def forward(inputs, *weights):
        grouped = inputs.reshape(N_SEQ, SEQ_DEV, LEN, D)
        places = positions.reshape(N_SEQ, SEQ_DEV, LEN)
        result = lax.map(jax.checkpoint(partial(group_block, weights)), (grouped, places))
        return result.reshape(NSEQ, LEN, D)
    layer, pullback = jax.vjp(forward, tokens.astype(jnp.float32), *params)
    gradients = pullback(cotangent.astype(jnp.float32))
    return (layer.astype(jnp.bfloat16), gradients[0].astype(jnp.bfloat16), gradients[1], gradients[2], gradients[3], gradients[4], gradients[5], gradients[6], gradients[7], gradients[8], gradients[9], gradients[10], gradients[11], gradients[12])
```

```python
import functools
import jax
import jax.numpy as jnp
from jax import lax
from jax.experimental import pallas as pl
from jax.experimental.pallas import tpu as pltpu
from jax.sharding import PartitionSpec as P

HEADS = 25
HEAD = 64
LANES = 128
TILE = 256
epsilon = 1e-05
F32 = jnp.float32
BF16 = jnp.bfloat16
NN = (((1,), (0,)), ((), ()))
NT = (((1,), (1,)), ((), ()))
TN = (((0,), (0,)), ((), ()))


def dot(left, right, dims=NN):
    return lax.dot_general(left, right, dims, preferred_element_type=F32)


def load_blocks(place_ref, span, count, source, target):
    for n in range(count):
        rows = pl.ds(pl.multiple_of(place_ref[n] * span, span), span)
        target[rows, :] = source(n)


def attend_forward(span, pieces, odd, place_ref, qkv_ref, *refs):
    out_refs, lse_ref = refs[:pieces], refs[pieces]
    queries, keys, values, mixed = refs[pieces + 1 :]
    pair, pairs = pl.program_id(0), pl.num_programs(0)
    for part, target in enumerate((queries, keys, values)):
        columns = slice(part * LANES, (part + 1) * LANES)
        load_blocks(
            place_ref, span, 2 * pieces, lambda n: qkv_ref[n * span : (n + 1) * span, columns], target
        )
    length = queries.shape[0]

    def one_head(head):
        lane = lax.broadcasted_iota(jnp.int32, (TILE, LANES), 1)
        mine = (lane // HEAD) == head
        for first in range(0, length, TILE):
            last = first + TILE
            query = jnp.where(mine, queries[first:last, :] * BF16(HEAD**-0.5), BF16(0))
            scores = dot(query, keys[0:last, :], NT)
            row = lax.broadcasted_iota(jnp.int32, (TILE, TILE), 0)
            column = lax.broadcasted_iota(jnp.int32, (TILE, TILE), 1)
            corner = jnp.where(column <= row, scores[:, first:last], -1e30)
            scores = corner if first == 0 else jnp.concatenate([scores[:, :first], corner], axis=1)
            row_max = jnp.max(scores, 1, keepdims=True)
            weights = jnp.exp(scores - row_max)
            total = jnp.sum(weights, 1, keepdims=True)
            part = dot(weights.astype(BF16), values[0:last, :]) / total
            lse_ref[0, head, first:last] = (row_max + jnp.log(total))[:, 0]
            if head == 0:
                mixed[first:last, :] = jnp.where(mine, part, 0.0).astype(BF16)
            else:
                mixed[first:last, :] = jnp.where(mine, part.astype(BF16), mixed[first:last, :])

    one_head(0)
    if odd:
        pl.when(pair < pairs - 1)(lambda: one_head(1))
    else:
        one_head(1)
    for piece in range(pieces):
        for half in range(2):
            rows = pl.ds(pl.multiple_of(place_ref[2 * piece + half] * span, span), span)
            out_refs[piece][half * span : (half + 1) * span, :] = mixed[rows, :]


def attend_backward(span, pieces, odd, place_ref, qkv_ref, *refs):
    grad_refs, lse_ref, out_ref = refs[:pieces], refs[pieces], refs[pieces + 1]
    queries, keys, values, grads, query_grad, key_sum, value_sum = refs[pieces + 2 :]
    pair, pairs = pl.program_id(0), pl.num_programs(0)
    for part, target in enumerate((queries, keys, values)):
        columns = slice(part * LANES, (part + 1) * LANES)
        load_blocks(
            place_ref, span, 2 * pieces, lambda n: qkv_ref[n * span : (n + 1) * span, columns], target
        )
    load_blocks(
        place_ref,
        span,
        2 * pieces,
        lambda n: grad_refs[n // 2][(n % 2) * span : (n % 2 + 1) * span, :],
        grads,
    )
    length = queries.shape[0]

    def one_head(head):
        lane = lax.broadcasted_iota(jnp.int32, (TILE, LANES), 1)
        mine = (lane // HEAD) == head
        for first in reversed(range(0, length, TILE)):
            last = first + TILE
            query = jnp.where(mine, queries[first:last, :] * BF16(HEAD**-0.5), BF16(0))
            grad = jnp.where(mine, grads[first:last, :], BF16(0))
            scores = dot(query, keys[0:last, :], NT)
            row = lax.broadcasted_iota(jnp.int32, (TILE, TILE), 0)
            column = lax.broadcasted_iota(jnp.int32, (TILE, TILE), 1)
            corner = jnp.where(column <= row, scores[:, first:last], -1e30)
            scores = corner if first == 0 else jnp.concatenate([scores[:, :first], corner], axis=1)
            weights = jnp.exp(scores - lse_ref[0, head, first:last][:, None])
            prob_grad = dot(grad, values[0:last, :], NT)
            product = weights * prob_grad
            inner = jnp.sum(product, 1, keepdims=True)
            score_grad = (product - weights * inner).astype(BF16)
            rounded = weights.astype(BF16)
            part = (dot(score_grad, keys[0:last, :]) * HEAD**-0.5).astype(BF16)
            key_part = dot(query, score_grad, TN)
            value_part = dot(grad, rounded, TN)
            if head == 0 and last == length:
                key_sum[...] = key_part
                value_sum[...] = value_part
            else:
                key_sum[:, 0:last] += key_part
                value_sum[:, 0:last] += value_part
            if head == 0:
                query_grad[first:last, :] = jnp.where(mine, part, BF16(0))
            else:
                query_grad[first:last, :] = jnp.where(mine, part, query_grad[first:last, :])

    one_head(0)
    if odd:
        pl.when(pair < pairs - 1)(lambda: one_head(1))
    else:
        one_head(1)
    keys[...] = key_sum[...].T.astype(BF16)
    values[...] = value_sum[...].T.astype(BF16)
    for n in range(2 * pieces):
        rows = pl.ds(pl.multiple_of(place_ref[n] * span, span), span)
        target = slice(n * span, (n + 1) * span)
        out_ref[target, 0:LANES] = query_grad[rows, :]
        out_ref[target, LANES : 2 * LANES] = keys[rows, :]
        out_ref[target, 2 * LANES :] = values[rows, :]


def call_forward(places, qkv, span, heads):
    length, width = qkv.shape
    pairs, pieces = width // (3 * LANES), length // (2 * span)
    return pl.pallas_call(
        functools.partial(attend_forward, span, pieces, heads % 2 == 1),
        grid_spec=pltpu.PrefetchScalarGridSpec(
            num_scalar_prefetch=1,
            grid=(pairs,),
            in_specs=[pl.BlockSpec((length, 3 * LANES), lambda j, p: (0, j))],
            out_specs=[pl.BlockSpec((2 * span, LANES), lambda j, p: (0, j))] * pieces
            + [pl.BlockSpec((1, 2, length), lambda j, p: (j, 0, 0))],
            scratch_shapes=[pltpu.VMEM((length, LANES), BF16)] * 4,
        ),
        out_shape=[jax.ShapeDtypeStruct((2 * span, pairs * LANES), BF16)] * pieces
        + [jax.ShapeDtypeStruct((pairs, 2, length), F32)],
        compiler_params=pltpu.CompilerParams(vmem_limit_bytes=40 * 2**20),
        cost_estimate=pl.CostEstimate(
            flops=heads * length * length * 5 * 256,
            bytes_accessed=4 * length * width,
            transcendentals=heads * length * length,
        ),
        name="attend_forward",
    )(places, qkv)


def call_backward(places, qkv, grads, lse, span, heads):
    length, width = qkv.shape
    pairs, pieces = width // (3 * LANES), length // (2 * span)
    return pl.pallas_call(
        functools.partial(attend_backward, span, pieces, heads % 2 == 1),
        grid_spec=pltpu.PrefetchScalarGridSpec(
            num_scalar_prefetch=1,
            grid=(pairs,),
            in_specs=[pl.BlockSpec((length, 3 * LANES), lambda j, p: (0, j))]
            + [pl.BlockSpec((2 * span, LANES), lambda j, p: (0, j))] * pieces
            + [pl.BlockSpec((1, 2, length), lambda j, p: (j, 0, 0))],
            out_specs=pl.BlockSpec((length, 3 * LANES), lambda j, p: (0, j)),
            scratch_shapes=[pltpu.VMEM((length, LANES), BF16)] * 5
            + [pltpu.VMEM((LANES, length), F32)] * 2,
        ),
        out_shape=jax.ShapeDtypeStruct(qkv.shape, BF16),
        compiler_params=pltpu.CompilerParams(vmem_limit_bytes=40 * 2**20),
        cost_estimate=pl.CostEstimate(
            flops=heads * length * length * 8 * 256,
            bytes_accessed=6 * length * width,
            transcendentals=heads * length * length,
        ),
        name="attend_backward",
    )(places, qkv, *grads, lse)


def statistics(values):
    centred = values - jnp.mean(values, -1, keepdims=True)
    spread = jnp.mean(centred * centred, -1, keepdims=True)
    inverse = lax.rsqrt(spread + epsilon)
    return centred * inverse, inverse


def norm_forward(values, gain, shift):
    return (statistics(values)[0] * gain + shift).astype(BF16)


def norm_backward(values, gain, grad):
    normal, inverse = statistics(values)
    scaled = grad * gain
    spread = jnp.mean(scaled * normal, -1, keepdims=True)
    result = inverse * (scaled - jnp.mean(scaled, -1, keepdims=True) - normal * spread)
    return result, jnp.sum(grad * normal, 0), jnp.sum(grad, 0)


def gelu_pair(u):
    scale = 0.7978845608028654
    inner = jnp.tanh(scale * (u + 0.044715 * (u * u * u)))
    value = 0.5 * u * (1.0 + inner)
    slope = 0.5 * (1.0 + inner) + 0.5 * u * (1.0 - inner * inner) * scale * (1.0 + 0.134145 * (u * u))
    return value, slope


def body(
    seq_count,
    tp_count,
    tokens,
    positions,
    ln1_gain,
    ln1_bias,
    query_key_value_weight,
    qv_bias,
    attention_output_weight,
    attention_output_bias,
    ln2_gain,
    ln2_bias,
    expand_weight,
    expand_bias,
    contract_weight,
    contract_bias,
    cotangent,
):
    devices = seq_count * tp_count
    both = ("seq", "tp")
    t = lax.axis_index("tp")
    core = lax.axis_index("seq") % 2
    core_bit = tp_count
    tp_bits = [1 << k for k in range(tp_count.bit_length() - 1)]
    high = tp_bits[-1]
    ff_bits = tp_bits[:-1] + [core_bit]
    chunks, rows, width = tokens.shape
    span = rows // 2
    length = rows * tp_count
    group_heads = -(-HEADS // tp_count)
    group = group_heads * HEAD
    pairs = -(-group_heads // 2)
    padded = pairs * LANES
    hidden = expand_weight.shape[1]
    peers = t ^ jnp.arange(tp_count)

    def swap(value, mask):
        return lax.ppermute(value, both, [(i, i ^ mask) for i in range(devices)])

    def gather_tp(value):
        if tp_count != 4:
            pieces = [value]
            for bit in tp_bits:
                pieces += [swap(piece, bit) for piece in pieces]
            return jnp.concatenate(pieces, 0)
        one, two = swap(value, 1), swap(value, 2)
        return jnp.concatenate([value, one, two, swap(one[:span], 2), swap(two[span:], 1)], 0)

    def sum_tp(partial):
        pieces = [partial[r * rows : (r + 1) * rows] for r in range(tp_count)]
        if tp_count != 4:
            for bit in reversed(tp_bits):
                pieces = [
                    piece + swap(other.astype(BF16), bit)
                    for piece, other in zip(pieces[:bit], pieces[bit:], strict=True)
                ]
            return pieces[0]
        upper = swap(pieces[3][:span].astype(BF16), 2)
        lower = swap(pieces[3][span:].astype(BF16), 1)
        one = jnp.concatenate([pieces[1][:span] + upper, pieces[1][span:]], 0)
        two = jnp.concatenate([pieces[2][:span], pieces[2][span:] + lower], 0)
        return pieces[0] + swap(one.astype(BF16), 1) + swap(two.astype(BF16), 2)

    def gather_ff(value):
        pieces = [value]
        for bit in ff_bits:
            pieces += [swap(piece, bit) for piece in pieces]
        return jnp.concatenate(pieces, 0)

    def sum_ff(partial):
        count = len(partial) // rows
        pieces = [partial[r * rows : (r + 1) * rows] for r in range(count)]
        while len(pieces) > 1:
            half = len(pieces) // 2
            bit = ff_bits[half.bit_length() - 1]
            pieces = [
                piece + swap(other.astype(BF16), bit)
                for piece, other in zip(pieces[:half], pieces[half:], strict=True)
            ]
        return pieces[0]

    def sum_all(value):
        for k in range(devices.bit_length() - 1):
            value = value + swap(value, 1 << k)
        return value

    def wanted(owner):
        index = lax.broadcasted_iota(jnp.int32, (1, 3 * padded), 1)
        within = index // (3 * LANES) * LANES + index % LANES
        feature = owner * group + within
        valid = (within < group) & (feature < width)
        return jnp.where(valid, index // LANES % 3 * width + feature, -1)

    columns = query_key_value_weight.shape[1]
    shard_index = lax.broadcasted_iota(jnp.int32, (columns, 1), 0)
    pick = jnp.concatenate(
        [(shard_index + columns * (t ^ r) == wanted(t)).astype(BF16) for r in range(tp_count)], 0
    )
    qkv_shards = [query_key_value_weight] + [swap(query_key_value_weight, r) for r in range(1, tp_count)]
    qkv_rows = dot(jnp.concatenate(qkv_shards, 1), pick).astype(BF16)
    qkv_weight = lax.all_gather(qkv_rows, "seq", axis=0, tiled=True)

    inputs = tokens.astype(F32)
    gain_one, shift_one = ln1_gain.astype(F32), ln1_bias.astype(F32)
    gain_two, shift_two = ln2_gain.astype(F32), ln2_bias.astype(F32)

    def head_columns(vector):
        whole = jnp.pad(vector, (0, tp_count * group - width))
        mine = lax.dynamic_slice_in_dim(whole, t * group, group)
        return jnp.pad(mine, (0, padded - group)).reshape(pairs, LANES)

    query_bias, value_bias = head_columns(qv_bias[0]), head_columns(qv_bias[1])
    qkv_bias = jnp.stack([query_bias, jnp.zeros_like(query_bias), value_bias], 1).reshape(-1)

    place = positions.reshape(chunks, tp_count, 2, span)[:, :, :, 0] // span
    places = jnp.take(place, peers, axis=1).reshape(chunks, 2 * tp_count)

    normal_one = [None] * chunks
    qkv, lse, own_out = [None] * chunks, [None] * chunks, [None] * chunks
    for c in range(chunks):
        normal_one[c] = gather_tp(norm_forward(inputs[c], gain_one, shift_one))

    out_row = [attention_output_weight] + [swap(attention_output_weight, r) for r in range(1, tp_count)]
    out_row = jnp.stack(out_row, 0)
    out_row = jnp.take(out_row, peers, axis=0).transpose(1, 0, 2).reshape(-1, width)
    out_whole = lax.all_gather(out_row, "seq", axis=0, tiled=True)
    out_whole = jnp.pad(out_whole, ((0, tp_count * group - width), (0, 0)))
    out_weight = [
        jnp.pad(
            lax.dynamic_slice_in_dim(out_whole, (t ^ r) * group, group, 0), ((0, padded - group), (0, 0))
        )
        for r in range(tp_count)
    ]

    stays = core == t // high
    block = t % high + core * high
    send = [
        (s * tp_count + i, s * tp_count + (i ^ high))
        for s in range(seq_count)
        for i in range(tp_count)
        if s % 2 == i // high
    ]

    def gather_block(shard):
        whole = lax.all_gather(shard, "seq", axis=0, tiled=True)
        return jnp.where(stays, whole, lax.ppermute(whole, both, send))

    expand = gather_block(expand_weight)
    contract = gather_block(contract_weight.T)
    hidden_bias = lax.dynamic_slice_in_dim(expand_bias, block * hidden, hidden).astype(F32)

    for c in range(chunks):
        qkv[c] = (dot(normal_one[c], qkv_weight) + qkv_bias).astype(BF16)
        *own_out[c], lse[c] = call_forward(places[c], qkv[c], span, group_heads)

    mixed, residual = [None] * chunks, [None] * chunks
    normal_two, output_rows = [None] * chunks, [None] * chunks
    for c in range(chunks):
        pieces = own_out[c]
        mixed[c] = jnp.concatenate([pieces[0]] + [swap(pieces[r], r) for r in range(1, tp_count)], 1)
        residual[c] = inputs[c] + dot(mixed[c], jnp.concatenate(out_weight, 0)) + attention_output_bias
        normal_two[c] = gather_ff(norm_forward(residual[c], gain_two, shift_two))
        output_rows[c] = gather_ff(cotangent[c])

    layer_out = []
    expand_grad = contract_grad = hidden_bias_grad = 0.0
    gain_two_grad = shift_two_grad = 0.0
    resid_grad, branch = [None] * chunks, [None] * chunks
    head_grads = [None] * chunks
    for c in range(chunks):
        activation_grad = dot(output_rows[c], contract)
        hidden_in = dot(normal_two[c], expand) + hidden_bias
        value, slope = gelu_pair(hidden_in)
        value = value.astype(BF16)
        hidden_grad = (activation_grad * slope).astype(BF16)
        feed = sum_ff(dot(value, contract, NT))
        layer_out.append((residual[c] + feed + contract_bias).astype(BF16))
        expand_grad = expand_grad + dot(normal_two[c], hidden_grad, TN)
        contract_grad = contract_grad + dot(output_rows[c], value, TN)
        hidden_bias_grad = hidden_bias_grad + jnp.sum(hidden_grad, 0, dtype=F32)
        norm_grad = sum_ff(dot(hidden_grad, expand, NT))
        from_norm, gain_part, shift_part = norm_backward(residual[c], gain_two, norm_grad)
        gain_two_grad, shift_two_grad = gain_two_grad + gain_part, shift_two_grad + shift_part
        resid_grad[c] = cotangent[c].astype(F32) + from_norm
        branch[c] = resid_grad[c].astype(BF16)
        pieces = [dot(branch[c], out_weight[r], NT).astype(BF16) for r in range(tp_count)]
        head_grads[c] = [pieces[0]] + [swap(pieces[r], r) for r in range(1, tp_count)]

    def sum_block(partial):
        rounded = partial.astype(BF16)
        other = lax.ppermute(rounded, both, [(b, a) for a, b in send])
        mine = jnp.where(stays, partial + other, 0.0).astype(BF16)
        return lax.psum_scatter(mine, "seq", scatter_dimension=0, tiled=True).astype(F32)

    fc_weight_grad = sum_block(expand_grad)
    proj_weight_grad = sum_block(contract_grad).T

    all_mixed, all_branch = jnp.concatenate(mixed, 0), jnp.concatenate(branch, 0)
    out_grad = dot(all_mixed, all_branch, TN).reshape(tp_count, padded, width)
    out_grad = out_grad[:, :group].astype(BF16)
    out_grad = jnp.take(out_grad, peers, axis=0).reshape(tp_count * group, width)[:width]
    out_grad = lax.psum_scatter(out_grad, "seq", scatter_dimension=0, tiled=True)
    out_grad = out_grad.reshape(-1, tp_count, width // tp_count).transpose(1, 0, 2)
    out_grad = jnp.take(out_grad, peers, axis=0)
    out_weight_grad = out_grad[0].astype(F32)
    for r in range(1, tp_count):
        out_weight_grad = out_weight_grad + swap(out_grad[r], r)

    qkv_grad, qkv_bias_grad = 0.0, 0.0
    gain_one_grad = shift_one_grad = 0.0
    input_grad = []
    for c in range(chunks):
        grads = call_backward(places[c], qkv[c], head_grads[c], lse[c], span, group_heads)
        norm_grad = sum_tp(dot(grads, qkv_weight, NT))
        qkv_grad = qkv_grad + dot(normal_one[c], grads, TN)
        qkv_bias_grad = qkv_bias_grad + jnp.sum(grads, 0, dtype=F32)
        from_norm, gain_part, shift_part = norm_backward(inputs[c], gain_one, norm_grad)
        gain_one_grad, shift_one_grad = gain_one_grad + gain_part, shift_one_grad + shift_part
        input_grad.append((resid_grad[c] + from_norm).astype(BF16))

    summed = lax.psum_scatter(qkv_grad.astype(BF16), "seq", scatter_dimension=0, tiled=True)
    spread = jnp.concatenate([summed] + [swap(summed, r) for r in range(1, tp_count)], 1)
    shard_column = lax.broadcasted_iota(jnp.int32, (1, columns), 1) + columns * t
    place_back = jnp.concatenate(
        [
            (wanted(t ^ r).reshape(-1, 1) == shard_column).astype(BF16)
            for r in range(tp_count)
        ],
        0,
    )
    qkv_weight_grad = dot(spread, place_back)

    qkv_bias_grad = qkv_bias_grad.reshape(pairs, 3, LANES)

    def whole_bias(part):
        mine = qkv_bias_grad[:, part].reshape(-1)[:group]
        whole = jnp.zeros((tp_count * group,), F32)
        return lax.dynamic_update_slice_in_dim(whole, mine, t * group, 0)[:width]

    hidden_whole = lax.dynamic_update_slice_in_dim(
        jnp.zeros(expand_bias.shape, F32), hidden_bias_grad, block * hidden, 0
    )
    out_bias_part = jnp.sum(all_branch, 0, dtype=F32)
    proj_bias_part = jnp.sum(cotangent, axis=(0, 1), dtype=F32)
    early = sum_all(
        jnp.concatenate([gain_two_grad, shift_two_grad, out_bias_part, proj_bias_part, hidden_whole])
    )
    late = sum_all(jnp.concatenate([gain_one_grad, shift_one_grad, whole_bias(0), whole_bias(2)]))

    def part(vector, index):
        return vector[index * width : (index + 1) * width]

    return (
        jnp.stack(layer_out),
        jnp.stack(input_grad),
        part(late, 0),
        part(late, 1),
        qkv_weight_grad,
        late[2 * width :].reshape(2, width),
        out_weight_grad,
        part(early, 2),
        part(early, 0),
        part(early, 1),
        fc_weight_grad,
        early[4 * width :],
        proj_weight_grad,
        part(early, 3),
    )


def solution(mesh):
    in_specs = (
        P("seq", "tp", None),
        P("seq", None),
        P(),
        P(),
        P("seq", "tp"),
        P(),
        P("seq", "tp"),
        P(),
        P(),
        P(),
        P("seq", "tp"),
        P(),
        P("tp", "seq"),
        P(),
        P("seq", "tp", None),
    )
    out_specs = (
        P("seq", "tp", None),
        P("seq", "tp", None),
        P(),
        P(),
        P("seq", "tp"),
        P(),
        P("seq", "tp"),
        P(),
        P(),
        P(),
        P("seq", "tp"),
        P(),
        P("tp", "seq"),
        P(),
    )
    placed = functools.partial(body, mesh.shape["seq"], mesh.shape["tp"])
    return jax.shard_map(placed, mesh=mesh, in_specs=in_specs, out_specs=out_specs, check_vma=False)
```

```python
import functools
import jax
import jax.numpy as jnp
from jax import lax
from jax.experimental import pallas as pl
from jax.experimental.pallas import tpu as pltpu
from jax.sharding import PartitionSpec as P

HEADS = 25
HEAD = 64
LANES = 128
TILE = 256
epsilon = 1e-05
F32 = jnp.float32
BF16 = jnp.bfloat16
NN = (((1,), (0,)), ((), ()))
NT = (((1,), (1,)), ((), ()))
TN = (((0,), (0,)), ((), ()))
MIB = 2**20
VMEM = pl.BlockSpec(memory_space=pltpu.VMEM)
SMEM = pl.BlockSpec(memory_space=pltpu.SMEM)
FAR = pl.BlockSpec(memory_space=pl.ANY)


def dot(left, right, dims=NN):
    return lax.dot_general(left, right, dims, preferred_element_type=F32)


def peer_id(count, mask):
    if mask < count:
        return {"tp": lax.axis_index("tp") ^ mask}
    return {"seq": lax.axis_index("seq") ^ 1}


def meet(count, masks):
    barrier = pltpu.get_barrier_semaphore()
    for mask in masks:
        pl.semaphore_signal(barrier, inc=1, device_id=peer_id(count, mask), device_id_type=pl.DeviceIdType.MESH)
    pl.semaphore_wait(barrier, len(masks))


def remote(count, source, target, send, recv, mask):
    return pltpu.make_async_remote_copy(
        src_ref=source,
        dst_ref=target,
        send_sem=send,
        recv_sem=recv,
        device_id=peer_id(count, mask),
        device_id_type=pl.DeviceIdType.MESH,
    )


def gather_kernel(count, tokens, own_ref, rows_ref, send_sems, recv_sems, local_sems):
    chunks = rows_ref.shape[0]
    span = tokens // 2
    direct_peers = (1, 2) if count == 4 else tuple(range(1, count))
    meet(count, direct_peers)

    def own(c):
        return pltpu.make_async_copy(
            own_ref.at[pl.ds(c * tokens, tokens)], rows_ref.at[c, pl.ds(0, tokens)], local_sems.at[c]
        )

    def direct(c, r):
        return remote(
            count,
            own_ref.at[pl.ds(c * tokens, tokens)],
            rows_ref.at[c, pl.ds(r * tokens, tokens)],
            send_sems.at[c, r],
            recv_sems.at[c, r],
            r,
        )

    def passed(c, half):
        start = (tokens, 2 * tokens + span)[half]
        return remote(
            count,
            rows_ref.at[c, pl.ds(start, span)],
            rows_ref.at[c, pl.ds(3 * tokens + half * span, span)],
            send_sems.at[c, 3 * half],
            recv_sems.at[c, 3 * half],
            2 - half,
        )

    for c in range(chunks):
        own(c).start()
        for r in direct_peers:
            direct(c, r).start()
    for c in range(chunks):
        for r in direct_peers:
            direct(c, r).wait_recv()
        if count == 4:
            passed(c, 0).start()
            passed(c, 1).start()
    for c in range(chunks):
        own(c).wait()
        for r in direct_peers:
            direct(c, r).wait_send()
        if count == 4:
            passed(c, 0).wait()
            passed(c, 1).wait()


def gather_rows(own, chunks, count):
    tokens = own.shape[0] // chunks
    return pl.pallas_call(
        functools.partial(gather_kernel, count, tokens),
        in_specs=[FAR],
        out_specs=FAR,
        out_shape=jax.ShapeDtypeStruct((chunks, tokens * count, own.shape[1]), BF16),
        scratch_shapes=[pltpu.SemaphoreType.DMA((chunks, count))] * 2 + [pltpu.SemaphoreType.DMA((chunks,))],
        compiler_params=pltpu.CompilerParams(collective_id=1, has_side_effects=True),
        cost_estimate=pl.CostEstimate(flops=0, bytes_accessed=120 * MIB, transcendentals=0),
        name="gather_rows",
    )(own)


def pick_one(index, options):
    result = options(0)
    for n in range(1, index[1]):
        result = lax.select(index[0] == n, options(n), result)
    return result


def to_places(count, span, holder, turned, source, target):
    for p in range(count):
        piece = pick_one((holder(p), count), source)
        first, second = piece[:span], piece[span:]
        swap = turned(p) == 1
        high = 2 * count - 1 - p
        target[p * span : (p + 1) * span, :] = lax.select(swap, second, first)
        target[high * span : (high + 1) * span, :] = lax.select(swap, first, second)


def from_places(count, span, pair, turned, source, store):
    for r in range(count):
        low = pick_one((pair(r), count), lambda p: source[p * span : (p + 1) * span, :])
        high = pick_one(
            (pair(r), count),
            lambda p: source[(2 * count - 1 - p) * span : (2 * count - p) * span, :],
        )
        swap = turned(r) == 1
        store(r, 0, lax.select(swap, high, low))
        store(r, 1, lax.select(swap, low, high))


def group_route(d):
    bit = d.bit_length() - 1
    return d - (1 << bit), bit


def forward_kernel(
    count,
    span,
    odd,
    masks,
    order_ref,
    place_ref,
    rows_ref,
    weight_ref,
    bias_ref,
    grad_ref,
    qkv_ref,
    mixed_ref,
    lse_ref,
    group_ref,
    rows,
    projected,
    outgoing,
    queries,
    keys,
    values,
    mixed,
    out_send,
    out_recv,
    group_send,
    group_recv,
    local_sems,
):
    chunks, length, _ = rows.shape
    pairs = weight_ref.shape[1] // (3 * LANES)
    tokens = 2 * span
    pieces = 1 << len(masks)

    def load_rows(c):
        return pltpu.make_async_copy(rows_ref.at[c], rows.at[c], local_sems.at[0, c])

    def save_qkv(c):
        return pltpu.make_async_copy(projected.at[c % 2], qkv_ref.at[c], local_sems.at[1, c])

    def keep(c):
        return pltpu.make_async_copy(
            outgoing.at[c, 0], mixed_ref.at[0, pl.ds(c * tokens, tokens)], local_sems.at[2, c]
        )

    def keep_grad(c):
        return pltpu.make_async_copy(
            grad_ref.at[pl.ds(c * tokens, tokens)], group_ref.at[0, c], local_sems.at[3, c]
        )

    def outward(c, r):
        return remote(
            count,
            outgoing.at[c, r],
            mixed_ref.at[r, pl.ds(c * tokens, tokens)],
            out_send.at[c, r],
            out_recv.at[c, r],
            r,
        )

    def grouped(c, d):
        origin, bit = group_route(d)
        source = grad_ref.at[pl.ds(c * tokens, tokens)] if origin == 0 else group_ref.at[origin, c]
        return remote(
            count, source, group_ref.at[d, c], group_send.at[c, d], group_recv.at[c, d], masks[bit]
        )

    for c in range(chunks):
        load_rows(c).start()
    meet(count, tuple(range(1, count)) + (count,))
    for c in range(chunks):
        keep_grad(c).start()
        for d in range(1, pieces):
            if group_route(d)[0] == 0:
                grouped(c, d).start()

    @pl.loop(0, chunks)
    def _(c):
        load_rows(c).wait()

        @pl.when(c >= 2)
        def _():
            save_qkv(c - 2).wait()

        @pl.loop(0, pairs)
        def _(j):
            columns = pl.ds(pl.multiple_of(j * 3 * LANES, LANES), 3 * LANES)
            block = (dot(rows[c], weight_ref[:, columns]) + bias_ref[:, columns]).astype(BF16)
            projected[c % 2, :, columns] = block
            for part, target in enumerate((queries, keys, values)):
                to_places(
                    count,
                    span,
                    lambda p: order_ref[c, p],
                    lambda p: order_ref[c, count + p],
                    lambda r: block[r * tokens : (r + 1) * tokens, part * LANES : (part + 1) * LANES],
                    target,
                )

            def one_head(head):
                lane = lax.broadcasted_iota(jnp.int32, (TILE, LANES), 1)
                mine = (lane // HEAD) == head
                for first in range(0, length, TILE):
                    last = first + TILE
                    query = jnp.where(mine, queries[first:last, :] * BF16(HEAD**-0.5), BF16(0))
                    scores = dot(query, keys[0:last, :], NT)
                    row = lax.broadcasted_iota(jnp.int32, (TILE, TILE), 0)
                    column = lax.broadcasted_iota(jnp.int32, (TILE, TILE), 1)
                    corner = jnp.where(column <= row, scores[:, first:last], -1e30)
                    scores = corner if first == 0 else jnp.concatenate([scores[:, :first], corner], axis=1)
                    row_max = jnp.max(scores, 1, keepdims=True)
                    weights = jnp.exp(scores - row_max)
                    total = jnp.sum(weights, 1, keepdims=True)
                    part = dot(weights.astype(BF16), values[0:last, :]) / total
                    lse_ref[c, j, head, first:last] = (row_max + jnp.log(total))[:, 0]
                    if head == 0:
                        mixed[first:last, :] = jnp.where(mine, part, 0.0).astype(BF16)
                    else:
                        mixed[first:last, :] = jnp.where(mine, part.astype(BF16), mixed[first:last, :])

            one_head(0)
            if odd:
                pl.when(j < pairs - 1)(lambda: one_head(1))
            else:
                one_head(1)
            lanes = pl.ds(pl.multiple_of(j * LANES, LANES), LANES)

            def put(r, half, value):
                outgoing[c, r, half * span : (half + 1) * span, lanes] = value

            from_places(
                count, span, lambda r: place_ref[c, r], lambda r: place_ref[c, count + r], mixed, put
            )

        save_qkv(c).start()
        keep(c).start()
        for r in range(1, count):
            outward(c, r).start()

    for c in range(chunks):
        keep_grad(c).wait()
    for d in range(1, pieces):
        origin = group_route(d)[0]
        for c in range(chunks):
            if origin != 0:
                grouped(c, d).start()
        for c in range(chunks):
            grouped(c, d).wait()
    for c in range(chunks):
        keep(c).wait()
        for r in range(1, count):
            outward(c, r).wait()
    for c in range(max(chunks - 2, 0), chunks):
        save_qkv(c).wait()


def call_forward(order, place, rows, weight, bias, grad, count, heads, masks):
    chunks, length, width = rows.shape
    columns = weight.shape[1]
    pairs, tokens, pieces = columns // (3 * LANES), length // count, 1 << len(masks)
    return pl.pallas_call(
        functools.partial(forward_kernel, count, tokens // 2, heads % 2 == 1, masks),
        in_specs=[SMEM, SMEM, FAR, VMEM, VMEM, FAR],
        out_specs=[FAR, FAR, VMEM, FAR],
        out_shape=[
            jax.ShapeDtypeStruct((chunks, length, columns), BF16),
            jax.ShapeDtypeStruct((count, chunks * tokens, pairs * LANES), BF16),
            jax.ShapeDtypeStruct((chunks, pairs, 2, length), F32),
            jax.ShapeDtypeStruct((pieces, chunks, tokens, width), BF16),
        ],
        scratch_shapes=[
            pltpu.VMEM((chunks, length, width), BF16),
            pltpu.VMEM((2, length, columns), BF16),
            pltpu.VMEM((chunks, count, tokens, pairs * LANES), BF16),
        ]
        + [pltpu.VMEM((length, LANES), BF16)] * 4
        + [pltpu.SemaphoreType.DMA((chunks, count))] * 2
        + [pltpu.SemaphoreType.DMA((chunks, pieces))] * 2
        + [pltpu.SemaphoreType.DMA((4, chunks))],
        compiler_params=pltpu.CompilerParams(
            collective_id=2, has_side_effects=True, vmem_limit_bytes=52 * MIB
        ),
        cost_estimate=pl.CostEstimate(
            flops=chunks * (2 * length * width * columns + heads * length * length * 5 * 256),
            bytes_accessed=80 * MIB,
            transcendentals=chunks * heads * length * length,
        ),
        name="attend_forward",
    )(order, place, rows, weight, bias, grad)


def backward_kernel(
    count,
    span,
    odd,
    order_ref,
    place_ref,
    qkv_ref,
    grad_ref,
    lse_ref,
    weight_ref,
    out_ref,
    sum_ref,
    arrived,
    block,
    result,
    queries,
    keys,
    values,
    grads,
    query_grad,
    key_sum,
    value_sum,
    first_out,
    first_in,
    side,
    second_out,
    second_in,
    head_send,
    head_recv,
    first_send,
    first_recv,
    second_send,
    second_recv,
    local_sems,
):
    chunks, length = out_ref.shape[:2]
    pairs = weight_ref.shape[1] // (3 * LANES)
    tokens = 2 * span

    def load_qkv(c):
        return pltpu.make_async_copy(qkv_ref.at[c], block.at[c % 2], local_sems.at[0, c])

    def load_own(c):
        return pltpu.make_async_copy(
            grad_ref.at[0, pl.ds(c * tokens, tokens)], arrived.at[c, 0], local_sems.at[1, c]
        )

    def save(c):
        return pltpu.make_async_copy(result, out_ref.at[c], local_sems.at[2, c])

    def inward(c, r):
        return remote(
            count,
            grad_ref.at[r, pl.ds(c * tokens, tokens)],
            arrived.at[c, r],
            head_send.at[c, r],
            head_recv.at[c, r],
            r,
        )

    def first(c, half):
        return remote(
            count,
            first_out.at[c, half],
            first_in.at[c, half],
            first_send.at[c, half],
            first_recv.at[c, half],
            2 - half,
        )

    def second(c, r):
        return remote(
            count,
            second_out.at[c, r - 1],
            second_in.at[c, r - 1],
            second_send.at[c, r - 1],
            second_recv.at[c, r - 1],
            r,
        )

    direct_peers = (1, 2) if count == 4 else tuple(range(1, count))

    def send_sums(c):
        if count == 4:
            first(c, 0).wait_recv()
            first(c, 1).wait_recv()
            second_out[c, 0, 0:span] = (side[0, 0:span] + first_in[c, 0].astype(F32)).astype(BF16)
            second_out[c, 0, span:tokens] = side[0, span:tokens].astype(BF16)
            second_out[c, 1, 0:span] = side[1, 0:span].astype(BF16)
            second_out[c, 1, span:tokens] = (side[1, span:tokens] + first_in[c, 1].astype(F32)).astype(
                BF16
            )
        for r in direct_peers:
            second(c, r).start()

    load_qkv(0).start()
    meet(count, tuple(range(1, count)))
    for c in range(chunks):
        load_own(c).start()
        for r in range(1, count):
            inward(c, r).start()

    @pl.loop(0, chunks)
    def _(c):
        load_qkv(c).wait()

        @pl.when(c < chunks - 1)
        def _():
            load_qkv(c + 1).start()

        load_own(c).wait()
        for r in range(1, count):
            inward(c, r).wait_recv()

        @pl.when(c >= 1)
        def _():
            save(c - 1).wait()

        @pl.loop(0, pairs)
        def _(j):
            @pl.when((j == pairs - 1) & (c >= 1))
            def _():
                send_sums(c - 1)

            def place(source, target):
                to_places(
                    count,
                    span,
                    lambda p: order_ref[c, p],
                    lambda p: order_ref[c, count + p],
                    source,
                    target,
                )

            for part, target in enumerate((queries, keys, values)):
                lanes = pl.ds(pl.multiple_of(j * 3 * LANES + part * LANES, LANES), LANES)
                place(lambda r: block[c % 2, r * tokens : (r + 1) * tokens, lanes], target)
            lanes = pl.ds(pl.multiple_of(j * LANES, LANES), LANES)
            place(lambda r: arrived[c, r, :, lanes], grads)

            def one_head(head):
                lane = lax.broadcasted_iota(jnp.int32, (TILE, LANES), 1)
                mine = (lane // HEAD) == head
                for first_row in reversed(range(0, length, TILE)):
                    last = first_row + TILE
                    query = jnp.where(mine, queries[first_row:last, :] * BF16(HEAD**-0.5), BF16(0))
                    grad = jnp.where(mine, grads[first_row:last, :], BF16(0))
                    scores = dot(query, keys[0:last, :], NT)
                    row = lax.broadcasted_iota(jnp.int32, (TILE, TILE), 0)
                    column = lax.broadcasted_iota(jnp.int32, (TILE, TILE), 1)
                    corner = jnp.where(column <= row, scores[:, first_row:last], -1e30)
                    scores = (
                        corner if first_row == 0 else jnp.concatenate([scores[:, :first_row], corner], axis=1)
                    )
                    weights = jnp.exp(scores - lse_ref[c, j, head, first_row:last][:, None])
                    prob_grad = dot(grad, values[0:last, :], NT)
                    product = weights * prob_grad
                    inner = jnp.sum(product, 1, keepdims=True)
                    score_grad = (product - weights * inner).astype(BF16)
                    rounded = weights.astype(BF16)
                    part = (dot(score_grad, keys[0:last, :]) * HEAD**-0.5).astype(BF16)
                    key_part = dot(query, score_grad, TN)
                    value_part = dot(grad, rounded, TN)
                    if head == 0 and last == length:
                        key_sum[...] = key_part
                        value_sum[...] = value_part
                    else:
                        key_sum[:, 0:last] += key_part
                        value_sum[:, 0:last] += value_part
                    if head == 0:
                        query_grad[first_row:last, :] = jnp.where(mine, part, BF16(0))
                    else:
                        query_grad[first_row:last, :] = jnp.where(mine, part, query_grad[first_row:last, :])

            one_head(0)
            if odd:
                pl.when(j < pairs - 1)(lambda: one_head(1))
            else:
                one_head(1)
            keys[...] = key_sum[...].T.astype(BF16)
            values[...] = value_sum[...].T.astype(BF16)
            for part, source in enumerate((query_grad, keys, values)):
                lanes = pl.ds(pl.multiple_of(j * 3 * LANES + part * LANES, LANES), LANES)

                def put(r, half, value):
                    start = r * tokens + half * span
                    result[start : start + span, lanes] = value

                from_places(
                    count, span, lambda r: place_ref[c, r], lambda r: place_ref[c, count + r], source, put
                )

        save(c).start()

        def share(first_piece, last_piece):
            return dot(result[first_piece * tokens : last_piece * tokens, :], weight_ref[...], NT)

        if count == 4:
            far = share(2, 4)
            first_out[c, 0] = far[tokens : tokens + span].astype(BF16)
            first_out[c, 1] = far[tokens + span :].astype(BF16)
            first(c, 0).start()
            first(c, 1).start()
            side[1] = far[:tokens]
            near = share(0, 2)
            side[0] = near[tokens:]
        else:
            for r in direct_peers:
                second_out[c, r - 1] = share(r, r + 1).astype(BF16)
            near = share(0, 1)
        sum_ref[pl.ds(pl.multiple_of(c * tokens, tokens), tokens), :] = near[:tokens]

    send_sums(chunks - 1)

    for c in range(chunks):
        total = sum_ref[c * tokens : (c + 1) * tokens, :]
        for r in direct_peers:
            second(c, r).wait_recv()
            total = total + second_in[c, r - 1].astype(F32)
        sum_ref[c * tokens : (c + 1) * tokens, :] = total
        for r in direct_peers:
            second(c, r).wait_send()
        if count == 4:
            first(c, 0).wait_send()
            first(c, 1).wait_send()
        for r in range(1, count):
            inward(c, r).wait_send()
    save(chunks - 1).wait()


def call_backward(order, place, qkv, grads, lse, weight, count, heads):
    chunks, length, columns = qkv.shape
    width = weight.shape[0]
    pairs, tokens = columns // (3 * LANES), length // count
    sides = 2 if count == 4 else count - 1
    return pl.pallas_call(
        functools.partial(backward_kernel, count, tokens // 2, heads % 2 == 1),
        in_specs=[SMEM, SMEM, FAR, FAR, VMEM, VMEM],
        out_specs=[FAR, VMEM],
        out_shape=[
            jax.ShapeDtypeStruct((chunks, length, columns), BF16),
            jax.ShapeDtypeStruct((chunks * tokens, width), F32),
        ],
        scratch_shapes=[
            pltpu.VMEM((chunks, count, tokens, pairs * LANES), BF16),
            pltpu.VMEM((2, length, columns), BF16),
            pltpu.VMEM((length, columns), BF16),
        ]
        + [pltpu.VMEM((length, LANES), BF16)] * 5
        + [pltpu.VMEM((LANES, length), F32)] * 2
        + [
            pltpu.VMEM((chunks, 2, tokens // 2, width), BF16),
            pltpu.VMEM((chunks, 2, tokens // 2, width), BF16),
            pltpu.VMEM((2, tokens, width), F32),
            pltpu.VMEM((chunks, sides, tokens, width), BF16),
            pltpu.VMEM((chunks, sides, tokens, width), BF16),
        ]
        + [pltpu.SemaphoreType.DMA((chunks, count))] * 2
        + [pltpu.SemaphoreType.DMA((chunks, 2))] * 2
        + [pltpu.SemaphoreType.DMA((chunks, sides))] * 2
        + [pltpu.SemaphoreType.DMA((3, chunks))],
        compiler_params=pltpu.CompilerParams(
            collective_id=3, has_side_effects=True, vmem_limit_bytes=60 * MIB
        ),
        cost_estimate=pl.CostEstimate(
            flops=chunks * (2 * length * width * columns + heads * length * length * 8 * 256),
            bytes_accessed=80 * MIB,
            transcendentals=chunks * heads * length * length,
        ),
        name="attend_backward",
    )(order, place, qkv, grads, lse, weight)


def gelu_pair(u):
    scale = 0.7978845608028654
    square = u * u
    inner = jnp.tanh(u * (scale + scale * 0.044715 * square))
    half = 0.5 + 0.5 * inner
    slope = half + u * (half * (1.0 - inner)) * (scale + scale * 0.134145 * square)
    return u * half, slope


def hidden_kernel(
    count, masks, own_ref, weight_ref, bias_ref, rows_ref, value_ref, slope_ref, rows, staged,
    group_send, group_recv, local_sems, save_sems,
):
    chunks, pieces, tokens, width = rows.shape

    def keep(c):
        return pltpu.make_async_copy(own_ref.at[pl.ds(c * tokens, tokens)], rows.at[c, 0], local_sems.at[0, c])

    def save_rows(c):
        return pltpu.make_async_copy(rows.at[c], rows_ref.at[c], local_sems.at[1, c])

    def grouped(c, d):
        origin, bit = group_route(d)
        source = own_ref.at[pl.ds(c * tokens, tokens)] if origin == 0 else rows.at[c, origin]
        return remote(count, source, rows.at[c, d], group_send.at[c, d], group_recv.at[c, d], masks[bit])

    def save(n, part):
        c, i = n // pieces, n % pieces
        p = (i % 2) * 2 + i // 2
        target = value_ref.at[p, c] if part == 0 else slope_ref.at[c, p]
        return pltpu.make_async_copy(staged.at[n % 2, part], target, save_sems.at[n % 2, part])

    for c in range(chunks):
        keep(c).start()
    meet(count, masks)
    for c in range(chunks):
        grouped(c, 1).start()
    for c in range(chunks):
        grouped(c, 2).start()

    @pl.loop(0, chunks)
    def _(c):
        keep(c).wait()

        @pl.loop(0, pieces)
        def _(i):
            p = (i % 2) * 2 + i // 2
            step = c * pieces + i

            @pl.when(i == 1)
            def _():
                grouped(c, 2).wait_recv()

            @pl.when(i == 2)
            def _():
                grouped(c, 1).wait_recv()
                grouped(c, 3).start()

            @pl.when(i == 3)
            def _():
                grouped(c, 3).wait_recv()
                save_rows(c).start()

            value, slope = gelu_pair(dot(rows[c, p], weight_ref[...]) + bias_ref[...])

            @pl.when(step >= 2)
            def _():
                for part in range(2):
                    save(step - 2, part).wait()

            staged[step % 2, 0] = value.astype(BF16)
            staged[step % 2, 1] = slope.astype(BF16)
            for part in range(2):
                save(step, part).start()

    for c in range(chunks):
        save_rows(c).wait()
        for d in range(1, pieces):
            grouped(c, d).wait_send()
    for step in range(chunks * pieces - 2, chunks * pieces):
        for part in range(2):
            save(step, part).wait()


def call_hidden(own, weight, bias, chunks, count, masks):
    width, hidden = weight.shape
    tokens, pieces = own.shape[0] // chunks, 1 << len(masks)
    return pl.pallas_call(
        functools.partial(hidden_kernel, count, masks),
        in_specs=[FAR, VMEM, VMEM],
        out_specs=[FAR] * 3,
        out_shape=[
            jax.ShapeDtypeStruct((chunks, pieces, tokens, width), BF16),
            jax.ShapeDtypeStruct((pieces, chunks, tokens, hidden), BF16),
            jax.ShapeDtypeStruct((chunks, pieces, tokens, hidden), BF16),
        ],
        scratch_shapes=[
            pltpu.VMEM((chunks, pieces, tokens, width), BF16),
            pltpu.VMEM((2, 2, tokens, hidden), BF16),
            pltpu.SemaphoreType.DMA((chunks, pieces)),
            pltpu.SemaphoreType.DMA((chunks, pieces)),
            pltpu.SemaphoreType.DMA((2, chunks)),
            pltpu.SemaphoreType.DMA((2, 2)),
        ],
        compiler_params=pltpu.CompilerParams(
            collective_id=4, has_side_effects=True, vmem_limit_bytes=44 * MIB
        ),
        cost_estimate=pl.CostEstimate(
            flops=2 * chunks * pieces * tokens * width * hidden, bytes_accessed=100 * MIB, transcendentals=0
        ),
        name="hidden_forward",
    )(own, weight, bias)


def group_kernel(count, masks, backward, *refs):
    if backward:
        grad_ref, slope_ref, contract_ref, weight_ref, part_ref, other_ref, sum_ref, out_ref, staged = refs[:9]
        sources = (grad_ref, slope_ref)
    else:
        value_ref, weight_ref, residual_ref, bias_ref, part_ref, other_ref, sum_ref = refs[:7]
        sources = (value_ref,)
    scratch = refs[9:] if backward else refs[7:]
    loaded, partial, from_core, over, from_side = scratch[:5]
    core_send, core_recv, side_send, side_recv, cargo_sems, load_sems, save_sems = scratch[5:]
    chunks, tokens, _ = over.shape
    steps = 4 * chunks
    high = count // 2
    stays = lax.rem(lax.axis_index("seq"), 2) == lax.axis_index("tp") // high

    def place(step):
        return lax.rem(step, 2 * chunks) // 2, 3 - step // (2 * chunks) - 2 * lax.rem(step, 2)

    def load(step, part):
        c, p = place(step)
        slot = lax.rem(step, 2)
        source = sources[part].at[p, c] if part == 0 else sources[part].at[c, p]
        return pltpu.make_async_copy(source, loaded.at[slot, part], load_sems.at[slot, part])

    def save(step):
        c, p = place(step)
        slot = lax.rem(step, 2)
        return pltpu.make_async_copy(staged.at[slot], out_ref.at[c, p], save_sems.at[slot])

    def to_core(c, p):
        return remote(
            count, partial.at[c, p], from_core.at[c, p - 2], core_send.at[c, p - 2], core_recv.at[c, p - 2], masks[1]
        )

    def to_side(c):
        return remote(count, over.at[c], from_side.at[c], side_send.at[c], side_recv.at[c], masks[0])

    def cargo():
        return remote(count, part_ref, other_ref, cargo_sems.at[0], cargo_sems.at[1], high)

    for part in range(len(sources)):
        load(0, part).start()
    meet(count, masks + (high,))

    @pl.when(jnp.logical_not(stays))
    def _():
        cargo().start()

    @pl.loop(0, steps)
    def _(step):
        c, p = place(step)
        slot = lax.rem(step, 2)
        for part in range(len(sources)):
            load(step, part).wait()

        @pl.when(step < steps - 1)
        def _():
            for part in range(len(sources)):
                load(step + 1, part).start()

        @pl.when((slot == 0) & (step >= 2) & (step <= 2 * chunks))
        def _():
            before = step // 2 - 1
            to_core(before, 3).wait_recv()
            over[before] = (partial[before, 1].astype(F32) + from_core[before, 1].astype(F32)).astype(BF16)
            to_side(before).start()

        if backward:
            hidden = dot(loaded[slot, 0], contract_ref[...]) * loaded[slot, 1].astype(F32)
            hidden = hidden.astype(BF16)

            @pl.when(step >= 2)
            def _():
                save(step - 2).wait()

            staged[slot] = hidden
            save(step).start()
        else:
            hidden = loaded[slot, 0]
        partial[c, p] = dot(hidden, weight_ref[...], NT).astype(BF16)

        @pl.when(p >= 2)
        def _():
            to_core(c, p).start()

    for c in range(chunks):
        to_core(c, 2).wait_recv()
        to_side(c).wait_recv()
        total = partial[c, 0].astype(F32) + from_core[c, 0].astype(F32) + from_side[c].astype(F32)
        mine = slice(c * tokens, (c + 1) * tokens)
        if backward:
            sum_ref[mine, :] = total
        else:
            sum_ref[mine, :] = (residual_ref[mine, :] + total + bias_ref[...]).astype(BF16)
        to_core(c, 2).wait_send()
        to_core(c, 3).wait_send()
        to_side(c).wait_send()
    if backward:
        for step in range(steps - 2, steps):
            save(step).wait()

    @pl.when(stays)
    def _():
        cargo().wait_recv()

    @pl.when(jnp.logical_not(stays))
    def _():
        cargo().wait_send()


def call_group(count, masks, backward, tiles, weights, part):
    pieces, chunks, tokens, width = tiles[0].shape
    outs = [
        jax.ShapeDtypeStruct(part.shape, BF16),
        jax.ShapeDtypeStruct((chunks * tokens, width), F32 if backward else BF16),
    ]
    scratch = [
        pltpu.VMEM((2, len(tiles), tokens, width), BF16),
        pltpu.VMEM((chunks, pieces, tokens, width), BF16),
        pltpu.VMEM((chunks, 2, tokens, width), BF16),
        pltpu.VMEM((chunks, tokens, width), BF16),
        pltpu.VMEM((chunks, tokens, width), BF16),
        pltpu.SemaphoreType.DMA((chunks, 2)),
        pltpu.SemaphoreType.DMA((chunks, 2)),
        pltpu.SemaphoreType.DMA((chunks,)),
        pltpu.SemaphoreType.DMA((chunks,)),
        pltpu.SemaphoreType.DMA((2,)),
        pltpu.SemaphoreType.DMA((2, len(tiles))),
        pltpu.SemaphoreType.DMA((2,)),
    ]
    if backward:
        outs.append(jax.ShapeDtypeStruct((chunks, pieces, tokens, width), BF16))
        scratch = [pltpu.VMEM((2, tokens, width), BF16)] + scratch
    return pl.pallas_call(
        functools.partial(group_kernel, count, masks, backward),
        in_specs=[FAR] * len(tiles) + [VMEM] * len(weights) + [FAR],
        out_specs=[FAR, VMEM] + [FAR] * (len(outs) - 2),
        out_shape=outs,
        scratch_shapes=scratch,
        compiler_params=pltpu.CompilerParams(
            collective_id=5 if backward else 6, has_side_effects=True, vmem_limit_bytes=56 * MIB
        ),
        cost_estimate=pl.CostEstimate(
            flops=(4 if backward else 2) * chunks * pieces * tokens * width * width,
            bytes_accessed=160 * MIB,
            transcendentals=0,
        ),
        name="group_backward" if backward else "group_forward",
    )(*tiles, *weights, part)


def statistics(values):
    centred = values - jnp.mean(values, -1, keepdims=True)
    spread = jnp.mean(centred * centred, -1, keepdims=True)
    inverse = lax.rsqrt(spread + epsilon)
    return centred * inverse, inverse


def norm_forward(values, gain, shift):
    return (statistics(values)[0] * gain + shift).astype(BF16)


def norm_backward(values, gain, grad):
    normal, inverse = statistics(values)
    scaled = grad * gain
    spread = jnp.mean(scaled * normal, -1, keepdims=True)
    result = inverse * (scaled - jnp.mean(scaled, -1, keepdims=True) - normal * spread)
    return result, jnp.sum(grad * normal, 0), jnp.sum(grad, 0)


def body(
    seq_count,
    tp_count,
    tokens,
    positions,
    ln1_gain,
    ln1_bias,
    query_key_value_weight,
    qv_bias,
    attention_output_weight,
    attention_output_bias,
    ln2_gain,
    ln2_bias,
    expand_weight,
    expand_bias,
    contract_weight,
    contract_bias,
    cotangent,
):
    devices = seq_count * tp_count
    both = ("seq", "tp")
    t = lax.axis_index("tp")
    core = lax.axis_index("seq") % 2
    core_bit = tp_count
    tp_bits = [1 << k for k in range(tp_count.bit_length() - 1)]
    high = tp_bits[-1]
    ff_bits = tp_bits[:-1] + [core_bit]
    chunks, rows, width = tokens.shape
    span = rows // 2
    group_heads = -(-HEADS // tp_count)
    group = group_heads * HEAD
    pairs = -(-group_heads // 2)
    padded = pairs * LANES
    hidden = expand_weight.shape[1]
    peers = t ^ jnp.arange(tp_count)

    def swap(value, mask):
        return lax.ppermute(value, both, [(i, i ^ mask) for i in range(devices)])

    def after(value, *earlier):
        return lax.optimization_barrier((value, *earlier))[0]

    def choose(pieces, index):
        result = pieces[0]
        for n in range(1, len(pieces)):
            result = jnp.where(index == n, pieces[n], result)
        return result

    def gather_ff(value):
        pieces = [value]
        for bit in ff_bits:
            pieces += [swap(piece, bit) for piece in pieces]
        return pieces

    def sum_ff(pieces):
        while len(pieces) > 1:
            half = len(pieces) // 2
            bit = ff_bits[half.bit_length() - 1]
            pieces = [
                piece + swap(other, bit) for piece, other in zip(pieces[:half], pieces[half:], strict=True)
            ]
        return pieces[0]

    def sum_all(value):
        for k in range(devices.bit_length() - 1):
            value = value + swap(value, 1 << k)
        return value

    columns = query_key_value_weight.shape[1]
    feature = lax.broadcasted_iota(jnp.int32, (1, padded), 1)

    def shard_columns(owner, holder):
        found = []
        for part in range(3):
            column = part * width + holder * group + feature - columns * owner
            valid = (feature < group) & (holder * group + feature < width)
            found.append(jnp.where(valid & (column >= 0) & (column < columns), column, -1))
        return found

    def to_block(packed):
        parts = []
        for part in range(3):
            chosen = jnp.zeros_like(packed[0])
            for r in range(tp_count):
                chosen = jnp.where(shard_columns(t ^ r, t)[part] >= 0, packed[r], chosen)
            parts.append(chosen.reshape(-1, pairs, 1, LANES))
        return jnp.concatenate(parts, 2).reshape(-1, 3 * padded)

    def from_block(value):
        value = value.reshape(-1, pairs, 3, LANES)
        packed = []
        for r in range(tp_count):
            chosen = jnp.zeros((value.shape[0], padded), value.dtype)
            for part in range(3):
                here = shard_columns(t ^ r, t)[part] >= 0
                chosen = jnp.where(here, value[:, :, part].reshape(-1, padded), chosen)
            packed.append(chosen)
        return packed

    shard_index = lax.broadcasted_iota(jnp.int32, (columns, 1), 0)
    pick = []
    for r in range(tp_count):
        first, second, third = shard_columns(t, t ^ r)
        pick.append((shard_index == jnp.maximum(jnp.maximum(first, second), third)).astype(BF16))
    pick = jnp.concatenate(pick, 1)
    packed = dot(query_key_value_weight, pick).astype(BF16)
    packed = [packed[:, r * padded : (r + 1) * padded] for r in range(tp_count)]
    packed = [packed[0]] + [swap(packed[r], r) for r in range(1, tp_count)]

    flat = tokens.reshape(-1, width)
    gain_one, shift_one = ln1_gain.astype(F32), ln1_bias.astype(F32)
    gain_two, shift_two = ln2_gain.astype(F32), ln2_bias.astype(F32)
    normal_own = norm_forward(flat.astype(F32), gain_one, shift_one)
    qkv_rows = to_block(packed)
    qkv_weight = lax.all_gather(qkv_rows, "seq", axis=0, tiled=True)

    def head_columns(vector):
        whole = jnp.pad(vector, (0, tp_count * group - width))
        mine = lax.dynamic_slice_in_dim(whole, t * group, group)
        return jnp.pad(mine, (0, padded - group)).reshape(pairs, LANES)

    query_bias, value_bias = head_columns(qv_bias[0]), head_columns(qv_bias[1])
    qkv_bias = jnp.stack([query_bias, jnp.zeros_like(query_bias), value_bias], 1).reshape(-1)

    place = positions.reshape(chunks, tp_count, 2, span)[:, :, 0, 0] // span
    place = jnp.take(place, peers, axis=1)
    turned = (place >= tp_count).astype(jnp.int32)
    pair = jnp.minimum(place, 2 * tp_count - 1 - place)
    holds = pair[:, None, :] == jnp.arange(tp_count)[None, :, None]
    holder = jnp.sum(jnp.where(holds, jnp.arange(tp_count), 0), 2)
    orders = jnp.concatenate([holder, jnp.sum(jnp.where(holds, turned[:, None, :], 0), 2)], 1).astype(jnp.int32)
    places = jnp.concatenate([pair, turned], 1).astype(jnp.int32)
    masks = tuple(ff_bits)
    members = 1 << len(masks)

    stays = core == t // high
    block = t % high + core * high
    send = [
        (s * tp_count + i, s * tp_count + (i ^ high))
        for s in range(seq_count)
        for i in range(tp_count)
        if s % 2 == i // high
    ]

    def gather_seq(shard):
        return lax.all_gather(shard, "seq", axis=0, tiled=True)

    def take_block(whole):
        return jnp.where(stays, whole, lax.ppermute(whole, both, send))

    def give_block(partial):
        return lax.ppermute(partial, both, [(b, a) for a, b in send])

    def keep_block(partial, other):
        return jnp.where(stays, partial.astype(F32) + other, 0.0).astype(BF16)

    def sum_seq(partial):
        return after(lax.psum_scatter(partial, "seq", scatter_dimension=0, tiled=True))

    shards = [attention_output_weight] + [swap(attention_output_weight, r) for r in range(1, tp_count)]
    out_row = jnp.concatenate([choose(shards, t ^ a) for a in range(tp_count)], 1)
    normal_one = gather_rows(after(normal_own, out_row, qkv_rows), chunks, tp_count)
    expand = take_block(gather_seq(expand_weight))
    contract_whole = gather_seq(after(contract_weight.T, normal_one))
    hidden_bias = lax.dynamic_slice_in_dim(expand_bias, block * hidden, hidden).astype(F32)

    out_weight = gather_seq(after(out_row, normal_one))

    qkv, heads_out, lse, output_rows = call_forward(
        orders,
        places,
        normal_one,
        qkv_weight,
        qkv_bias.astype(F32).reshape(1, -1),
        cotangent.reshape(-1, width),
        tp_count,
        group_heads,
        masks,
    )
    contract = take_block(after(contract_whole, heads_out))
    pieces = [heads_out[r, :, :group] for r in range(tp_count)]
    mixed = jnp.concatenate([choose(pieces, t ^ a) for a in range(tp_count)], 1)[:, :width]
    residual = flat.astype(F32) + dot(mixed, out_weight) + attention_output_bias
    normal = norm_forward(residual, gain_two, shift_two)

    flat_rows = output_rows.reshape(-1, width)
    if tp_count == 4:
        normal_two, value, slope = call_hidden(
            normal, expand, hidden_bias.reshape(1, -1), chunks, tp_count, masks
        )
        value = value.reshape(-1, hidden)
        contract_grad = dot(flat_rows, value, TN).astype(BF16)
        other, norm_grad, hidden_grad = call_group(
            tp_count, masks, True, [output_rows, slope], [contract, expand], contract_grad
        )
        contract_grad = keep_block(contract_grad, other)
        proj_weight_grad = sum_seq(contract_grad)
        normal_two, hidden_grad = normal_two.reshape(-1, width), hidden_grad.reshape(-1, hidden)
        expand_grad = dot(normal_two, after(hidden_grad, contract_grad), TN).astype(BF16)
        expand_grad = after(expand_grad, proj_weight_grad)
        other, layer_out = call_group(
            tp_count,
            masks,
            False,
            [value.reshape(members, chunks, rows, hidden)],
            [contract, residual, contract_bias.astype(F32).reshape(1, -1)],
            expand_grad,
        )
        expand_grad = keep_block(expand_grad, other)
    else:
        normal_two = jnp.concatenate(gather_ff(normal), 0)
        value, slope = gelu_pair(dot(normal_two, expand) + hidden_bias)
        value = value.astype(BF16)
        contract_grad = dot(flat_rows, value, TN).astype(BF16)
        hidden_grad = (dot(flat_rows, contract) * slope).astype(BF16)
        partial = dot(hidden_grad, expand, NT).astype(BF16).reshape(members, -1, width)
        norm_grad = sum_ff([partial[d] for d in range(members)]).astype(F32)
        proj_weight_grad = sum_seq(keep_block(contract_grad, give_block(contract_grad)))
        expand_grad = dot(normal_two, hidden_grad, TN).astype(BF16)
        expand_grad = keep_block(expand_grad, give_block(expand_grad))
        members_value = value.reshape(members, -1, hidden)
        feed = [dot(members_value[d], contract, NT).astype(BF16) for d in range(members)]
        layer_out = (residual + sum_ff(feed) + contract_bias).astype(BF16)
    fc_weight_grad = sum_seq(expand_grad)
    hidden_bias_grad = jnp.sum(hidden_grad, 0, dtype=F32)

    from_norm, gain_two_grad, shift_two_grad = norm_backward(residual, gain_two, norm_grad)
    resid_grad = cotangent.reshape(-1, width).astype(F32) + from_norm
    branch = resid_grad.astype(BF16)
    head_grad = dot(branch, out_weight, NT).astype(BF16)
    head_grad = jnp.pad(head_grad, ((0, 0), (0, tp_count * group - width)))
    pieces = [head_grad[:, a * group : (a + 1) * group] for a in range(tp_count)]
    pieces = [jnp.pad(choose(pieces, t ^ r), ((0, 0), (0, padded - group))) for r in range(tp_count)]
    out_grad = sum_seq(dot(mixed, branch, TN).astype(BF16))

    qkv_grads, one_grad = call_backward(
        orders,
        places,
        after(qkv, expand_grad, out_grad),
        jnp.stack(pieces),
        lse,
        qkv_weight,
        tp_count,
        group_heads,
    )
    qkv_grads = after(qkv_grads, fc_weight_grad)
    out_grad = [out_grad[:, a * (width // tp_count) : (a + 1) * (width // tp_count)] for a in range(tp_count)]
    out_weight_grad = choose(out_grad, t).astype(F32)
    for r in range(1, tp_count):
        out_weight_grad = out_weight_grad + swap(choose(out_grad, t ^ r), r)

    qkv_grads = qkv_grads.reshape(-1, 3 * padded)
    qkv_grad = dot(normal_one.reshape(-1, width), qkv_grads, TN)
    qkv_bias_grad = jnp.sum(qkv_grads, 0, dtype=F32)
    from_norm, gain_one_grad, shift_one_grad = norm_backward(flat.astype(F32), gain_one, one_grad)
    input_grad = (resid_grad + from_norm).astype(BF16).reshape(tokens.shape)

    summed = lax.psum_scatter(qkv_grad.astype(BF16), "seq", scatter_dimension=0, tiled=True)
    packed = from_block(summed)
    packed = [packed[0]] + [swap(packed[r], r) for r in range(1, tp_count)]
    qkv_weight_grad = dot(jnp.concatenate(packed, 1), pick, NT)

    qkv_bias_grad = qkv_bias_grad.reshape(pairs, 3, LANES)

    def whole_bias(part):
        mine = qkv_bias_grad[:, part].reshape(-1)[:group]
        whole = jnp.zeros((tp_count * group,), F32)
        return lax.dynamic_update_slice_in_dim(whole, mine, t * group, 0)[:width]

    hidden_whole = lax.dynamic_update_slice_in_dim(
        jnp.zeros(expand_bias.shape, F32), hidden_bias_grad, block * hidden, 0
    )
    out_bias_part = jnp.sum(branch, 0, dtype=F32)
    proj_bias_part = jnp.sum(cotangent, axis=(0, 1), dtype=F32)
    early = sum_all(
        jnp.concatenate([gain_two_grad, shift_two_grad, out_bias_part, proj_bias_part, hidden_whole])
    )
    late = sum_all(jnp.concatenate([gain_one_grad, shift_one_grad, whole_bias(0), whole_bias(2)]))

    def part(vector, index):
        return vector[index * width : (index + 1) * width]

    return (
        layer_out.reshape(tokens.shape),
        input_grad,
        part(late, 0),
        part(late, 1),
        qkv_weight_grad,
        late[2 * width :].reshape(2, width),
        out_weight_grad,
        part(early, 2),
        part(early, 0),
        part(early, 1),
        fc_weight_grad.astype(F32),
        early[4 * width :],
        proj_weight_grad.astype(F32).T,
        part(early, 3),
    )


def solution(mesh):
    in_specs = (
        P("seq", "tp", None),
        P("seq", None),
        P(),
        P(),
        P("seq", "tp"),
        P(),
        P("seq", "tp"),
        P(),
        P(),
        P(),
        P("seq", "tp"),
        P(),
        P("tp", "seq"),
        P(),
        P("seq", "tp", None),
    )
    out_specs = (
        P("seq", "tp", None),
        P("seq", "tp", None),
        P(),
        P(),
        P("seq", "tp"),
        P(),
        P("seq", "tp"),
        P(),
        P(),
        P(),
        P("seq", "tp"),
        P(),
        P("tp", "seq"),
        P(),
    )
    placed = functools.partial(body, mesh.shape["seq"], mesh.shape["tp"])
    return jax.shard_map(placed, mesh=mesh, in_specs=in_specs, out_specs=out_specs, check_vma=False)
```

```python
import functools
import jax
import jax.numpy as jnp
from jax import lax
from jax.experimental import pallas as pl
from jax.experimental.pallas import tpu as pltpu
from jax.sharding import PartitionSpec as P

HEADS = 25
HEAD = 64
LANES = 128
TILE = 256
epsilon = 1e-05
F32 = jnp.float32
BF16 = jnp.bfloat16
NN = (((1,), (0,)), ((), ()))
NT = (((1,), (1,)), ((), ()))
TN = (((0,), (0,)), ((), ()))
MIB = 2**20
VMEM = pl.BlockSpec(memory_space=pltpu.VMEM)
SMEM = pl.BlockSpec(memory_space=pltpu.SMEM)
FAR = pl.BlockSpec(memory_space=pl.ANY)


def dot(left, right, dims=NN):
    return lax.dot_general(left, right, dims, preferred_element_type=F32)


def peer_id(count, mask):
    if mask < count:
        return {"tp": lax.axis_index("tp") ^ mask}
    return {"seq": lax.axis_index("seq") ^ 1}


def meet(count, masks):
    barrier = pltpu.get_barrier_semaphore()
    for mask in masks:
        pl.semaphore_signal(barrier, inc=1, device_id=peer_id(count, mask), device_id_type=pl.DeviceIdType.MESH)
    pl.semaphore_wait(barrier, len(masks))


def remote(count, source, target, send, recv, mask):
    return pltpu.make_async_remote_copy(
        src_ref=source,
        dst_ref=target,
        send_sem=send,
        recv_sem=recv,
        device_id=peer_id(count, mask),
        device_id_type=pl.DeviceIdType.MESH,
    )


def block_stays(count):
    return lax.rem(lax.axis_index("seq"), 2) == lax.axis_index("tp") // (count // 2)


def pass_block(count, source, target, sems):
    return remote(count, source, target, sems.at[0], sems.at[1], count // 2)


def when(condition, action):
    pl.when(condition)(action)


def gather_kernel(count, tokens, own_ref, rows_ref, send_sems, recv_sems, local_sems):
    chunks = rows_ref.shape[0]
    span = tokens // 2
    direct_peers = (1, 2) if count == 4 else tuple(range(1, count))
    meet(count, direct_peers)

    def own(c):
        return pltpu.make_async_copy(
            own_ref.at[pl.ds(c * tokens, tokens)], rows_ref.at[c, pl.ds(0, tokens)], local_sems.at[c]
        )

    def direct(c, r):
        return remote(
            count,
            own_ref.at[pl.ds(c * tokens, tokens)],
            rows_ref.at[c, pl.ds(r * tokens, tokens)],
            send_sems.at[c, r],
            recv_sems.at[c, r],
            r,
        )

    def passed(c, half):
        start = (tokens, 2 * tokens + span)[half]
        return remote(
            count,
            rows_ref.at[c, pl.ds(start, span)],
            rows_ref.at[c, pl.ds(3 * tokens + half * span, span)],
            send_sems.at[c, 3 * half],
            recv_sems.at[c, 3 * half],
            2 - half,
        )

    for c in range(chunks):
        own(c).start()
        for r in direct_peers:
            direct(c, r).start()
    for c in range(chunks):
        for r in direct_peers:
            direct(c, r).wait_recv()
        if count == 4:
            passed(c, 0).start()
            passed(c, 1).start()
    for c in range(chunks):
        own(c).wait()
        for r in direct_peers:
            direct(c, r).wait_send()
        if count == 4:
            passed(c, 0).wait()
            passed(c, 1).wait()


def gather_rows(own, chunks, count):
    tokens = own.shape[0] // chunks
    return pl.pallas_call(
        functools.partial(gather_kernel, count, tokens),
        in_specs=[FAR],
        out_specs=FAR,
        out_shape=jax.ShapeDtypeStruct((chunks, tokens * count, own.shape[1]), BF16),
        scratch_shapes=[pltpu.SemaphoreType.DMA((chunks, count))] * 2 + [pltpu.SemaphoreType.DMA((chunks,))],
        compiler_params=pltpu.CompilerParams(collective_id=1, has_side_effects=True),
        cost_estimate=pl.CostEstimate(flops=0, bytes_accessed=120 * MIB, transcendentals=0),
        name="gather_rows",
    )(own)


def pick_one(index, options):
    result = options(0)
    for n in range(1, index[1]):
        result = lax.select(index[0] == n, options(n), result)
    return result


def to_places(count, span, holder, turned, source, target):
    for p in range(count):
        piece = pick_one((holder(p), count), source)
        first, second = piece[:span], piece[span:]
        swap = turned(p) == 1
        high = 2 * count - 1 - p
        target[p * span : (p + 1) * span, :] = lax.select(swap, second, first)
        target[high * span : (high + 1) * span, :] = lax.select(swap, first, second)


def from_places(count, span, pair, turned, source, store):
    for r in range(count):
        low = pick_one((pair(r), count), lambda p: source[p * span : (p + 1) * span, :])
        high = pick_one(
            (pair(r), count),
            lambda p: source[(2 * count - 1 - p) * span : (2 * count - p) * span, :],
        )
        swap = turned(r) == 1
        store(r, 0, lax.select(swap, high, low))
        store(r, 1, lax.select(swap, low, high))


def group_route(d):
    bit = d.bit_length() - 1
    return d - (1 << bit), bit


def forward_kernel(
    count,
    span,
    odd,
    masks,
    order_ref,
    place_ref,
    rows_ref,
    weight_ref,
    bias_ref,
    grad_ref,
    block_ref,
    qkv_ref,
    mixed_ref,
    lse_ref,
    group_ref,
    other_ref,
    rows,
    projected,
    outgoing,
    queries,
    keys,
    values,
    mixed,
    out_send,
    out_recv,
    group_send,
    group_recv,
    local_sems,
    block_sems,
):
    stays = block_stays(count)
    chunks, length, _ = rows.shape
    pairs = weight_ref.shape[1] // (3 * LANES)
    tokens = 2 * span
    pieces = 1 << len(masks)

    def load_rows(c):
        return pltpu.make_async_copy(rows_ref.at[c], rows.at[c], local_sems.at[0, c])

    def save_qkv(c):
        return pltpu.make_async_copy(projected.at[c % 2], qkv_ref.at[c], local_sems.at[1, c])

    def keep(c):
        return pltpu.make_async_copy(
            outgoing.at[c, 0], mixed_ref.at[0, pl.ds(c * tokens, tokens)], local_sems.at[2, c]
        )

    def keep_grad(c):
        return pltpu.make_async_copy(
            grad_ref.at[pl.ds(c * tokens, tokens)], group_ref.at[0, c], local_sems.at[3, c]
        )

    def outward(c, r):
        return remote(
            count,
            outgoing.at[c, r],
            mixed_ref.at[r, pl.ds(c * tokens, tokens)],
            out_send.at[c, r],
            out_recv.at[c, r],
            r,
        )

    def grouped(c, d):
        origin, bit = group_route(d)
        source = grad_ref.at[pl.ds(c * tokens, tokens)] if origin == 0 else group_ref.at[origin, c]
        return remote(
            count, source, group_ref.at[d, c], group_send.at[c, d], group_recv.at[c, d], masks[bit]
        )

    for c in range(chunks):
        load_rows(c).start()
    meet(count, tuple(range(1, count)) + (count,))
    when(stays, lambda: pass_block(count, block_ref, other_ref, block_sems).start())
    for c in range(chunks):
        keep_grad(c).start()
        for d in range(1, pieces):
            if group_route(d)[0] == 0:
                grouped(c, d).start()

    @pl.loop(0, chunks)
    def _(c):
        load_rows(c).wait()

        @pl.when(c >= 2)
        def _():
            save_qkv(c - 2).wait()

        @pl.loop(0, pairs)
        def _(j):
            columns = pl.ds(pl.multiple_of(j * 3 * LANES, LANES), 3 * LANES)
            block = (dot(rows[c], weight_ref[:, columns]) + bias_ref[:, columns]).astype(BF16)
            projected[c % 2, :, columns] = block
            for part, target in enumerate((queries, keys, values)):
                to_places(
                    count,
                    span,
                    lambda p: order_ref[c, p],
                    lambda p: order_ref[c, count + p],
                    lambda r: block[r * tokens : (r + 1) * tokens, part * LANES : (part + 1) * LANES],
                    target,
                )

            def one_head(head):
                lane = lax.broadcasted_iota(jnp.int32, (TILE, LANES), 1)
                mine = (lane // HEAD) == head
                for first in range(0, length, TILE):
                    last = first + TILE
                    query = jnp.where(mine, queries[first:last, :] * BF16(HEAD**-0.5), BF16(0))
                    scores = dot(query, keys[0:last, :], NT)
                    row = lax.broadcasted_iota(jnp.int32, (TILE, TILE), 0)
                    column = lax.broadcasted_iota(jnp.int32, (TILE, TILE), 1)
                    corner = jnp.where(column <= row, scores[:, first:last], -1e30)
                    scores = corner if first == 0 else jnp.concatenate([scores[:, :first], corner], axis=1)
                    row_max = jnp.max(scores, 1, keepdims=True)
                    weights = jnp.exp(scores - row_max)
                    total = jnp.sum(weights, 1, keepdims=True)
                    part = dot(weights.astype(BF16), values[0:last, :]) / total
                    lse_ref[c, j, head, first:last] = (row_max + jnp.log(total))[:, 0]
                    if head == 0:
                        mixed[first:last, :] = jnp.where(mine, part, 0.0).astype(BF16)
                    else:
                        mixed[first:last, :] = jnp.where(mine, part.astype(BF16), mixed[first:last, :])

            one_head(0)
            if odd:
                pl.when(j < pairs - 1)(lambda: one_head(1))
            else:
                one_head(1)
            lanes = pl.ds(pl.multiple_of(j * LANES, LANES), LANES)

            def put(r, half, value):
                outgoing[c, r, half * span : (half + 1) * span, lanes] = value

            from_places(
                count, span, lambda r: place_ref[c, r], lambda r: place_ref[c, count + r], mixed, put
            )

        save_qkv(c).start()
        keep(c).start()
        for r in range(1, count):
            outward(c, r).start()

    for c in range(chunks):
        keep_grad(c).wait()
    for d in range(1, pieces):
        origin = group_route(d)[0]
        for c in range(chunks):
            if origin != 0:
                grouped(c, d).start()
        for c in range(chunks):
            grouped(c, d).wait()
    for c in range(chunks):
        keep(c).wait()
        for r in range(1, count):
            outward(c, r).wait()
    for c in range(max(chunks - 2, 0), chunks):
        save_qkv(c).wait()
    when(stays, lambda: pass_block(count, block_ref, other_ref, block_sems).wait_send())
    when(jnp.logical_not(stays), lambda: pass_block(count, block_ref, other_ref, block_sems).wait_recv())


def call_forward(order, place, rows, weight, bias, grad, block, count, heads, masks):
    chunks, length, width = rows.shape
    columns = weight.shape[1]
    pairs, tokens, pieces = columns // (3 * LANES), length // count, 1 << len(masks)
    return pl.pallas_call(
        functools.partial(forward_kernel, count, tokens // 2, heads % 2 == 1, masks),
        in_specs=[SMEM, SMEM, FAR, VMEM, VMEM, FAR, FAR],
        out_specs=[FAR, FAR, VMEM, FAR, FAR],
        out_shape=[
            jax.ShapeDtypeStruct((chunks, length, columns), BF16),
            jax.ShapeDtypeStruct((count, chunks * tokens, pairs * LANES), BF16),
            jax.ShapeDtypeStruct((chunks, pairs, 2, length), F32),
            jax.ShapeDtypeStruct((pieces, chunks, tokens, width), BF16),
            jax.ShapeDtypeStruct(block.shape, BF16),
        ],
        scratch_shapes=[
            pltpu.VMEM((chunks, length, width), BF16),
            pltpu.VMEM((2, length, columns), BF16),
            pltpu.VMEM((chunks, count, tokens, pairs * LANES), BF16),
        ]
        + [pltpu.VMEM((length, LANES), BF16)] * 4
        + [pltpu.SemaphoreType.DMA((chunks, count))] * 2
        + [pltpu.SemaphoreType.DMA((chunks, pieces))] * 2
        + [pltpu.SemaphoreType.DMA((4, chunks)), pltpu.SemaphoreType.DMA((2,))],
        compiler_params=pltpu.CompilerParams(
            collective_id=2, has_side_effects=True, vmem_limit_bytes=52 * MIB
        ),
        cost_estimate=pl.CostEstimate(
            flops=chunks * (2 * length * width * columns + heads * length * length * 5 * 256),
            bytes_accessed=80 * MIB,
            transcendentals=chunks * heads * length * length,
        ),
        name="attend_forward",
    )(order, place, rows, weight, bias, grad, block)


def backward_kernel(
    count,
    span,
    odd,
    order_ref,
    place_ref,
    qkv_ref,
    grad_ref,
    lse_ref,
    weight_ref,
    out_ref,
    sum_ref,
    arrived,
    block,
    result,
    queries,
    keys,
    values,
    grads,
    query_grad,
    key_sum,
    value_sum,
    first_out,
    first_in,
    side,
    second_out,
    second_in,
    head_send,
    head_recv,
    first_send,
    first_recv,
    second_send,
    second_recv,
    local_sems,
):
    chunks, length = out_ref.shape[:2]
    pairs = weight_ref.shape[1] // (3 * LANES)
    tokens = 2 * span

    def load_qkv(c):
        return pltpu.make_async_copy(qkv_ref.at[c], block.at[c % 2], local_sems.at[0, c])

    def load_own(c):
        return pltpu.make_async_copy(
            grad_ref.at[0, pl.ds(c * tokens, tokens)], arrived.at[c, 0], local_sems.at[1, c]
        )

    def save(c):
        return pltpu.make_async_copy(result, out_ref.at[c], local_sems.at[2, c])

    def inward(c, r):
        return remote(
            count,
            grad_ref.at[r, pl.ds(c * tokens, tokens)],
            arrived.at[c, r],
            head_send.at[c, r],
            head_recv.at[c, r],
            r,
        )

    def first(c, half):
        return remote(
            count,
            first_out.at[c, half],
            first_in.at[c, half],
            first_send.at[c, half],
            first_recv.at[c, half],
            2 - half,
        )

    def second(c, r):
        return remote(
            count,
            second_out.at[c, r - 1],
            second_in.at[c, r - 1],
            second_send.at[c, r - 1],
            second_recv.at[c, r - 1],
            r,
        )

    direct_peers = (1, 2) if count == 4 else tuple(range(1, count))

    def send_sums(c):
        if count == 4:
            first(c, 0).wait_recv()
            first(c, 1).wait_recv()
            second_out[c, 0, 0:span] = (side[0, 0:span] + first_in[c, 0].astype(F32)).astype(BF16)
            second_out[c, 0, span:tokens] = side[0, span:tokens].astype(BF16)
            second_out[c, 1, 0:span] = side[1, 0:span].astype(BF16)
            second_out[c, 1, span:tokens] = (side[1, span:tokens] + first_in[c, 1].astype(F32)).astype(
                BF16
            )
        for r in direct_peers:
            second(c, r).start()

    load_qkv(0).start()
    meet(count, tuple(range(1, count)))
    for c in range(chunks):
        load_own(c).start()
        for r in range(1, count):
            inward(c, r).start()

    @pl.loop(0, chunks)
    def _(c):
        load_qkv(c).wait()

        @pl.when(c < chunks - 1)
        def _():
            load_qkv(c + 1).start()

        load_own(c).wait()
        for r in range(1, count):
            inward(c, r).wait_recv()

        @pl.when(c >= 1)
        def _():
            save(c - 1).wait()

        @pl.loop(0, pairs)
        def _(j):
            @pl.when((j == pairs - 1) & (c >= 1))
            def _():
                send_sums(c - 1)

            def place(source, target):
                to_places(
                    count,
                    span,
                    lambda p: order_ref[c, p],
                    lambda p: order_ref[c, count + p],
                    source,
                    target,
                )

            for part, target in enumerate((queries, keys, values)):
                lanes = pl.ds(pl.multiple_of(j * 3 * LANES + part * LANES, LANES), LANES)
                place(lambda r: block[c % 2, r * tokens : (r + 1) * tokens, lanes], target)
            lanes = pl.ds(pl.multiple_of(j * LANES, LANES), LANES)
            place(lambda r: arrived[c, r, :, lanes], grads)

            def one_head(head):
                lane = lax.broadcasted_iota(jnp.int32, (TILE, LANES), 1)
                mine = (lane // HEAD) == head
                for first_row in reversed(range(0, length, TILE)):
                    last = first_row + TILE
                    query = jnp.where(mine, queries[first_row:last, :] * BF16(HEAD**-0.5), BF16(0))
                    grad = jnp.where(mine, grads[first_row:last, :], BF16(0))
                    scores = dot(query, keys[0:last, :], NT)
                    row = lax.broadcasted_iota(jnp.int32, (TILE, TILE), 0)
                    column = lax.broadcasted_iota(jnp.int32, (TILE, TILE), 1)
                    corner = jnp.where(column <= row, scores[:, first_row:last], -1e30)
                    scores = (
                        corner if first_row == 0 else jnp.concatenate([scores[:, :first_row], corner], axis=1)
                    )
                    weights = jnp.exp(scores - lse_ref[c, j, head, first_row:last][:, None])
                    prob_grad = dot(grad, values[0:last, :], NT)
                    product = weights * prob_grad
                    inner = jnp.sum(product, 1, keepdims=True)
                    score_grad = (product - weights * inner).astype(BF16)
                    rounded = weights.astype(BF16)
                    part = (dot(score_grad, keys[0:last, :]) * HEAD**-0.5).astype(BF16)
                    key_part = dot(query, score_grad, TN)
                    value_part = dot(grad, rounded, TN)
                    if head == 0 and last == length:
                        key_sum[...] = key_part
                        value_sum[...] = value_part
                    else:
                        key_sum[:, 0:last] += key_part
                        value_sum[:, 0:last] += value_part
                    if head == 0:
                        query_grad[first_row:last, :] = jnp.where(mine, part, BF16(0))
                    else:
                        query_grad[first_row:last, :] = jnp.where(mine, part, query_grad[first_row:last, :])

            one_head(0)
            if odd:
                pl.when(j < pairs - 1)(lambda: one_head(1))
            else:
                one_head(1)
            keys[...] = key_sum[...].T.astype(BF16)
            values[...] = value_sum[...].T.astype(BF16)
            for part, source in enumerate((query_grad, keys, values)):
                lanes = pl.ds(pl.multiple_of(j * 3 * LANES + part * LANES, LANES), LANES)

                def put(r, half, value):
                    start = r * tokens + half * span
                    result[start : start + span, lanes] = value

                from_places(
                    count, span, lambda r: place_ref[c, r], lambda r: place_ref[c, count + r], source, put
                )

        save(c).start()

        def share(first_piece, last_piece):
            return dot(result[first_piece * tokens : last_piece * tokens, :], weight_ref[...], NT)

        if count == 4:
            far = share(2, 4)
            first_out[c, 0] = far[tokens : tokens + span].astype(BF16)
            first_out[c, 1] = far[tokens + span :].astype(BF16)
            first(c, 0).start()
            first(c, 1).start()
            side[1] = far[:tokens]
            near = share(0, 2)
            side[0] = near[tokens:]
        else:
            for r in direct_peers:
                second_out[c, r - 1] = share(r, r + 1).astype(BF16)
            near = share(0, 1)
        sum_ref[pl.ds(pl.multiple_of(c * tokens, tokens), tokens), :] = near[:tokens]

    send_sums(chunks - 1)

    for c in range(chunks):
        total = sum_ref[c * tokens : (c + 1) * tokens, :]
        for r in direct_peers:
            second(c, r).wait_recv()
            total = total + second_in[c, r - 1].astype(F32)
        sum_ref[c * tokens : (c + 1) * tokens, :] = total
        for r in direct_peers:
            second(c, r).wait_send()
        if count == 4:
            first(c, 0).wait_send()
            first(c, 1).wait_send()
        for r in range(1, count):
            inward(c, r).wait_send()
    save(chunks - 1).wait()


def call_backward(order, place, qkv, grads, lse, weight, count, heads):
    chunks, length, columns = qkv.shape
    width = weight.shape[0]
    pairs, tokens = columns // (3 * LANES), length // count
    sides = 2 if count == 4 else count - 1
    return pl.pallas_call(
        functools.partial(backward_kernel, count, tokens // 2, heads % 2 == 1),
        in_specs=[SMEM, SMEM, FAR, FAR, VMEM, VMEM],
        out_specs=[FAR, VMEM],
        out_shape=[
            jax.ShapeDtypeStruct((chunks, length, columns), BF16),
            jax.ShapeDtypeStruct((chunks * tokens, width), F32),
        ],
        scratch_shapes=[
            pltpu.VMEM((chunks, count, tokens, pairs * LANES), BF16),
            pltpu.VMEM((2, length, columns), BF16),
            pltpu.VMEM((length, columns), BF16),
        ]
        + [pltpu.VMEM((length, LANES), BF16)] * 5
        + [pltpu.VMEM((LANES, length), F32)] * 2
        + [
            pltpu.VMEM((chunks, 2, tokens // 2, width), BF16),
            pltpu.VMEM((chunks, 2, tokens // 2, width), BF16),
            pltpu.VMEM((2, tokens, width), F32),
            pltpu.VMEM((chunks, sides, tokens, width), BF16),
            pltpu.VMEM((chunks, sides, tokens, width), BF16),
        ]
        + [pltpu.SemaphoreType.DMA((chunks, count))] * 2
        + [pltpu.SemaphoreType.DMA((chunks, 2))] * 2
        + [pltpu.SemaphoreType.DMA((chunks, sides))] * 2
        + [pltpu.SemaphoreType.DMA((3, chunks))],
        compiler_params=pltpu.CompilerParams(
            collective_id=3, has_side_effects=True, vmem_limit_bytes=60 * MIB
        ),
        cost_estimate=pl.CostEstimate(
            flops=chunks * (2 * length * width * columns + heads * length * length * 8 * 256),
            bytes_accessed=80 * MIB,
            transcendentals=chunks * heads * length * length,
        ),
        name="attend_backward",
    )(order, place, qkv, grads, lse, weight)


def gelu_pair(u):
    scale = 0.7978845608028654
    square = u * u
    inner = jnp.tanh(u * (scale + scale * 0.044715 * square))
    half = 0.5 + 0.5 * inner
    slope = half + u * (half * (1.0 - inner)) * (scale + scale * 0.134145 * square)
    return u * half, slope


def load_block(stays, whole_ref, other_ref, weight, sem, start):
    if start:
        when(stays, lambda: pltpu.make_async_copy(whole_ref, weight, sem).start())
        when(jnp.logical_not(stays), lambda: pltpu.make_async_copy(other_ref, weight, sem).start())
    else:
        pltpu.make_async_copy(whole_ref, weight, sem).wait()


def hidden_kernel(
    count, masks, own_ref, whole_ref, other_ref, bias_ref, block_ref, rows_ref, value_ref, slope_ref, moved_ref,
    rows, staged, weight, group_send, group_recv, local_sems, save_sems, weight_sem, block_sems,
):
    stays = block_stays(count)
    chunks, pieces, tokens, width = rows.shape

    def keep(c):
        return pltpu.make_async_copy(own_ref.at[pl.ds(c * tokens, tokens)], rows.at[c, 0], local_sems.at[0, c])

    def save_rows(c):
        return pltpu.make_async_copy(rows.at[c], rows_ref.at[c], local_sems.at[1, c])

    def grouped(c, d):
        origin, bit = group_route(d)
        source = own_ref.at[pl.ds(c * tokens, tokens)] if origin == 0 else rows.at[c, origin]
        return remote(count, source, rows.at[c, d], group_send.at[c, d], group_recv.at[c, d], masks[bit])

    def save(n, part):
        c, i = n // pieces, n % pieces
        p = (i % 2) * 2 + i // 2
        target = value_ref.at[p, c] if part == 0 else slope_ref.at[c, p]
        return pltpu.make_async_copy(staged.at[n % 2, part], target, save_sems.at[n % 2, part])

    load_block(stays, whole_ref, other_ref, weight, weight_sem.at[0], True)
    for c in range(chunks):
        keep(c).start()
    meet(count, masks + (count // 2,))
    for c in range(chunks):
        grouped(c, 1).start()
    for c in range(chunks):
        grouped(c, 2).start()
    when(stays, lambda: pass_block(count, block_ref, moved_ref, block_sems).start())
    load_block(stays, whole_ref, other_ref, weight, weight_sem.at[0], False)

    @pl.loop(0, chunks)
    def _(c):
        keep(c).wait()

        @pl.loop(0, pieces)
        def _(i):
            p = (i % 2) * 2 + i // 2
            step = c * pieces + i

            @pl.when(i == 1)
            def _():
                grouped(c, 2).wait_recv()

            @pl.when(i == 2)
            def _():
                grouped(c, 1).wait_recv()
                grouped(c, 3).start()

            @pl.when(i == 3)
            def _():
                grouped(c, 3).wait_recv()
                save_rows(c).start()

            value, slope = gelu_pair(dot(rows[c, p], weight[...]) + bias_ref[...])

            @pl.when(step >= 2)
            def _():
                for part in range(2):
                    save(step - 2, part).wait()

            staged[step % 2, 0] = value.astype(BF16)
            staged[step % 2, 1] = slope.astype(BF16)
            for part in range(2):
                save(step, part).start()

    for c in range(chunks):
        save_rows(c).wait()
        for d in range(1, pieces):
            grouped(c, d).wait_send()
    for step in range(chunks * pieces - 2, chunks * pieces):
        for part in range(2):
            save(step, part).wait()
    when(stays, lambda: pass_block(count, block_ref, moved_ref, block_sems).wait_send())
    when(jnp.logical_not(stays), lambda: pass_block(count, block_ref, moved_ref, block_sems).wait_recv())


def call_hidden(own, whole, other, bias, block, chunks, count, masks):
    width, hidden = whole.shape
    tokens, pieces = own.shape[0] // chunks, 1 << len(masks)
    return pl.pallas_call(
        functools.partial(hidden_kernel, count, masks),
        in_specs=[FAR, FAR, FAR, VMEM, FAR],
        out_specs=[FAR] * 4,
        out_shape=[
            jax.ShapeDtypeStruct((chunks, pieces, tokens, width), BF16),
            jax.ShapeDtypeStruct((pieces, chunks, tokens, hidden), BF16),
            jax.ShapeDtypeStruct((chunks, pieces, tokens, hidden), BF16),
            jax.ShapeDtypeStruct(block.shape, BF16),
        ],
        scratch_shapes=[
            pltpu.VMEM((chunks, pieces, tokens, width), BF16),
            pltpu.VMEM((2, 2, tokens, hidden), BF16),
            pltpu.VMEM((width, hidden), BF16),
            pltpu.SemaphoreType.DMA((chunks, pieces)),
            pltpu.SemaphoreType.DMA((chunks, pieces)),
            pltpu.SemaphoreType.DMA((2, chunks)),
            pltpu.SemaphoreType.DMA((2, 2)),
            pltpu.SemaphoreType.DMA((1,)),
            pltpu.SemaphoreType.DMA((2,)),
        ],
        compiler_params=pltpu.CompilerParams(
            collective_id=4, has_side_effects=True, vmem_limit_bytes=44 * MIB
        ),
        cost_estimate=pl.CostEstimate(
            flops=2 * chunks * pieces * tokens * width * hidden, bytes_accessed=100 * MIB, transcendentals=0
        ),
        name="hidden_forward",
    )(own, whole, other, bias, block)


def group_kernel(count, masks, backward, *refs):
    if backward:
        grad_ref, slope_ref, *blocks, part_ref, other_ref, sum_ref, out_ref, staged, contract = refs[:12]
        sources = (grad_ref, slope_ref)
        targets = (contract, refs[12])
        scratch = refs[12:]
    else:
        value_ref, *blocks, residual_ref, bias_ref, part_ref, other_ref, sum_ref = refs[:8]
        sources = (value_ref,)
        targets = (refs[8],)
        scratch = refs[8:]
    weight, loaded, partial, from_core, over, from_side = scratch[:6]
    core_send, core_recv, side_send, side_recv, cargo_sems, load_sems, save_sems, weight_sems = scratch[6:]
    chunks, tokens, _ = over.shape
    steps = 4 * chunks
    high = count // 2
    stays = block_stays(count)

    def place(step):
        return lax.rem(step, 2 * chunks) // 2, 3 - step // (2 * chunks) - 2 * lax.rem(step, 2)

    def load(step, part):
        c, p = place(step)
        slot = lax.rem(step, 2)
        source = sources[part].at[p, c] if part == 0 else sources[part].at[c, p]
        return pltpu.make_async_copy(source, loaded.at[slot, part], load_sems.at[slot, part])

    def save(step):
        c, p = place(step)
        slot = lax.rem(step, 2)
        return pltpu.make_async_copy(staged.at[slot], out_ref.at[c, p], save_sems.at[slot])

    def to_core(c, p):
        return remote(
            count, partial.at[c, p], from_core.at[c, p - 2], core_send.at[c, p - 2], core_recv.at[c, p - 2], masks[1]
        )

    def to_side(c):
        return remote(count, over.at[c], from_side.at[c], side_send.at[c], side_recv.at[c], masks[0])

    def cargo():
        return pass_block(count, part_ref, other_ref, cargo_sems)

    def load_blocks(start):
        for n, target in enumerate(targets):
            load_block(stays, blocks[2 * n], blocks[2 * n + 1], target, weight_sems.at[n], start)

    load_blocks(True)
    for part in range(len(sources)):
        load(0, part).start()
    meet(count, masks + (high,))
    when(jnp.logical_not(stays), lambda: cargo().start())
    load_blocks(False)

    @pl.loop(0, steps)
    def _(step):
        c, p = place(step)
        slot = lax.rem(step, 2)
        for part in range(len(sources)):
            load(step, part).wait()

        @pl.when(step < steps - 1)
        def _():
            for part in range(len(sources)):
                load(step + 1, part).start()

        @pl.when((slot == 0) & (step >= 2) & (step <= 2 * chunks))
        def _():
            before = step // 2 - 1
            to_core(before, 3).wait_recv()
            over[before] = (partial[before, 1].astype(F32) + from_core[before, 1].astype(F32)).astype(BF16)
            to_side(before).start()

        if backward:
            hidden = dot(loaded[slot, 0], contract[...]) * loaded[slot, 1].astype(F32)
            hidden = hidden.astype(BF16)

            @pl.when(step >= 2)
            def _():
                save(step - 2).wait()

            staged[slot] = hidden
            save(step).start()
        else:
            hidden = loaded[slot, 0]
        partial[c, p] = dot(hidden, weight[...], NT).astype(BF16)

        @pl.when(p >= 2)
        def _():
            to_core(c, p).start()

    for c in range(chunks):
        to_core(c, 2).wait_recv()
        to_side(c).wait_recv()
        total = partial[c, 0].astype(F32) + from_core[c, 0].astype(F32) + from_side[c].astype(F32)
        mine = slice(c * tokens, (c + 1) * tokens)
        if backward:
            sum_ref[mine, :] = total
        else:
            sum_ref[mine, :] = (residual_ref[mine, :] + total + bias_ref[...]).astype(BF16)
        to_core(c, 2).wait_send()
        to_core(c, 3).wait_send()
        to_side(c).wait_send()
    if backward:
        for step in range(steps - 2, steps):
            save(step).wait()

    when(stays, lambda: cargo().wait_recv())
    when(jnp.logical_not(stays), lambda: cargo().wait_send())


def call_group(count, masks, backward, tiles, blocks, rest, part):
    pieces, chunks, tokens, width = tiles[0].shape
    outs = [
        jax.ShapeDtypeStruct(part.shape, BF16),
        jax.ShapeDtypeStruct((chunks * tokens, width), F32 if backward else BF16),
    ]
    scratch = [
        pltpu.VMEM((width, width), BF16),
        pltpu.VMEM((2, len(tiles), tokens, width), BF16),
        pltpu.VMEM((chunks, pieces, tokens, width), BF16),
        pltpu.VMEM((chunks, 2, tokens, width), BF16),
        pltpu.VMEM((chunks, tokens, width), BF16),
        pltpu.VMEM((chunks, tokens, width), BF16),
        pltpu.SemaphoreType.DMA((chunks, 2)),
        pltpu.SemaphoreType.DMA((chunks, 2)),
        pltpu.SemaphoreType.DMA((chunks,)),
        pltpu.SemaphoreType.DMA((chunks,)),
        pltpu.SemaphoreType.DMA((2,)),
        pltpu.SemaphoreType.DMA((2, len(tiles))),
        pltpu.SemaphoreType.DMA((2,)),
        pltpu.SemaphoreType.DMA((2,)),
    ]
    if backward:
        outs.append(jax.ShapeDtypeStruct((chunks, pieces, tokens, width), BF16))
        scratch = [pltpu.VMEM((2, tokens, width), BF16), pltpu.VMEM((width, width), BF16)] + scratch
    return pl.pallas_call(
        functools.partial(group_kernel, count, masks, backward),
        in_specs=[FAR] * (len(tiles) + len(blocks)) + [VMEM] * len(rest) + [FAR],
        out_specs=[FAR, VMEM] + [FAR] * (len(outs) - 2),
        out_shape=outs,
        scratch_shapes=scratch,
        compiler_params=pltpu.CompilerParams(
            collective_id=5 if backward else 6, has_side_effects=True, vmem_limit_bytes=56 * MIB
        ),
        cost_estimate=pl.CostEstimate(
            flops=(4 if backward else 2) * chunks * pieces * tokens * width * width,
            bytes_accessed=160 * MIB,
            transcendentals=0,
        ),
        name="group_backward" if backward else "group_forward",
    )(*tiles, *blocks, *rest, part)


def statistics(values):
    centred = values - jnp.mean(values, -1, keepdims=True)
    spread = jnp.mean(centred * centred, -1, keepdims=True)
    inverse = lax.rsqrt(spread + epsilon)
    return centred * inverse, inverse


def norm_forward(values, gain, shift):
    return (statistics(values)[0] * gain + shift).astype(BF16)


def norm_backward(values, gain, grad):
    normal, inverse = statistics(values)
    scaled = grad * gain
    spread = jnp.mean(scaled * normal, -1, keepdims=True)
    result = inverse * (scaled - jnp.mean(scaled, -1, keepdims=True) - normal * spread)
    return result, jnp.sum(grad * normal, 0), jnp.sum(grad, 0)


def body(
    seq_count,
    tp_count,
    tokens,
    positions,
    ln1_gain,
    ln1_bias,
    query_key_value_weight,
    qv_bias,
    attention_output_weight,
    attention_output_bias,
    ln2_gain,
    ln2_bias,
    expand_weight,
    expand_bias,
    contract_weight,
    contract_bias,
    cotangent,
):
    devices = seq_count * tp_count
    both = ("seq", "tp")
    t = lax.axis_index("tp")
    core = lax.axis_index("seq") % 2
    core_bit = tp_count
    tp_bits = [1 << k for k in range(tp_count.bit_length() - 1)]
    high = tp_bits[-1]
    ff_bits = tp_bits[:-1] + [core_bit]
    chunks, rows, width = tokens.shape
    span = rows // 2
    group_heads = -(-HEADS // tp_count)
    group = group_heads * HEAD
    pairs = -(-group_heads // 2)
    padded = pairs * LANES
    hidden = expand_weight.shape[1]
    peers = t ^ jnp.arange(tp_count)

    def swap(value, mask):
        return lax.ppermute(value, both, [(i, i ^ mask) for i in range(devices)])

    def after(value, *earlier):
        return lax.optimization_barrier((value, *earlier))[0]

    def choose(pieces, index):
        result = pieces[0]
        for n in range(1, len(pieces)):
            result = jnp.where(index == n, pieces[n], result)
        return result

    def gather_ff(value):
        pieces = [value]
        for bit in ff_bits:
            pieces += [swap(piece, bit) for piece in pieces]
        return pieces

    def sum_ff(pieces):
        while len(pieces) > 1:
            half = len(pieces) // 2
            bit = ff_bits[half.bit_length() - 1]
            pieces = [
                piece + swap(other, bit) for piece, other in zip(pieces[:half], pieces[half:], strict=True)
            ]
        return pieces[0]

    def sum_all(value):
        for k in range(devices.bit_length() - 1):
            value = value + swap(value, 1 << k)
        return value

    columns = query_key_value_weight.shape[1]
    feature = lax.broadcasted_iota(jnp.int32, (1, padded), 1)

    def shard_columns(owner, holder):
        found = []
        for part in range(3):
            column = part * width + holder * group + feature - columns * owner
            valid = (feature < group) & (holder * group + feature < width)
            found.append(jnp.where(valid & (column >= 0) & (column < columns), column, -1))
        return found

    def to_block(packed):
        parts = []
        for part in range(3):
            chosen = jnp.zeros_like(packed[0])
            for r in range(tp_count):
                chosen = jnp.where(shard_columns(t ^ r, t)[part] >= 0, packed[r], chosen)
            parts.append(chosen.reshape(-1, pairs, 1, LANES))
        return jnp.concatenate(parts, 2).reshape(-1, 3 * padded)

    def from_block(value):
        value = value.reshape(-1, pairs, 3, LANES)
        packed = []
        for r in range(tp_count):
            chosen = jnp.zeros((value.shape[0], padded), value.dtype)
            for part in range(3):
                here = shard_columns(t ^ r, t)[part] >= 0
                chosen = jnp.where(here, value[:, :, part].reshape(-1, padded), chosen)
            packed.append(chosen)
        return packed

    shard_index = lax.broadcasted_iota(jnp.int32, (columns, 1), 0)
    pick = []
    for r in range(tp_count):
        first, second, third = shard_columns(t, t ^ r)
        pick.append((shard_index == jnp.maximum(jnp.maximum(first, second), third)).astype(BF16))
    pick = jnp.concatenate(pick, 1)
    packed = dot(query_key_value_weight, pick).astype(BF16)
    packed = [packed[:, r * padded : (r + 1) * padded] for r in range(tp_count)]
    packed = [packed[0]] + [swap(packed[r], r) for r in range(1, tp_count)]

    flat = tokens.reshape(-1, width)
    gain_one, shift_one = ln1_gain.astype(F32), ln1_bias.astype(F32)
    gain_two, shift_two = ln2_gain.astype(F32), ln2_bias.astype(F32)
    normal_own = norm_forward(flat.astype(F32), gain_one, shift_one)
    packed[-1] = after(packed[-1], normal_own)
    qkv_rows = to_block(packed)
    qkv_weight = lax.all_gather(qkv_rows, "seq", axis=0, tiled=True)

    def head_columns(vector):
        whole = jnp.pad(vector, (0, tp_count * group - width))
        mine = lax.dynamic_slice_in_dim(whole, t * group, group)
        return jnp.pad(mine, (0, padded - group)).reshape(pairs, LANES)

    query_bias, value_bias = head_columns(qv_bias[0]), head_columns(qv_bias[1])
    qkv_bias = jnp.stack([query_bias, jnp.zeros_like(query_bias), value_bias], 1).reshape(-1)

    place = positions.reshape(chunks, tp_count, 2, span)[:, :, 0, 0] // span
    place = jnp.take(place, peers, axis=1)
    turned = (place >= tp_count).astype(jnp.int32)
    pair = jnp.minimum(place, 2 * tp_count - 1 - place)
    holds = pair[:, None, :] == jnp.arange(tp_count)[None, :, None]
    holder = jnp.sum(jnp.where(holds, jnp.arange(tp_count), 0), 2)
    orders = jnp.concatenate([holder, jnp.sum(jnp.where(holds, turned[:, None, :], 0), 2)], 1).astype(jnp.int32)
    places = jnp.concatenate([pair, turned], 1).astype(jnp.int32)
    masks = tuple(ff_bits)
    members = 1 << len(masks)

    stays = core == t // high
    block = t % high + core * high
    send = [
        (s * tp_count + i, s * tp_count + (i ^ high))
        for s in range(seq_count)
        for i in range(tp_count)
        if s % 2 == i // high
    ]

    def gather_seq(shard):
        return lax.all_gather(shard, "seq", axis=0, tiled=True)

    def take_block(whole):
        return lax.ppermute(whole, both, send)

    def give_block(partial):
        return lax.ppermute(partial, both, [(b, a) for a, b in send])

    def keep_block(partial, other):
        return jnp.where(stays, partial.astype(F32) + other, 0.0).astype(BF16)

    def sum_seq(partial):
        return after(lax.psum_scatter(partial, "seq", scatter_dimension=0, tiled=True))

    shards = [attention_output_weight] + [swap(attention_output_weight, r) for r in range(1, tp_count)]
    out_row = jnp.concatenate([choose(shards, t ^ a) for a in range(tp_count)], 1)
    normal_one = gather_rows(after(normal_own, out_row, qkv_rows), chunks, tp_count)
    expand_whole = gather_seq(expand_weight)
    contract_whole = gather_seq(after(contract_weight.T, normal_one))
    hidden_bias = lax.dynamic_slice_in_dim(expand_bias, block * hidden, hidden).astype(F32)

    out_weight = gather_seq(after(out_row, normal_one))

    qkv, heads_out, lse, output_rows, expand_other = call_forward(
        orders,
        places,
        normal_one,
        qkv_weight,
        qkv_bias.astype(F32).reshape(1, -1),
        cotangent.reshape(-1, width),
        expand_whole,
        tp_count,
        group_heads,
        masks,
    )
    pieces = [heads_out[r, :, :group] for r in range(tp_count)]
    mixed = jnp.concatenate([choose(pieces, t ^ a) for a in range(tp_count)], 1)[:, :width]
    residual = flat.astype(F32) + dot(mixed, out_weight) + attention_output_bias
    normal = norm_forward(residual, gain_two, shift_two)

    def second_norm_back(norm_grad):
        from_norm, gain_two_grad, shift_two_grad = norm_backward(residual, gain_two, norm_grad)
        resid_grad = cotangent.reshape(-1, width).astype(F32) + from_norm
        branch = resid_grad.astype(BF16)
        head_grad = dot(branch, out_weight, NT).astype(BF16)
        head_grad = jnp.pad(head_grad, ((0, 0), (0, tp_count * group - width)))
        pieces = [head_grad[:, a * group : (a + 1) * group] for a in range(tp_count)]
        pieces = [jnp.pad(choose(pieces, t ^ r), ((0, 0), (0, padded - group))) for r in range(tp_count)]
        out_part = dot(mixed, branch, TN).astype(BF16)
        out_grad = sum_seq(out_part)
        return gain_two_grad, shift_two_grad, resid_grad, branch, jnp.stack(pieces), out_grad

    flat_rows = output_rows.reshape(-1, width)
    if tp_count == 4:
        normal_two, value, slope, contract_other = call_hidden(
            normal,
            expand_whole,
            expand_other,
            hidden_bias.reshape(1, -1),
            contract_whole,
            chunks,
            tp_count,
            masks,
        )
        value = value.reshape(-1, hidden)
        contract_grad = dot(flat_rows, value, TN).astype(BF16)
        other, norm_grad, hidden_grad = call_group(
            tp_count,
            masks,
            True,
            [output_rows, slope],
            [contract_whole, contract_other, expand_whole, expand_other],
            [],
            contract_grad,
        )
        contract_grad = keep_block(contract_grad, other)
        proj_weight_grad = sum_seq(contract_grad)
        normal_two, hidden_grad = normal_two.reshape(-1, width), hidden_grad.reshape(-1, hidden)
        expand_grad = dot(normal_two, after(hidden_grad, contract_grad), TN).astype(BF16)
        from_second = second_norm_back(norm_grad)
        expand_grad = after(expand_grad, proj_weight_grad, from_second[4])
        other, layer_out = call_group(
            tp_count,
            masks,
            False,
            [value.reshape(members, chunks, rows, hidden)],
            [contract_whole, contract_other],
            [residual, contract_bias.astype(F32).reshape(1, -1)],
            expand_grad,
        )
        expand_grad = keep_block(expand_grad, other)
    else:
        expand = jnp.where(stays, expand_whole, expand_other)
        contract = jnp.where(stays, contract_whole, take_block(contract_whole))
        normal_two = jnp.concatenate(gather_ff(normal), 0)
        value, slope = gelu_pair(dot(normal_two, expand) + hidden_bias)
        value = value.astype(BF16)
        contract_grad = dot(flat_rows, value, TN).astype(BF16)
        hidden_grad = (dot(flat_rows, contract) * slope).astype(BF16)
        partial = dot(hidden_grad, expand, NT).astype(BF16).reshape(members, -1, width)
        from_second = second_norm_back(sum_ff([partial[d] for d in range(members)]).astype(F32))
        proj_weight_grad = sum_seq(keep_block(contract_grad, give_block(contract_grad)))
        expand_grad = dot(normal_two, hidden_grad, TN).astype(BF16)
        expand_grad = keep_block(expand_grad, give_block(expand_grad))
        members_value = value.reshape(members, -1, hidden)
        feed = [dot(members_value[d], contract, NT).astype(BF16) for d in range(members)]
        layer_out = (residual + sum_ff(feed) + contract_bias).astype(BF16)
    fc_weight_grad = sum_seq(expand_grad)
    hidden_bias_grad = jnp.sum(hidden_grad, 0, dtype=F32)

    gain_two_grad, shift_two_grad, resid_grad, branch, head_grads, out_grad = from_second
    qkv_grads, one_grad = call_backward(
        orders,
        places,
        after(qkv, expand_grad, out_grad),
        head_grads,
        lse,
        qkv_weight,
        tp_count,
        group_heads,
    )
    qkv_grads = after(qkv_grads, fc_weight_grad)
    out_grad = [out_grad[:, a * (width // tp_count) : (a + 1) * (width // tp_count)] for a in range(tp_count)]
    out_weight_grad = choose(out_grad, t).astype(F32)
    for r in range(1, tp_count):
        out_weight_grad = out_weight_grad + swap(choose(out_grad, t ^ r), r)

    qkv_grads = qkv_grads.reshape(-1, 3 * padded)
    qkv_grad = dot(normal_one.reshape(-1, width), qkv_grads, TN)
    qkv_bias_grad = jnp.sum(qkv_grads, 0, dtype=F32)
    from_norm, gain_one_grad, shift_one_grad = norm_backward(flat.astype(F32), gain_one, one_grad)
    input_grad = (resid_grad + from_norm).astype(BF16).reshape(tokens.shape)

    summed = lax.psum_scatter(qkv_grad.astype(BF16), "seq", scatter_dimension=0, tiled=True)
    qkv_bias_grad = qkv_bias_grad.reshape(pairs, 3, LANES)

    def whole_bias(part):
        mine = qkv_bias_grad[:, part].reshape(-1)[:group]
        whole = jnp.zeros((tp_count * group,), F32)
        return lax.dynamic_update_slice_in_dim(whole, mine, t * group, 0)[:width]

    hidden_whole = lax.dynamic_update_slice_in_dim(
        jnp.zeros(expand_bias.shape, F32), hidden_bias_grad, block * hidden, 0
    )
    out_bias_part = jnp.sum(branch, 0, dtype=F32)
    proj_bias_part = jnp.sum(cotangent, axis=(0, 1), dtype=F32)
    vector = sum_all(
        jnp.concatenate(
            [
                gain_two_grad,
                shift_two_grad,
                out_bias_part,
                proj_bias_part,
                gain_one_grad,
                shift_one_grad,
                whole_bias(0),
                whole_bias(2),
                hidden_whole,
            ]
        )
    )
    packed = from_block(after(summed, vector, input_grad))
    packed = [packed[0]] + [swap(packed[r], r) for r in range(1, tp_count)]
    qkv_weight_grad = dot(jnp.concatenate(packed, 1), pick, NT)

    def part(vector, index):
        return vector[index * width : (index + 1) * width]

    return (
        layer_out.reshape(tokens.shape),
        input_grad,
        part(vector, 4),
        part(vector, 5),
        qkv_weight_grad,
        vector[6 * width : 8 * width].reshape(2, width),
        out_weight_grad,
        part(vector, 2),
        part(vector, 0),
        part(vector, 1),
        fc_weight_grad.astype(F32),
        vector[8 * width :],
        proj_weight_grad.astype(F32).T,
        part(vector, 3),
    )


def solution(mesh):
    in_specs = (
        P("seq", "tp", None),
        P("seq", None),
        P(),
        P(),
        P("seq", "tp"),
        P(),
        P("seq", "tp"),
        P(),
        P(),
        P(),
        P("seq", "tp"),
        P(),
        P("tp", "seq"),
        P(),
        P("seq", "tp", None),
    )
    out_specs = (
        P("seq", "tp", None),
        P("seq", "tp", None),
        P(),
        P(),
        P("seq", "tp"),
        P(),
        P("seq", "tp"),
        P(),
        P(),
        P(),
        P("seq", "tp"),
        P(),
        P("tp", "seq"),
        P(),
    )
    placed = functools.partial(body, mesh.shape["seq"], mesh.shape["tp"])
    return jax.shard_map(placed, mesh=mesh, in_specs=in_specs, out_specs=out_specs, check_vma=False)
```

```python
import functools
import jax
import jax.numpy as jnp
from jax import lax
from jax.experimental import pallas as pl
from jax.experimental.pallas import tpu as pltpu
from jax.sharding import PartitionSpec as P

HEADS = 25
HEAD = 64
LANES = 128
TILE = 256
epsilon = 1e-05
F32 = jnp.float32
BF16 = jnp.bfloat16
NN = (((1,), (0,)), ((), ()))
NT = (((1,), (1,)), ((), ()))
TN = (((0,), (0,)), ((), ()))
MIB = 2**20
VMEM = pl.BlockSpec(memory_space=pltpu.VMEM)
SMEM = pl.BlockSpec(memory_space=pltpu.SMEM)
FAR = pl.BlockSpec(memory_space=pl.ANY)


def dot(left, right, dims=NN):
    return lax.dot_general(left, right, dims, preferred_element_type=F32)


def peer_id(count, mask):
    if mask < count:
        return {"tp": lax.axis_index("tp") ^ mask}
    return {"seq": lax.axis_index("seq") ^ 1}


def meet(count, masks):
    barrier = pltpu.get_barrier_semaphore()
    for mask in masks:
        pl.semaphore_signal(barrier, inc=1, device_id=peer_id(count, mask), device_id_type=pl.DeviceIdType.MESH)
    pl.semaphore_wait(barrier, len(masks))


def remote(count, source, target, send, recv, mask):
    return pltpu.make_async_remote_copy(
        src_ref=source,
        dst_ref=target,
        send_sem=send,
        recv_sem=recv,
        device_id=peer_id(count, mask),
        device_id_type=pl.DeviceIdType.MESH,
    )


def block_stays(count):
    return lax.rem(lax.axis_index("seq"), 2) == lax.axis_index("tp") // (count // 2)


def pass_block(count, source, target, sems):
    return remote(count, source, target, sems.at[0], sems.at[1], count // 2)


def when(condition, action):
    pl.when(condition)(action)


def gather_kernel(count, tokens, own_ref, rows_ref, send_sems, recv_sems, local_sems):
    chunks = rows_ref.shape[0]
    span = tokens // 2
    direct_peers = (1, 2) if count == 4 else tuple(range(1, count))
    meet(count, direct_peers)

    def own(c):
        return pltpu.make_async_copy(
            own_ref.at[pl.ds(c * tokens, tokens)], rows_ref.at[c, pl.ds(0, tokens)], local_sems.at[c]
        )

    def direct(c, r):
        return remote(
            count,
            own_ref.at[pl.ds(c * tokens, tokens)],
            rows_ref.at[c, pl.ds(r * tokens, tokens)],
            send_sems.at[c, r],
            recv_sems.at[c, r],
            r,
        )

    def passed(c, half):
        start = (tokens, 2 * tokens + span)[half]
        return remote(
            count,
            rows_ref.at[c, pl.ds(start, span)],
            rows_ref.at[c, pl.ds(3 * tokens + half * span, span)],
            send_sems.at[c, 3 * half],
            recv_sems.at[c, 3 * half],
            2 - half,
        )

    for c in range(chunks):
        own(c).start()
        for r in direct_peers:
            direct(c, r).start()
    for c in range(chunks):
        for r in direct_peers:
            direct(c, r).wait_recv()
        if count == 4:
            passed(c, 0).start()
            passed(c, 1).start()
    for c in range(chunks):
        own(c).wait()
        for r in direct_peers:
            direct(c, r).wait_send()
        if count == 4:
            passed(c, 0).wait()
            passed(c, 1).wait()


def gather_rows(own, chunks, count):
    tokens = own.shape[0] // chunks
    return pl.pallas_call(
        functools.partial(gather_kernel, count, tokens),
        in_specs=[FAR],
        out_specs=FAR,
        out_shape=jax.ShapeDtypeStruct((chunks, tokens * count, own.shape[1]), BF16),
        scratch_shapes=[pltpu.SemaphoreType.DMA((chunks, count))] * 2 + [pltpu.SemaphoreType.DMA((chunks,))],
        compiler_params=pltpu.CompilerParams(collective_id=1, has_side_effects=True),
        cost_estimate=pl.CostEstimate(flops=0, bytes_accessed=120 * MIB, transcendentals=0),
        name="gather_rows",
    )(own)


def pick_one(index, options):
    result = options(0)
    for n in range(1, index[1]):
        result = lax.select(index[0] == n, options(n), result)
    return result


def to_places(count, span, holder, turned, source, target):
    for p in range(count):
        piece = pick_one((holder(p), count), source)
        first, second = piece[:span], piece[span:]
        swap = turned(p) == 1
        high = 2 * count - 1 - p
        target[p * span : (p + 1) * span, :] = lax.select(swap, second, first)
        target[high * span : (high + 1) * span, :] = lax.select(swap, first, second)


def from_places(count, span, pair, turned, source, store):
    for r in range(count):
        low = pick_one((pair(r), count), lambda p: source[p * span : (p + 1) * span, :])
        high = pick_one(
            (pair(r), count),
            lambda p: source[(2 * count - 1 - p) * span : (2 * count - p) * span, :],
        )
        swap = turned(r) == 1
        store(r, 0, lax.select(swap, high, low))
        store(r, 1, lax.select(swap, low, high))


def group_route(d):
    bit = d.bit_length() - 1
    return d - (1 << bit), bit


def forward_kernel(
    count,
    span,
    odd,
    masks,
    order_ref,
    place_ref,
    rows_ref,
    weight_ref,
    bias_ref,
    grad_ref,
    block_ref,
    qkv_ref,
    mixed_ref,
    lse_ref,
    group_ref,
    other_ref,
    rows,
    projected,
    outgoing,
    queries,
    keys,
    values,
    mixed,
    out_send,
    out_recv,
    group_send,
    group_recv,
    local_sems,
    block_sems,
):
    stays = block_stays(count)
    chunks, length, _ = rows.shape
    pairs = weight_ref.shape[1] // (3 * LANES)
    tokens = 2 * span
    pieces = 1 << len(masks)

    def load_rows(c):
        return pltpu.make_async_copy(rows_ref.at[c], rows.at[c], local_sems.at[0, c])

    def save_qkv(c):
        return pltpu.make_async_copy(projected.at[c % 2], qkv_ref.at[c], local_sems.at[1, c])

    def keep(c):
        return pltpu.make_async_copy(
            outgoing.at[c, 0], mixed_ref.at[0, pl.ds(c * tokens, tokens)], local_sems.at[2, c]
        )

    def keep_grad(c):
        return pltpu.make_async_copy(
            grad_ref.at[pl.ds(c * tokens, tokens)], group_ref.at[0, c], local_sems.at[3, c]
        )

    def outward(c, r):
        return remote(
            count,
            outgoing.at[c, r],
            mixed_ref.at[r, pl.ds(c * tokens, tokens)],
            out_send.at[c, r],
            out_recv.at[c, r],
            r,
        )

    def grouped(c, d):
        origin, bit = group_route(d)
        source = grad_ref.at[pl.ds(c * tokens, tokens)] if origin == 0 else group_ref.at[origin, c]
        return remote(
            count, source, group_ref.at[d, c], group_send.at[c, d], group_recv.at[c, d], masks[bit]
        )

    for c in range(chunks):
        load_rows(c).start()
    meet(count, tuple(range(1, count)) + (count,))
    when(stays, lambda: pass_block(count, block_ref, other_ref, block_sems).start())
    for c in range(chunks):
        keep_grad(c).start()
        for d in range(1, pieces):
            if group_route(d)[0] == 0:
                grouped(c, d).start()

    @pl.loop(0, chunks)
    def _(c):
        load_rows(c).wait()

        @pl.when(c >= 2)
        def _():
            save_qkv(c - 2).wait()

        @pl.loop(0, pairs)
        def _(j):
            columns = pl.ds(pl.multiple_of(j * 3 * LANES, LANES), 3 * LANES)
            block = (dot(rows[c], weight_ref[:, columns]) + bias_ref[:, columns]).astype(BF16)
            projected[c % 2, :, columns] = block
            for part, target in enumerate((queries, keys, values)):
                to_places(
                    count,
                    span,
                    lambda p: order_ref[c, p],
                    lambda p: order_ref[c, count + p],
                    lambda r: block[r * tokens : (r + 1) * tokens, part * LANES : (part + 1) * LANES],
                    target,
                )

            def one_head(head):
                lane = lax.broadcasted_iota(jnp.int32, (TILE, LANES), 1)
                mine = (lane // HEAD) == head
                for first in range(0, length, TILE):
                    last = first + TILE
                    query = jnp.where(mine, queries[first:last, :] * BF16(HEAD**-0.5), BF16(0))
                    scores = dot(query, keys[0:last, :], NT)
                    row = lax.broadcasted_iota(jnp.int32, (TILE, TILE), 0)
                    column = lax.broadcasted_iota(jnp.int32, (TILE, TILE), 1)
                    corner = jnp.where(column <= row, scores[:, first:last], -1e30)
                    scores = corner if first == 0 else jnp.concatenate([scores[:, :first], corner], axis=1)
                    row_max = jnp.max(scores, 1, keepdims=True)
                    weights = jnp.exp(scores - row_max)
                    total = jnp.sum(weights, 1, keepdims=True)
                    part = dot(weights.astype(BF16), values[0:last, :]) / total
                    lse_ref[c, j, head, first:last] = (row_max + jnp.log(total))[:, 0]
                    if head == 0:
                        mixed[first:last, :] = jnp.where(mine, part, 0.0).astype(BF16)
                    else:
                        mixed[first:last, :] = jnp.where(mine, part.astype(BF16), mixed[first:last, :])

            one_head(0)
            if odd:
                pl.when(j < pairs - 1)(lambda: one_head(1))
            else:
                one_head(1)
            lanes = pl.ds(pl.multiple_of(j * LANES, LANES), LANES)

            def put(r, half, value):
                outgoing[c, r, half * span : (half + 1) * span, lanes] = value

            from_places(
                count, span, lambda r: place_ref[c, r], lambda r: place_ref[c, count + r], mixed, put
            )

        save_qkv(c).start()
        keep(c).start()
        for r in range(1, count):
            outward(c, r).start()

    for c in range(chunks):
        keep_grad(c).wait()
    for d in range(1, pieces):
        origin = group_route(d)[0]
        for c in range(chunks):
            if origin != 0:
                grouped(c, d).start()
        for c in range(chunks):
            grouped(c, d).wait()
    for c in range(chunks):
        keep(c).wait()
        for r in range(1, count):
            outward(c, r).wait()
    for c in range(max(chunks - 2, 0), chunks):
        save_qkv(c).wait()
    when(stays, lambda: pass_block(count, block_ref, other_ref, block_sems).wait_send())
    when(jnp.logical_not(stays), lambda: pass_block(count, block_ref, other_ref, block_sems).wait_recv())


def call_forward(order, place, rows, weight, bias, grad, block, count, heads, masks):
    chunks, length, width = rows.shape
    columns = weight.shape[1]
    pairs, tokens, pieces = columns // (3 * LANES), length // count, 1 << len(masks)
    return pl.pallas_call(
        functools.partial(forward_kernel, count, tokens // 2, heads % 2 == 1, masks),
        in_specs=[SMEM, SMEM, FAR, VMEM, VMEM, FAR, FAR],
        out_specs=[FAR, FAR, VMEM, FAR, FAR],
        out_shape=[
            jax.ShapeDtypeStruct((chunks, length, columns), BF16),
            jax.ShapeDtypeStruct((count, chunks * tokens, pairs * LANES), BF16),
            jax.ShapeDtypeStruct((chunks, pairs, 2, length), F32),
            jax.ShapeDtypeStruct((pieces, chunks, tokens, width), BF16),
            jax.ShapeDtypeStruct(block.shape, BF16),
        ],
        scratch_shapes=[
            pltpu.VMEM((chunks, length, width), BF16),
            pltpu.VMEM((2, length, columns), BF16),
            pltpu.VMEM((chunks, count, tokens, pairs * LANES), BF16),
        ]
        + [pltpu.VMEM((length, LANES), BF16)] * 4
        + [pltpu.SemaphoreType.DMA((chunks, count))] * 2
        + [pltpu.SemaphoreType.DMA((chunks, pieces))] * 2
        + [pltpu.SemaphoreType.DMA((4, chunks)), pltpu.SemaphoreType.DMA((2,))],
        compiler_params=pltpu.CompilerParams(
            collective_id=2, has_side_effects=True, vmem_limit_bytes=52 * MIB
        ),
        cost_estimate=pl.CostEstimate(
            flops=chunks * (2 * length * width * columns + heads * length * length * 5 * 256),
            bytes_accessed=80 * MIB,
            transcendentals=chunks * heads * length * length,
        ),
        name="attend_forward",
    )(order, place, rows, weight, bias, grad, block)


def backward_kernel(
    count,
    span,
    odd,
    order_ref,
    place_ref,
    qkv_ref,
    grad_ref,
    lse_ref,
    weight_ref,
    rows_ref,
    out_ref,
    sum_ref,
    product_ref,
    bias_ref,
    arrived,
    block,
    result,
    queries,
    keys,
    values,
    grads,
    query_grad,
    key_sum,
    value_sum,
    first_out,
    first_in,
    side,
    second_out,
    second_in,
    head_send,
    head_recv,
    first_send,
    first_recv,
    second_send,
    second_recv,
    local_sems,
    left,
    right,
    product,
    rounded_product,
    tile_sems,
    product_sem,
):
    chunks, length = out_ref.shape[:2]
    pairs = weight_ref.shape[1] // (3 * LANES)
    tokens = 2 * span

    def load_qkv(c):
        return pltpu.make_async_copy(qkv_ref.at[c], block.at[c % 2], local_sems.at[0, c])

    def load_own(c):
        return pltpu.make_async_copy(
            grad_ref.at[0, pl.ds(c * tokens, tokens)], arrived.at[c, 0], local_sems.at[1, c]
        )

    def save(c):
        return pltpu.make_async_copy(result, out_ref.at[c], local_sems.at[2, c])

    def inward(c, r):
        return remote(
            count,
            grad_ref.at[r, pl.ds(c * tokens, tokens)],
            arrived.at[c, r],
            head_send.at[c, r],
            head_recv.at[c, r],
            r,
        )

    def first(c, half):
        return remote(
            count,
            first_out.at[c, half],
            first_in.at[c, half],
            first_send.at[c, half],
            first_recv.at[c, half],
            2 - half,
        )

    def second(c, r):
        return remote(
            count,
            second_out.at[c, r - 1],
            second_in.at[c, r - 1],
            second_send.at[c, r - 1],
            second_recv.at[c, r - 1],
            r,
        )

    direct_peers = (1, 2) if count == 4 else tuple(range(1, count))

    def send_sums(c):
        if count == 4:
            first(c, 0).wait_recv()
            first(c, 1).wait_recv()
            second_out[c, 0, 0:span] = (side[0, 0:span] + first_in[c, 0].astype(F32)).astype(BF16)
            second_out[c, 0, span:tokens] = side[0, span:tokens].astype(BF16)
            second_out[c, 1, 0:span] = side[1, 0:span].astype(BF16)
            second_out[c, 1, span:tokens] = (side[1, span:tokens] + first_in[c, 1].astype(F32)).astype(
                BF16
            )
        for r in direct_peers:
            second(c, r).start()

    load_qkv(0).start()
    meet(count, tuple(range(1, count)))
    for c in range(chunks):
        load_own(c).start()
        for r in range(1, count):
            inward(c, r).start()

    @pl.loop(0, chunks)
    def _(c):
        load_qkv(c).wait()

        @pl.when(c < chunks - 1)
        def _():
            load_qkv(c + 1).start()

        load_own(c).wait()
        for r in range(1, count):
            inward(c, r).wait_recv()

        @pl.when(c >= 1)
        def _():
            save(c - 1).wait()

        @pl.loop(0, pairs)
        def _(j):
            @pl.when((j == pairs - 1) & (c >= 1))
            def _():
                send_sums(c - 1)

            def place(source, target):
                to_places(
                    count,
                    span,
                    lambda p: order_ref[c, p],
                    lambda p: order_ref[c, count + p],
                    source,
                    target,
                )

            for part, target in enumerate((queries, keys, values)):
                lanes = pl.ds(pl.multiple_of(j * 3 * LANES + part * LANES, LANES), LANES)
                place(lambda r: block[c % 2, r * tokens : (r + 1) * tokens, lanes], target)
            lanes = pl.ds(pl.multiple_of(j * LANES, LANES), LANES)
            place(lambda r: arrived[c, r, :, lanes], grads)

            def one_head(head):
                lane = lax.broadcasted_iota(jnp.int32, (TILE, LANES), 1)
                mine = (lane // HEAD) == head
                for first_row in reversed(range(0, length, TILE)):
                    last = first_row + TILE
                    query = jnp.where(mine, queries[first_row:last, :] * BF16(HEAD**-0.5), BF16(0))
                    grad = jnp.where(mine, grads[first_row:last, :], BF16(0))
                    scores = dot(query, keys[0:last, :], NT)
                    row = lax.broadcasted_iota(jnp.int32, (TILE, TILE), 0)
                    column = lax.broadcasted_iota(jnp.int32, (TILE, TILE), 1)
                    corner = jnp.where(column <= row, scores[:, first_row:last], -1e30)
                    scores = (
                        corner if first_row == 0 else jnp.concatenate([scores[:, :first_row], corner], axis=1)
                    )
                    weights = jnp.exp(scores - lse_ref[c, j, head, first_row:last][:, None])
                    prob_grad = dot(grad, values[0:last, :], NT)
                    product = weights * prob_grad
                    inner = jnp.sum(product, 1, keepdims=True)
                    score_grad = (product - weights * inner).astype(BF16)
                    rounded = weights.astype(BF16)
                    part = (dot(score_grad, keys[0:last, :]) * HEAD**-0.5).astype(BF16)
                    key_part = dot(query, score_grad, TN)
                    value_part = dot(grad, rounded, TN)
                    if head == 0 and last == length:
                        key_sum[...] = key_part
                        value_sum[...] = value_part
                    else:
                        key_sum[:, 0:last] += key_part
                        value_sum[:, 0:last] += value_part
                    if head == 0:
                        query_grad[first_row:last, :] = jnp.where(mine, part, BF16(0))
                    else:
                        query_grad[first_row:last, :] = jnp.where(mine, part, query_grad[first_row:last, :])

            one_head(0)
            if odd:
                pl.when(j < pairs - 1)(lambda: one_head(1))
            else:
                one_head(1)
            keys[...] = key_sum[...].T.astype(BF16)
            values[...] = value_sum[...].T.astype(BF16)
            for part, source in enumerate((query_grad, keys, values)):
                lanes = pl.ds(pl.multiple_of(j * 3 * LANES + part * LANES, LANES), LANES)

                def put(r, half, value):
                    start = r * tokens + half * span
                    result[start : start + span, lanes] = value

                from_places(
                    count, span, lambda r: place_ref[c, r], lambda r: place_ref[c, count + r], source, put
                )

        save(c).start()

        def share(first_piece, last_piece):
            return dot(result[first_piece * tokens : last_piece * tokens, :], weight_ref[...], NT)

        if count == 4:
            far = share(2, 4)
            first_out[c, 0] = far[tokens : tokens + span].astype(BF16)
            first_out[c, 1] = far[tokens + span :].astype(BF16)
            first(c, 0).start()
            first(c, 1).start()
            side[1] = far[:tokens]
            near = share(0, 2)
            side[0] = near[tokens:]
        else:
            for r in direct_peers:
                second_out[c, r - 1] = share(r, r + 1).astype(BF16)
            near = share(0, 1)
        sum_ref[pl.ds(pl.multiple_of(c * tokens, tokens), tokens), :] = near[:tokens]

    save(chunks - 1).wait()
    depth, third = left.shape[1], product.shape[1]
    tiles = length // depth
    rounds = chunks * tiles

    def load(n, side_index):
        c, k = lax.rem(n, rounds) // tiles, lax.rem(n, tiles)
        span_rows = pl.ds(pl.multiple_of(k * depth, depth), depth)
        slot = lax.rem(n, 2)
        if side_index == 0:
            source, target = rows_ref.at[c, span_rows], left.at[slot]
        else:
            lanes = pl.ds(pl.multiple_of(n // rounds * third, third), third)
            source, target = out_ref.at[c, span_rows, lanes], right.at[slot]
        return pltpu.make_async_copy(source, target, tile_sems.at[slot, side_index])

    def save_product(part):
        lanes = pl.ds(pl.multiple_of(part * third, third), third)
        return pltpu.make_async_copy(rounded_product, product_ref.at[:, lanes], product_sem.at[0])

    for side_index in range(2):
        load(0, side_index).start()

    @pl.loop(0, 3 * rounds)
    def _(n):
        slot = lax.rem(n, 2)
        part = n // rounds
        lanes = pl.ds(pl.multiple_of(part * third, third), third)
        for side_index in range(2):
            load(n, side_index).wait()

        @pl.when(n < 3 * rounds - 1)
        def _():
            for side_index in range(2):
                load(n + 1, side_index).start()

        @pl.when(n == rounds)
        def _():
            send_sums(chunks - 1)

        term = dot(left[slot], right[slot], TN)
        column_sum = jnp.sum(right[slot].astype(F32), 0, keepdims=True)

        @pl.when(lax.rem(n, rounds) == 0)
        def _():
            product[...] = term
            bias_ref[:, lanes] = column_sum

        @pl.when(lax.rem(n, rounds) != 0)
        def _():
            product[...] += term
            bias_ref[:, lanes] += column_sum

        @pl.when(lax.rem(n, rounds) == rounds - 1)
        def _():
            when(part >= 1, lambda: save_product(part - 1).wait())
            rounded_product[...] = product[...].astype(BF16)
            save_product(part).start()

    for c in range(chunks):
        total = sum_ref[c * tokens : (c + 1) * tokens, :]
        for r in direct_peers:
            second(c, r).wait_recv()
            total = total + second_in[c, r - 1].astype(F32)
        sum_ref[c * tokens : (c + 1) * tokens, :] = total
        for r in direct_peers:
            second(c, r).wait_send()
        if count == 4:
            first(c, 0).wait_send()
            first(c, 1).wait_send()
        for r in range(1, count):
            inward(c, r).wait_send()
    save_product(2).wait()


def call_backward(order, place, qkv, grads, lse, weight, rows, count, heads):
    chunks, length, columns = qkv.shape
    width = weight.shape[0]
    pairs, tokens = columns // (3 * LANES), length // count
    sides = 2 if count == 4 else count - 1
    return pl.pallas_call(
        functools.partial(backward_kernel, count, tokens // 2, heads % 2 == 1),
        in_specs=[SMEM, SMEM, FAR, FAR, VMEM, VMEM, FAR],
        out_specs=[FAR, VMEM, FAR, VMEM],
        out_shape=[
            jax.ShapeDtypeStruct((chunks, length, columns), BF16),
            jax.ShapeDtypeStruct((chunks * tokens, width), F32),
            jax.ShapeDtypeStruct((width, columns), BF16),
            jax.ShapeDtypeStruct((1, columns), F32),
        ],
        scratch_shapes=[
            pltpu.VMEM((chunks, count, tokens, pairs * LANES), BF16),
            pltpu.VMEM((2, length, columns), BF16),
            pltpu.VMEM((length, columns), BF16),
        ]
        + [pltpu.VMEM((length, LANES), BF16)] * 5
        + [pltpu.VMEM((LANES, length), F32)] * 2
        + [
            pltpu.VMEM((chunks, 2, tokens // 2, width), BF16),
            pltpu.VMEM((chunks, 2, tokens // 2, width), BF16),
            pltpu.VMEM((2, tokens, width), F32),
            pltpu.VMEM((chunks, sides, tokens, width), BF16),
            pltpu.VMEM((chunks, sides, tokens, width), BF16),
        ]
        + [pltpu.SemaphoreType.DMA((chunks, count))] * 2
        + [pltpu.SemaphoreType.DMA((chunks, 2))] * 2
        + [pltpu.SemaphoreType.DMA((chunks, sides))] * 2
        + [
            pltpu.SemaphoreType.DMA((3, chunks)),
            pltpu.VMEM((2, 2 * tokens, width), BF16),
            pltpu.VMEM((2, 2 * tokens, columns // 3), BF16),
            pltpu.VMEM((width, columns // 3), F32),
            pltpu.VMEM((width, columns // 3), BF16),
            pltpu.SemaphoreType.DMA((2, 2)),
            pltpu.SemaphoreType.DMA((1,)),
        ],
        compiler_params=pltpu.CompilerParams(
            collective_id=3, has_side_effects=True, vmem_limit_bytes=60 * MIB
        ),
        cost_estimate=pl.CostEstimate(
            flops=chunks * (2 * length * width * columns + heads * length * length * 8 * 256),
            bytes_accessed=80 * MIB,
            transcendentals=chunks * heads * length * length,
        ),
        name="attend_backward",
    )(order, place, qkv, grads, lse, weight, rows)


def gelu_pair(u):
    scale = 0.7978845608028654
    square = u * u
    inner = jnp.tanh(u * (scale + scale * 0.044715 * square))
    half = 0.5 + 0.5 * inner
    slope = half + u * (half * (1.0 - inner)) * (scale + scale * 0.134145 * square)
    return u * half, slope


def load_block(stays, whole_ref, other_ref, weight, sem, start):
    if start:
        when(stays, lambda: pltpu.make_async_copy(whole_ref, weight, sem).start())
        when(jnp.logical_not(stays), lambda: pltpu.make_async_copy(other_ref, weight, sem).start())
    else:
        pltpu.make_async_copy(whole_ref, weight, sem).wait()


def hidden_kernel(
    count, masks, own_ref, whole_ref, other_ref, bias_ref, block_ref, rows_ref, value_ref, slope_ref, moved_ref,
    rows, staged, weight, group_send, group_recv, local_sems, save_sems, weight_sem, block_sems,
):
    stays = block_stays(count)
    chunks, pieces, tokens, width = rows.shape

    def keep(c):
        return pltpu.make_async_copy(own_ref.at[pl.ds(c * tokens, tokens)], rows.at[c, 0], local_sems.at[0, c])

    def save_rows(c):
        return pltpu.make_async_copy(rows.at[c], rows_ref.at[c], local_sems.at[1, c])

    def grouped(c, d):
        origin, bit = group_route(d)
        source = own_ref.at[pl.ds(c * tokens, tokens)] if origin == 0 else rows.at[c, origin]
        return remote(count, source, rows.at[c, d], group_send.at[c, d], group_recv.at[c, d], masks[bit])

    def save(n, part):
        c, i = n // pieces, n % pieces
        p = (i % 2) * 2 + i // 2
        target = value_ref.at[p, c] if part == 0 else slope_ref.at[c, p]
        return pltpu.make_async_copy(staged.at[n % 2, part], target, save_sems.at[n % 2, part])

    load_block(stays, whole_ref, other_ref, weight, weight_sem.at[0], True)
    for c in range(chunks):
        keep(c).start()
    meet(count, masks + (count // 2,))
    for c in range(chunks):
        grouped(c, 1).start()
    for c in range(chunks):
        grouped(c, 2).start()
    when(stays, lambda: pass_block(count, block_ref, moved_ref, block_sems).start())
    load_block(stays, whole_ref, other_ref, weight, weight_sem.at[0], False)

    @pl.loop(0, chunks)
    def _(c):
        keep(c).wait()

        @pl.loop(0, pieces)
        def _(i):
            p = (i % 2) * 2 + i // 2
            step = c * pieces + i

            @pl.when(i == 1)
            def _():
                grouped(c, 2).wait_recv()

            @pl.when(i == 2)
            def _():
                grouped(c, 1).wait_recv()
                grouped(c, 3).start()

            @pl.when(i == 3)
            def _():
                grouped(c, 3).wait_recv()
                save_rows(c).start()

            value, slope = gelu_pair(dot(rows[c, p], weight[...]) + bias_ref[...])

            @pl.when(step >= 2)
            def _():
                for part in range(2):
                    save(step - 2, part).wait()

            staged[step % 2, 0] = value.astype(BF16)
            staged[step % 2, 1] = slope.astype(BF16)
            for part in range(2):
                save(step, part).start()

    for c in range(chunks):
        save_rows(c).wait()
        for d in range(1, pieces):
            grouped(c, d).wait_send()
    for step in range(chunks * pieces - 2, chunks * pieces):
        for part in range(2):
            save(step, part).wait()
    when(stays, lambda: pass_block(count, block_ref, moved_ref, block_sems).wait_send())
    when(jnp.logical_not(stays), lambda: pass_block(count, block_ref, moved_ref, block_sems).wait_recv())


def call_hidden(own, whole, other, bias, block, chunks, count, masks):
    width, hidden = whole.shape
    tokens, pieces = own.shape[0] // chunks, 1 << len(masks)
    return pl.pallas_call(
        functools.partial(hidden_kernel, count, masks),
        in_specs=[FAR, FAR, FAR, VMEM, FAR],
        out_specs=[FAR] * 4,
        out_shape=[
            jax.ShapeDtypeStruct((chunks, pieces, tokens, width), BF16),
            jax.ShapeDtypeStruct((pieces, chunks, tokens, hidden), BF16),
            jax.ShapeDtypeStruct((chunks, pieces, tokens, hidden), BF16),
            jax.ShapeDtypeStruct(block.shape, BF16),
        ],
        scratch_shapes=[
            pltpu.VMEM((chunks, pieces, tokens, width), BF16),
            pltpu.VMEM((2, 2, tokens, hidden), BF16),
            pltpu.VMEM((width, hidden), BF16),
            pltpu.SemaphoreType.DMA((chunks, pieces)),
            pltpu.SemaphoreType.DMA((chunks, pieces)),
            pltpu.SemaphoreType.DMA((2, chunks)),
            pltpu.SemaphoreType.DMA((2, 2)),
            pltpu.SemaphoreType.DMA((1,)),
            pltpu.SemaphoreType.DMA((2,)),
        ],
        compiler_params=pltpu.CompilerParams(
            collective_id=4, has_side_effects=True, vmem_limit_bytes=44 * MIB
        ),
        cost_estimate=pl.CostEstimate(
            flops=2 * chunks * pieces * tokens * width * hidden, bytes_accessed=100 * MIB, transcendentals=0
        ),
        name="hidden_forward",
    )(own, whole, other, bias, block)


def group_kernel(count, masks, backward, *refs):
    if backward:
        grad_ref, slope_ref, *blocks, part_ref, other_ref, sum_ref, out_ref, bias_ref, staged, contract = refs[:13]
        sources = (grad_ref, slope_ref)
        targets = (contract, refs[13])
        scratch = refs[13:]
    else:
        value_ref, *blocks, residual_ref, bias_ref, part_ref, other_ref, sum_ref = refs[:8]
        sources = (value_ref,)
        targets = (refs[8],)
        scratch = refs[8:]
    weight, loaded, partial, from_core, over, from_side = scratch[:6]
    core_send, core_recv, side_send, side_recv, cargo_sems, load_sems, save_sems, weight_sems = scratch[6:]
    chunks, tokens, _ = over.shape
    steps = 4 * chunks
    high = count // 2
    stays = block_stays(count)

    def place(step):
        return lax.rem(step, 2 * chunks) // 2, 3 - step // (2 * chunks) - 2 * lax.rem(step, 2)

    def load(step, part):
        c, p = place(step)
        slot = lax.rem(step, 2)
        source = sources[part].at[p, c] if part == 0 else sources[part].at[c, p]
        return pltpu.make_async_copy(source, loaded.at[slot, part], load_sems.at[slot, part])

    def save(step):
        c, p = place(step)
        slot = lax.rem(step, 2)
        return pltpu.make_async_copy(staged.at[slot], out_ref.at[c, p], save_sems.at[slot])

    def to_core(c, p):
        return remote(
            count, partial.at[c, p], from_core.at[c, p - 2], core_send.at[c, p - 2], core_recv.at[c, p - 2], masks[1]
        )

    def to_side(c):
        return remote(count, over.at[c], from_side.at[c], side_send.at[c], side_recv.at[c], masks[0])

    def put_sum(value):
        bias_ref[...] = value

    def cargo():
        return pass_block(count, part_ref, other_ref, cargo_sems)

    def load_blocks(start):
        for n, target in enumerate(targets):
            load_block(stays, blocks[2 * n], blocks[2 * n + 1], target, weight_sems.at[n], start)

    load_blocks(True)
    for part in range(len(sources)):
        load(0, part).start()
    meet(count, masks + (high,))
    when(jnp.logical_not(stays), lambda: cargo().start())
    load_blocks(False)

    @pl.loop(0, steps)
    def _(step):
        c, p = place(step)
        slot = lax.rem(step, 2)
        for part in range(len(sources)):
            load(step, part).wait()

        @pl.when(step < steps - 1)
        def _():
            for part in range(len(sources)):
                load(step + 1, part).start()

        @pl.when((slot == 0) & (step >= 2) & (step <= 2 * chunks))
        def _():
            before = step // 2 - 1
            to_core(before, 3).wait_recv()
            over[before] = (partial[before, 1].astype(F32) + from_core[before, 1].astype(F32)).astype(BF16)
            to_side(before).start()

        if backward:
            hidden = dot(loaded[slot, 0], contract[...]) * loaded[slot, 1].astype(F32)
            hidden = hidden.astype(BF16)

            @pl.when(step >= 2)
            def _():
                save(step - 2).wait()

            staged[slot] = hidden
            save(step).start()
            column_sum = jnp.sum(hidden.astype(F32), 0, keepdims=True)
            when(step == 0, lambda: put_sum(column_sum))
            when(step > 0, lambda: put_sum(bias_ref[...] + column_sum))
        else:
            hidden = loaded[slot, 0]
        partial[c, p] = dot(hidden, weight[...], NT).astype(BF16)

        @pl.when(p >= 2)
        def _():
            to_core(c, p).start()

    for c in range(chunks):
        to_core(c, 2).wait_recv()
        to_side(c).wait_recv()
        total = partial[c, 0].astype(F32) + from_core[c, 0].astype(F32) + from_side[c].astype(F32)
        mine = slice(c * tokens, (c + 1) * tokens)
        if backward:
            sum_ref[mine, :] = total
        else:
            sum_ref[mine, :] = (residual_ref[mine, :] + total + bias_ref[...]).astype(BF16)
        to_core(c, 2).wait_send()
        to_core(c, 3).wait_send()
        to_side(c).wait_send()
    if backward:
        for step in range(steps - 2, steps):
            save(step).wait()

    when(stays, lambda: cargo().wait_recv())
    when(jnp.logical_not(stays), lambda: cargo().wait_send())


def call_group(count, masks, backward, tiles, blocks, rest, part):
    pieces, chunks, tokens, width = tiles[0].shape
    outs = [
        jax.ShapeDtypeStruct(part.shape, BF16),
        jax.ShapeDtypeStruct((chunks * tokens, width), F32 if backward else BF16),
    ]
    scratch = [
        pltpu.VMEM((width, width), BF16),
        pltpu.VMEM((2, len(tiles), tokens, width), BF16),
        pltpu.VMEM((chunks, pieces, tokens, width), BF16),
        pltpu.VMEM((chunks, 2, tokens, width), BF16),
        pltpu.VMEM((chunks, tokens, width), BF16),
        pltpu.VMEM((chunks, tokens, width), BF16),
        pltpu.SemaphoreType.DMA((chunks, 2)),
        pltpu.SemaphoreType.DMA((chunks, 2)),
        pltpu.SemaphoreType.DMA((chunks,)),
        pltpu.SemaphoreType.DMA((chunks,)),
        pltpu.SemaphoreType.DMA((2,)),
        pltpu.SemaphoreType.DMA((2, len(tiles))),
        pltpu.SemaphoreType.DMA((2,)),
        pltpu.SemaphoreType.DMA((2,)),
    ]
    if backward:
        outs.append(jax.ShapeDtypeStruct((chunks, pieces, tokens, width), BF16))
        outs.append(jax.ShapeDtypeStruct((1, width), F32))
        scratch = [pltpu.VMEM((2, tokens, width), BF16), pltpu.VMEM((width, width), BF16)] + scratch
    return pl.pallas_call(
        functools.partial(group_kernel, count, masks, backward),
        in_specs=[FAR] * (len(tiles) + len(blocks)) + [VMEM] * len(rest) + [FAR],
        out_specs=[FAR, VMEM] + ([FAR, VMEM] if backward else []),
        out_shape=outs,
        scratch_shapes=scratch,
        compiler_params=pltpu.CompilerParams(
            collective_id=5 if backward else 6, has_side_effects=True, vmem_limit_bytes=56 * MIB
        ),
        cost_estimate=pl.CostEstimate(
            flops=(4 if backward else 2) * chunks * pieces * tokens * width * width,
            bytes_accessed=160 * MIB,
            transcendentals=0,
        ),
        name="group_backward" if backward else "group_forward",
    )(*tiles, *blocks, *rest, part)


def statistics(values):
    centred = values - jnp.mean(values, -1, keepdims=True)
    spread = jnp.mean(centred * centred, -1, keepdims=True)
    inverse = lax.rsqrt(spread + epsilon)
    return centred * inverse, inverse


def norm_forward(values, gain, shift):
    return (statistics(values)[0] * gain + shift).astype(BF16)


def norm_backward(values, gain, grad):
    normal, inverse = statistics(values)
    scaled = grad * gain
    spread = jnp.mean(scaled * normal, -1, keepdims=True)
    result = inverse * (scaled - jnp.mean(scaled, -1, keepdims=True) - normal * spread)
    return result, jnp.sum(grad * normal, 0), jnp.sum(grad, 0)


def body(
    seq_count,
    tp_count,
    tokens,
    positions,
    ln1_gain,
    ln1_bias,
    query_key_value_weight,
    qv_bias,
    attention_output_weight,
    attention_output_bias,
    ln2_gain,
    ln2_bias,
    expand_weight,
    expand_bias,
    contract_weight,
    contract_bias,
    cotangent,
):
    devices = seq_count * tp_count
    both = ("seq", "tp")
    t = lax.axis_index("tp")
    core = lax.axis_index("seq") % 2
    core_bit = tp_count
    tp_bits = [1 << k for k in range(tp_count.bit_length() - 1)]
    high = tp_bits[-1]
    ff_bits = tp_bits[:-1] + [core_bit]
    chunks, rows, width = tokens.shape
    span = rows // 2
    group_heads = -(-HEADS // tp_count)
    group = group_heads * HEAD
    pairs = -(-group_heads // 2)
    padded = pairs * LANES
    hidden = expand_weight.shape[1]
    peers = t ^ jnp.arange(tp_count)

    def swap(value, mask):
        return lax.ppermute(value, both, [(i, i ^ mask) for i in range(devices)])

    def after(value, *earlier):
        return lax.optimization_barrier((value, *earlier))[0]

    def choose(pieces, index):
        result = pieces[0]
        for n in range(1, len(pieces)):
            result = jnp.where(index == n, pieces[n], result)
        return result

    def gather_ff(value):
        pieces = [value]
        for bit in ff_bits:
            pieces += [swap(piece, bit) for piece in pieces]
        return pieces

    def sum_ff(pieces):
        while len(pieces) > 1:
            half = len(pieces) // 2
            bit = ff_bits[half.bit_length() - 1]
            pieces = [
                piece + swap(other, bit) for piece, other in zip(pieces[:half], pieces[half:], strict=True)
            ]
        return pieces[0]

    def sum_all(value):
        for k in range(devices.bit_length() - 1):
            value = value + swap(value, 1 << k)
        return value

    columns = query_key_value_weight.shape[1]
    feature = lax.broadcasted_iota(jnp.int32, (1, padded), 1)

    def shard_columns(owner, holder):
        found = []
        for part in range(3):
            column = part * width + holder * group + feature - columns * owner
            valid = (feature < group) & (holder * group + feature < width)
            found.append(jnp.where(valid & (column >= 0) & (column < columns), column, -1))
        return found

    def to_block(packed):
        parts = []
        for part in range(3):
            chosen = jnp.zeros_like(packed[0])
            for r in range(tp_count):
                chosen = jnp.where(shard_columns(t ^ r, t)[part] >= 0, packed[r], chosen)
            parts.append(chosen.reshape(-1, pairs, 1, LANES))
        return jnp.concatenate(parts, 2).reshape(-1, 3 * padded)

    def from_block(value):
        value = value.reshape(-1, pairs, 3, LANES)
        packed = []
        for r in range(tp_count):
            chosen = jnp.zeros((value.shape[0], padded), value.dtype)
            for part in range(3):
                here = shard_columns(t ^ r, t)[part] >= 0
                chosen = jnp.where(here, value[:, :, part].reshape(-1, padded), chosen)
            packed.append(chosen)
        return packed

    shard_index = lax.broadcasted_iota(jnp.int32, (columns, 1), 0)
    pick = []
    for r in range(tp_count):
        first, second, third = shard_columns(t, t ^ r)
        pick.append((shard_index == jnp.maximum(jnp.maximum(first, second), third)).astype(BF16))
    pick = jnp.concatenate(pick, 1)
    packed = dot(query_key_value_weight, pick).astype(BF16)
    packed = [packed[:, r * padded : (r + 1) * padded] for r in range(tp_count)]
    packed = [packed[0]] + [swap(packed[r], r) for r in range(1, tp_count)]

    flat = tokens.reshape(-1, width)
    gain_one, shift_one = ln1_gain.astype(F32), ln1_bias.astype(F32)
    gain_two, shift_two = ln2_gain.astype(F32), ln2_bias.astype(F32)
    normal_own = norm_forward(flat.astype(F32), gain_one, shift_one)
    packed[-1] = after(packed[-1], normal_own)
    qkv_rows = to_block(packed)
    qkv_weight = lax.all_gather(qkv_rows, "seq", axis=0, tiled=True)

    def head_columns(vector):
        whole = jnp.pad(vector, (0, tp_count * group - width))
        mine = lax.dynamic_slice_in_dim(whole, t * group, group)
        return jnp.pad(mine, (0, padded - group)).reshape(pairs, LANES)

    query_bias, value_bias = head_columns(qv_bias[0]), head_columns(qv_bias[1])
    qkv_bias = jnp.stack([query_bias, jnp.zeros_like(query_bias), value_bias], 1).reshape(-1)

    place = positions.reshape(chunks, tp_count, 2, span)[:, :, 0, 0] // span
    place = jnp.take(place, peers, axis=1)
    turned = (place >= tp_count).astype(jnp.int32)
    pair = jnp.minimum(place, 2 * tp_count - 1 - place)
    holds = pair[:, None, :] == jnp.arange(tp_count)[None, :, None]
    holder = jnp.sum(jnp.where(holds, jnp.arange(tp_count), 0), 2)
    orders = jnp.concatenate([holder, jnp.sum(jnp.where(holds, turned[:, None, :], 0), 2)], 1).astype(jnp.int32)
    places = jnp.concatenate([pair, turned], 1).astype(jnp.int32)
    masks = tuple(ff_bits)
    members = 1 << len(masks)

    stays = core == t // high
    block = t % high + core * high
    send = [
        (s * tp_count + i, s * tp_count + (i ^ high))
        for s in range(seq_count)
        for i in range(tp_count)
        if s % 2 == i // high
    ]

    def gather_seq(shard):
        return lax.all_gather(shard, "seq", axis=0, tiled=True)

    def take_block(whole):
        return lax.ppermute(whole, both, send)

    def give_block(partial):
        return lax.ppermute(partial, both, [(b, a) for a, b in send])

    def keep_block(partial, other):
        return jnp.where(stays, partial.astype(F32) + other, 0.0).astype(BF16)

    def sum_seq(partial):
        return after(lax.psum_scatter(partial, "seq", scatter_dimension=0, tiled=True))

    shards = [attention_output_weight] + [swap(attention_output_weight, r) for r in range(1, tp_count)]
    out_row = jnp.concatenate([choose(shards, t ^ a) for a in range(tp_count)], 1)
    normal_one = gather_rows(after(normal_own, out_row, qkv_rows), chunks, tp_count)
    expand_whole = gather_seq(expand_weight)
    contract_whole = gather_seq(after(contract_weight.T, normal_one))
    hidden_bias = lax.dynamic_slice_in_dim(expand_bias, block * hidden, hidden).astype(F32)

    out_weight = gather_seq(after(out_row, normal_one))

    qkv, heads_out, lse, output_rows, expand_other = call_forward(
        orders,
        places,
        normal_one,
        qkv_weight,
        qkv_bias.astype(F32).reshape(1, -1),
        cotangent.reshape(-1, width),
        expand_whole,
        tp_count,
        group_heads,
        masks,
    )
    pieces = [heads_out[r, :, :group] for r in range(tp_count)]
    mixed = jnp.concatenate([choose(pieces, t ^ a) for a in range(tp_count)], 1)[:, :width]
    residual = flat.astype(F32) + dot(mixed, out_weight) + attention_output_bias
    normal = norm_forward(residual, gain_two, shift_two)

    def second_norm_back(norm_grad):
        from_norm, gain_two_grad, shift_two_grad = norm_backward(residual, gain_two, norm_grad)
        resid_grad = cotangent.reshape(-1, width).astype(F32) + from_norm
        branch = resid_grad.astype(BF16)
        head_grad = dot(branch, out_weight, NT).astype(BF16)
        head_grad = jnp.pad(head_grad, ((0, 0), (0, tp_count * group - width)))
        pieces = [head_grad[:, a * group : (a + 1) * group] for a in range(tp_count)]
        pieces = [jnp.pad(choose(pieces, t ^ r), ((0, 0), (0, padded - group))) for r in range(tp_count)]
        out_part = dot(mixed, branch, TN).astype(BF16)
        out_grad = sum_seq(out_part)
        return gain_two_grad, shift_two_grad, resid_grad, branch, jnp.stack(pieces), out_grad

    flat_rows = output_rows.reshape(-1, width)
    if tp_count == 4:
        normal_two, value, slope, contract_other = call_hidden(
            normal,
            expand_whole,
            expand_other,
            hidden_bias.reshape(1, -1),
            contract_whole,
            chunks,
            tp_count,
            masks,
        )
        value = value.reshape(-1, hidden)
        contract_grad = dot(flat_rows, value, TN).astype(BF16)
        other, norm_grad, hidden_grad, hidden_bias_grad = call_group(
            tp_count,
            masks,
            True,
            [output_rows, slope],
            [contract_whole, contract_other, expand_whole, expand_other],
            [],
            contract_grad,
        )
        contract_grad = keep_block(contract_grad, other)
        proj_weight_grad = sum_seq(contract_grad)
        normal_two, hidden_grad = normal_two.reshape(-1, width), hidden_grad.reshape(-1, hidden)
        expand_grad = dot(normal_two, after(hidden_grad, contract_grad), TN).astype(BF16)
        from_second = second_norm_back(norm_grad)

        def group_forward(expand_grad):
            return call_group(
                tp_count,
                masks,
                False,
                [value.reshape(members, chunks, rows, hidden)],
                [contract_whole, contract_other],
                [residual, contract_bias.astype(F32).reshape(1, -1)],
                expand_grad,
            )

    else:
        expand = jnp.where(stays, expand_whole, expand_other)
        contract = jnp.where(stays, contract_whole, take_block(contract_whole))
        normal_two = jnp.concatenate(gather_ff(normal), 0)
        value, slope = gelu_pair(dot(normal_two, expand) + hidden_bias)
        value = value.astype(BF16)
        contract_grad = dot(flat_rows, value, TN).astype(BF16)
        hidden_grad = (dot(flat_rows, contract) * slope).astype(BF16)
        partial = dot(hidden_grad, expand, NT).astype(BF16).reshape(members, -1, width)
        hidden_bias_grad = jnp.sum(hidden_grad, 0, dtype=F32)
        from_second = second_norm_back(sum_ff([partial[d] for d in range(members)]).astype(F32))
        proj_weight_grad = sum_seq(keep_block(contract_grad, give_block(contract_grad)))
        expand_grad = dot(normal_two, hidden_grad, TN).astype(BF16)

        def group_forward(expand_grad):
            members_value = value.reshape(members, -1, hidden)
            feed = [dot(members_value[d], contract, NT).astype(BF16) for d in range(members)]
            return give_block(expand_grad), (residual + sum_ff(feed) + contract_bias).astype(BF16)


    gain_two_grad, shift_two_grad, resid_grad, branch, head_grads, out_grad = from_second
    _, one_grad, qkv_grad, qkv_bias_grad = call_backward(
        orders,
        places,
        after(qkv, expand_grad),
        head_grads,
        lse,
        qkv_weight,
        normal_one,
        tp_count,
        group_heads,
    )
    qkv_grad = after(qkv_grad, proj_weight_grad, out_grad)
    out_grad = [out_grad[:, a * (width // tp_count) : (a + 1) * (width // tp_count)] for a in range(tp_count)]
    out_weight_grad = choose(out_grad, t).astype(F32)
    for r in range(1, tp_count):
        out_weight_grad = out_weight_grad + swap(choose(out_grad, t ^ r), r)


    summed = lax.psum_scatter(qkv_grad, "seq", scatter_dimension=0, tiled=True)
    other, layer_out = group_forward(after(expand_grad, qkv_grad))
    expand_grad = keep_block(expand_grad, after(other, summed))
    fc_weight_grad = sum_seq(expand_grad)

    packed = from_block(after(summed, expand_grad))
    one_grad = after(one_grad, packed[-1])
    packed = [packed[0]] + [swap(packed[r], r) for r in range(1, tp_count)]
    qkv_weight_grad = dot(jnp.concatenate(packed, 1), pick, NT)
    from_norm, gain_one_grad, shift_one_grad = norm_backward(flat.astype(F32), gain_one, one_grad)
    input_grad = (resid_grad + from_norm).astype(BF16).reshape(tokens.shape)
    qkv_bias_grad = qkv_bias_grad.reshape(pairs, 3, LANES)

    def whole_bias(part):
        mine = qkv_bias_grad[:, part].reshape(-1)[:group]
        whole = jnp.zeros((tp_count * group,), F32)
        return lax.dynamic_update_slice_in_dim(whole, mine, t * group, 0)[:width]

    hidden_whole = lax.dynamic_update_slice_in_dim(
        jnp.zeros(expand_bias.shape, F32), hidden_bias_grad.reshape(-1), block * hidden, 0
    )
    out_bias_part = jnp.sum(branch, 0, dtype=F32)
    proj_bias_part = jnp.sum(cotangent, axis=(0, 1), dtype=F32)
    vector = sum_all(
        jnp.concatenate(
            [
                gain_two_grad,
                shift_two_grad,
                out_bias_part,
                proj_bias_part,
                gain_one_grad,
                shift_one_grad,
                whole_bias(0),
                whole_bias(2),
                hidden_whole,
            ]
        )
    )
    def part(vector, index):
        return vector[index * width : (index + 1) * width]

    return (
        layer_out.reshape(tokens.shape),
        input_grad,
        part(vector, 4),
        part(vector, 5),
        qkv_weight_grad,
        vector[6 * width : 8 * width].reshape(2, width),
        out_weight_grad,
        part(vector, 2),
        part(vector, 0),
        part(vector, 1),
        fc_weight_grad.astype(F32),
        vector[8 * width :],
        proj_weight_grad.astype(F32).T,
        part(vector, 3),
    )


def solution(mesh):
    in_specs = (
        P("seq", "tp", None),
        P("seq", None),
        P(),
        P(),
        P("seq", "tp"),
        P(),
        P("seq", "tp"),
        P(),
        P(),
        P(),
        P("seq", "tp"),
        P(),
        P("tp", "seq"),
        P(),
        P("seq", "tp", None),
    )
    out_specs = (
        P("seq", "tp", None),
        P("seq", "tp", None),
        P(),
        P(),
        P("seq", "tp"),
        P(),
        P("seq", "tp"),
        P(),
        P(),
        P(),
        P("seq", "tp"),
        P(),
        P("tp", "seq"),
        P(),
    )
    placed = functools.partial(body, mesh.shape["seq"], mesh.shape["tp"])
    return jax.shard_map(placed, mesh=mesh, in_specs=in_specs, out_specs=out_specs, check_vma=False)
```

```python
import functools
import jax
import jax.numpy as jnp
from jax import lax
from jax.experimental import pallas as pl
from jax.experimental.pallas import tpu as pltpu
from jax.sharding import PartitionSpec as P

HEADS = 25
HEAD = 64
LANES = 128
TILE = 256
epsilon = 1e-05
F32 = jnp.float32
BF16 = jnp.bfloat16
NN = (((1,), (0,)), ((), ()))
NT = (((1,), (1,)), ((), ()))
TN = (((0,), (0,)), ((), ()))
MIB = 2**20
VMEM = pl.BlockSpec(memory_space=pltpu.VMEM)
SMEM = pl.BlockSpec(memory_space=pltpu.SMEM)
FAR = pl.BlockSpec(memory_space=pl.ANY)


def dot(left, right, dims=NN):
    return lax.dot_general(left, right, dims, preferred_element_type=F32)


def peer_id(count, mask):
    if mask < count:
        return {"tp": lax.axis_index("tp") ^ mask}
    if mask == count:
        return {"seq": lax.axis_index("seq") ^ 1}
    return {"seq": lax.axis_index("seq") ^ 1, "tp": lax.axis_index("tp") ^ (mask - count)}


def meet(count, masks):
    barrier = pltpu.get_barrier_semaphore()
    for mask in masks:
        pl.semaphore_signal(barrier, inc=1, device_id=peer_id(count, mask), device_id_type=pl.DeviceIdType.MESH)
    pl.semaphore_wait(barrier, len(masks))


def remote(count, source, target, send, recv, mask):
    return pltpu.make_async_remote_copy(
        src_ref=source,
        dst_ref=target,
        send_sem=send,
        recv_sem=recv,
        device_id=peer_id(count, mask),
        device_id_type=pl.DeviceIdType.MESH,
    )


def block_stays(count):
    return lax.rem(lax.axis_index("seq"), 2) == lax.axis_index("tp") // (count // 2)


def pass_block(count, source, target, sems):
    return remote(count, source, target, sems.at[0], sems.at[1], count // 2)


def when(condition, action):
    pl.when(condition)(action)


def gather_kernel(count, tokens, own_ref, rows_ref, send_sems, recv_sems, local_sems):
    chunks = rows_ref.shape[0]
    span = tokens // 2
    direct_peers = (1, 2) if count == 4 else tuple(range(1, count))
    meet(count, direct_peers)

    def own(c):
        return pltpu.make_async_copy(
            own_ref.at[pl.ds(c * tokens, tokens)], rows_ref.at[c, pl.ds(0, tokens)], local_sems.at[c]
        )

    def direct(c, r):
        return remote(
            count,
            own_ref.at[pl.ds(c * tokens, tokens)],
            rows_ref.at[c, pl.ds(r * tokens, tokens)],
            send_sems.at[c, r],
            recv_sems.at[c, r],
            r,
        )

    def passed(c, half):
        start = (tokens, 2 * tokens + span)[half]
        return remote(
            count,
            rows_ref.at[c, pl.ds(start, span)],
            rows_ref.at[c, pl.ds(3 * tokens + half * span, span)],
            send_sems.at[c, 3 * half],
            recv_sems.at[c, 3 * half],
            2 - half,
        )

    for c in range(chunks):
        own(c).start()
        for r in direct_peers:
            direct(c, r).start()
    for c in range(chunks):
        for r in direct_peers:
            direct(c, r).wait_recv()
        if count == 4:
            passed(c, 0).start()
            passed(c, 1).start()
    for c in range(chunks):
        own(c).wait()
        for r in direct_peers:
            direct(c, r).wait_send()
        if count == 4:
            passed(c, 0).wait()
            passed(c, 1).wait()


def gather_rows(own, chunks, count):
    tokens = own.shape[0] // chunks
    return pl.pallas_call(
        functools.partial(gather_kernel, count, tokens),
        in_specs=[FAR],
        out_specs=FAR,
        out_shape=jax.ShapeDtypeStruct((chunks, tokens * count, own.shape[1]), BF16),
        scratch_shapes=[pltpu.SemaphoreType.DMA((chunks, count))] * 2 + [pltpu.SemaphoreType.DMA((chunks,))],
        compiler_params=pltpu.CompilerParams(collective_id=1, has_side_effects=True),
        cost_estimate=pl.CostEstimate(flops=0, bytes_accessed=120 * MIB, transcendentals=0),
        name="gather_rows",
    )(own)


def pick_one(index, options):
    result = options(0)
    for n in range(1, index[1]):
        result = lax.select(index[0] == n, options(n), result)
    return result


def to_places(count, span, holder, turned, source, target):
    for p in range(count):
        piece = pick_one((holder(p), count), source)
        first, second = piece[:span], piece[span:]
        swap = turned(p) == 1
        high = 2 * count - 1 - p
        target[p * span : (p + 1) * span, :] = lax.select(swap, second, first)
        target[high * span : (high + 1) * span, :] = lax.select(swap, first, second)


def from_places(count, span, pair, turned, source, store):
    for r in range(count):
        low = pick_one((pair(r), count), lambda p: source[p * span : (p + 1) * span, :])
        high = pick_one(
            (pair(r), count),
            lambda p: source[(2 * count - 1 - p) * span : (2 * count - p) * span, :],
        )
        swap = turned(r) == 1
        store(r, 0, lax.select(swap, high, low))
        store(r, 1, lax.select(swap, low, high))


def group_route(d):
    bit = d.bit_length() - 1
    return d - (1 << bit), bit


def forward_kernel(
    count,
    span,
    odd,
    masks,
    order_ref,
    place_ref,
    rows_ref,
    weight_ref,
    bias_ref,
    grad_ref,
    block_ref,
    qkv_ref,
    mixed_ref,
    lse_ref,
    group_ref,
    other_ref,
    rows,
    projected,
    outgoing,
    queries,
    keys,
    values,
    mixed,
    out_send,
    out_recv,
    group_send,
    group_recv,
    local_sems,
    block_sems,
):
    stays = block_stays(count)
    chunks, length, _ = rows.shape
    pairs = weight_ref.shape[1] // (3 * LANES)
    tokens = 2 * span
    pieces = 1 << len(masks)

    def load_rows(c):
        return pltpu.make_async_copy(rows_ref.at[c], rows.at[c], local_sems.at[0, c])

    def save_qkv(c):
        return pltpu.make_async_copy(projected.at[c % 2], qkv_ref.at[c], local_sems.at[1, c])

    def keep(c):
        return pltpu.make_async_copy(
            outgoing.at[c, 0], mixed_ref.at[0, pl.ds(c * tokens, tokens)], local_sems.at[2, c]
        )

    def keep_grad(c):
        return pltpu.make_async_copy(
            grad_ref.at[pl.ds(c * tokens, tokens)], group_ref.at[0, c], local_sems.at[3, c]
        )

    def outward(c, r):
        return remote(
            count,
            outgoing.at[c, r],
            mixed_ref.at[r, pl.ds(c * tokens, tokens)],
            out_send.at[c, r],
            out_recv.at[c, r],
            r,
        )

    def grouped(c, d):
        origin, bit = group_route(d)
        source = grad_ref.at[pl.ds(c * tokens, tokens)] if origin == 0 else group_ref.at[origin, c]
        return remote(
            count, source, group_ref.at[d, c], group_send.at[c, d], group_recv.at[c, d], masks[bit]
        )

    for c in range(chunks):
        load_rows(c).start()
    meet(count, tuple(range(1, count)) + (count,))
    when(stays, lambda: pass_block(count, block_ref, other_ref, block_sems).start())
    for c in range(chunks):
        keep_grad(c).start()
        for d in range(1, pieces):
            if group_route(d)[0] == 0:
                grouped(c, d).start()

    @pl.loop(0, chunks)
    def _(c):
        load_rows(c).wait()

        @pl.when(c >= 2)
        def _():
            save_qkv(c - 2).wait()

        @pl.loop(0, pairs)
        def _(j):
            columns = pl.ds(pl.multiple_of(j * 3 * LANES, LANES), 3 * LANES)
            block = (dot(rows[c], weight_ref[:, columns]) + bias_ref[:, columns]).astype(BF16)
            projected[c % 2, :, columns] = block
            for part, target in enumerate((queries, keys, values)):
                to_places(
                    count,
                    span,
                    lambda p: order_ref[c, p],
                    lambda p: order_ref[c, count + p],
                    lambda r: block[r * tokens : (r + 1) * tokens, part * LANES : (part + 1) * LANES],
                    target,
                )

            def one_head(head):
                lane = lax.broadcasted_iota(jnp.int32, (TILE, LANES), 1)
                mine = (lane // HEAD) == head
                for first in range(0, length, TILE):
                    last = first + TILE
                    query = jnp.where(mine, queries[first:last, :] * BF16(HEAD**-0.5), BF16(0))
                    scores = dot(query, keys[0:last, :], NT)
                    row = lax.broadcasted_iota(jnp.int32, (TILE, TILE), 0)
                    column = lax.broadcasted_iota(jnp.int32, (TILE, TILE), 1)
                    corner = jnp.where(column <= row, scores[:, first:last], -1e30)
                    scores = corner if first == 0 else jnp.concatenate([scores[:, :first], corner], axis=1)
                    row_max = jnp.max(scores, 1, keepdims=True)
                    weights = jnp.exp(scores - row_max)
                    total = jnp.sum(weights, 1, keepdims=True)
                    part = dot(weights.astype(BF16), values[0:last, :]) / total
                    lse_ref[c, j, head, first:last] = (row_max + jnp.log(total))[:, 0]
                    if head == 0:
                        mixed[first:last, :] = jnp.where(mine, part, 0.0).astype(BF16)
                    else:
                        mixed[first:last, :] = jnp.where(mine, part.astype(BF16), mixed[first:last, :])

            one_head(0)
            if odd:
                pl.when(j < pairs - 1)(lambda: one_head(1))
            else:
                one_head(1)
            lanes = pl.ds(pl.multiple_of(j * LANES, LANES), LANES)

            def put(r, half, value):
                outgoing[c, r, half * span : (half + 1) * span, lanes] = value

            from_places(
                count, span, lambda r: place_ref[c, r], lambda r: place_ref[c, count + r], mixed, put
            )

        save_qkv(c).start()
        keep(c).start()
        for r in range(1, count):
            outward(c, r).start()

    for c in range(chunks):
        keep_grad(c).wait()
    for d in range(1, pieces):
        origin = group_route(d)[0]
        for c in range(chunks):
            if origin != 0:
                grouped(c, d).start()
        for c in range(chunks):
            grouped(c, d).wait()
    for c in range(chunks):
        keep(c).wait()
        for r in range(1, count):
            outward(c, r).wait()
    for c in range(max(chunks - 2, 0), chunks):
        save_qkv(c).wait()
    when(stays, lambda: pass_block(count, block_ref, other_ref, block_sems).wait_send())
    when(jnp.logical_not(stays), lambda: pass_block(count, block_ref, other_ref, block_sems).wait_recv())


def call_forward(order, place, rows, weight, bias, grad, block, count, heads, masks):
    chunks, length, width = rows.shape
    columns = weight.shape[1]
    pairs, tokens, pieces = columns // (3 * LANES), length // count, 1 << len(masks)
    return pl.pallas_call(
        functools.partial(forward_kernel, count, tokens // 2, heads % 2 == 1, masks),
        in_specs=[SMEM, SMEM, FAR, VMEM, VMEM, FAR, FAR],
        out_specs=[FAR, FAR, VMEM, FAR, FAR],
        out_shape=[
            jax.ShapeDtypeStruct((chunks, length, columns), BF16),
            jax.ShapeDtypeStruct((count, chunks * tokens, pairs * LANES), BF16),
            jax.ShapeDtypeStruct((chunks, pairs, 2, length), F32),
            jax.ShapeDtypeStruct((pieces, chunks, tokens, width), BF16),
            jax.ShapeDtypeStruct(block.shape, BF16),
        ],
        scratch_shapes=[
            pltpu.VMEM((chunks, length, width), BF16),
            pltpu.VMEM((2, length, columns), BF16),
            pltpu.VMEM((chunks, count, tokens, pairs * LANES), BF16),
        ]
        + [pltpu.VMEM((length, LANES), BF16)] * 4
        + [pltpu.SemaphoreType.DMA((chunks, count))] * 2
        + [pltpu.SemaphoreType.DMA((chunks, pieces))] * 2
        + [pltpu.SemaphoreType.DMA((4, chunks)), pltpu.SemaphoreType.DMA((2,))],
        compiler_params=pltpu.CompilerParams(
            collective_id=2, has_side_effects=True, vmem_limit_bytes=52 * MIB
        ),
        cost_estimate=pl.CostEstimate(
            flops=chunks * (2 * length * width * columns + heads * length * length * 5 * 256),
            bytes_accessed=80 * MIB,
            transcendentals=chunks * heads * length * length,
        ),
        name="attend_forward",
    )(order, place, rows, weight, bias, grad, block)


def backward_kernel(
    count,
    span,
    odd,
    order_ref,
    place_ref,
    qkv_ref,
    grad_ref,
    lse_ref,
    weight_ref,
    rows_ref,
    out_ref,
    sum_ref,
    product_ref,
    bias_ref,
    arrived,
    block,
    result,
    queries,
    keys,
    values,
    grads,
    query_grad,
    key_sum,
    value_sum,
    first_out,
    first_in,
    side,
    second_out,
    second_in,
    head_send,
    head_recv,
    first_send,
    first_recv,
    second_send,
    second_recv,
    local_sems,
    left,
    right,
    product,
    rounded_product,
    tile_sems,
    product_sem,
):
    chunks, length = out_ref.shape[:2]
    pairs = weight_ref.shape[1] // (3 * LANES)
    tokens = 2 * span

    def load_qkv(c):
        return pltpu.make_async_copy(qkv_ref.at[c], block.at[c % 2], local_sems.at[0, c])

    def load_own(c):
        return pltpu.make_async_copy(
            grad_ref.at[0, pl.ds(c * tokens, tokens)], arrived.at[c, 0], local_sems.at[1, c]
        )

    def save(c):
        return pltpu.make_async_copy(result, out_ref.at[c], local_sems.at[2, c])

    def inward(c, r):
        return remote(
            count,
            grad_ref.at[r, pl.ds(c * tokens, tokens)],
            arrived.at[c, r],
            head_send.at[c, r],
            head_recv.at[c, r],
            r,
        )

    def first(c, half):
        return remote(
            count,
            first_out.at[c, half],
            first_in.at[c, half],
            first_send.at[c, half],
            first_recv.at[c, half],
            2 - half,
        )

    def second(c, r):
        return remote(
            count,
            second_out.at[c, r - 1],
            second_in.at[c, r - 1],
            second_send.at[c, r - 1],
            second_recv.at[c, r - 1],
            r,
        )

    direct_peers = (1, 2) if count == 4 else tuple(range(1, count))

    def send_sums(c):
        if count == 4:
            first(c, 0).wait_recv()
            first(c, 1).wait_recv()
            second_out[c, 0, 0:span] = (side[0, 0:span] + first_in[c, 0].astype(F32)).astype(BF16)
            second_out[c, 0, span:tokens] = side[0, span:tokens].astype(BF16)
            second_out[c, 1, 0:span] = side[1, 0:span].astype(BF16)
            second_out[c, 1, span:tokens] = (side[1, span:tokens] + first_in[c, 1].astype(F32)).astype(
                BF16
            )
        for r in direct_peers:
            second(c, r).start()

    load_qkv(0).start()
    meet(count, tuple(range(1, count)))
    for c in range(chunks):
        load_own(c).start()
        for r in range(1, count):
            inward(c, r).start()

    @pl.loop(0, chunks)
    def _(c):
        load_qkv(c).wait()

        @pl.when(c < chunks - 1)
        def _():
            load_qkv(c + 1).start()

        load_own(c).wait()
        for r in range(1, count):
            inward(c, r).wait_recv()

        @pl.when(c >= 1)
        def _():
            save(c - 1).wait()

        @pl.loop(0, pairs)
        def _(j):
            @pl.when((j == pairs - 1) & (c >= 1))
            def _():
                send_sums(c - 1)

            def place(source, target):
                to_places(
                    count,
                    span,
                    lambda p: order_ref[c, p],
                    lambda p: order_ref[c, count + p],
                    source,
                    target,
                )

            for part, target in enumerate((queries, keys, values)):
                lanes = pl.ds(pl.multiple_of(j * 3 * LANES + part * LANES, LANES), LANES)
                place(lambda r: block[c % 2, r * tokens : (r + 1) * tokens, lanes], target)
            lanes = pl.ds(pl.multiple_of(j * LANES, LANES), LANES)
            place(lambda r: arrived[c, r, :, lanes], grads)

            def one_head(head):
                lane = lax.broadcasted_iota(jnp.int32, (TILE, LANES), 1)
                mine = (lane // HEAD) == head
                for first_row in reversed(range(0, length, TILE)):
                    last = first_row + TILE
                    query = jnp.where(mine, queries[first_row:last, :] * BF16(HEAD**-0.5), BF16(0))
                    grad = jnp.where(mine, grads[first_row:last, :], BF16(0))
                    scores = dot(query, keys[0:last, :], NT)
                    row = lax.broadcasted_iota(jnp.int32, (TILE, TILE), 0)
                    column = lax.broadcasted_iota(jnp.int32, (TILE, TILE), 1)
                    corner = jnp.where(column <= row, scores[:, first_row:last], -1e30)
                    scores = (
                        corner if first_row == 0 else jnp.concatenate([scores[:, :first_row], corner], axis=1)
                    )
                    weights = jnp.exp(scores - lse_ref[c, j, head, first_row:last][:, None])
                    prob_grad = dot(grad, values[0:last, :], NT)
                    product = weights * prob_grad
                    inner = jnp.sum(product, 1, keepdims=True)
                    score_grad = (product - weights * inner).astype(BF16)
                    rounded = weights.astype(BF16)
                    part = (dot(score_grad, keys[0:last, :]) * HEAD**-0.5).astype(BF16)
                    key_part = dot(query, score_grad, TN)
                    value_part = dot(grad, rounded, TN)
                    if head == 0 and last == length:
                        key_sum[...] = key_part
                        value_sum[...] = value_part
                    else:
                        key_sum[:, 0:last] += key_part
                        value_sum[:, 0:last] += value_part
                    if head == 0:
                        query_grad[first_row:last, :] = jnp.where(mine, part, BF16(0))
                    else:
                        query_grad[first_row:last, :] = jnp.where(mine, part, query_grad[first_row:last, :])

            one_head(0)
            if odd:
                pl.when(j < pairs - 1)(lambda: one_head(1))
            else:
                one_head(1)
            keys[...] = key_sum[...].T.astype(BF16)
            values[...] = value_sum[...].T.astype(BF16)
            for part, source in enumerate((query_grad, keys, values)):
                lanes = pl.ds(pl.multiple_of(j * 3 * LANES + part * LANES, LANES), LANES)

                def put(r, half, value):
                    start = r * tokens + half * span
                    result[start : start + span, lanes] = value

                from_places(
                    count, span, lambda r: place_ref[c, r], lambda r: place_ref[c, count + r], source, put
                )

        save(c).start()

        def share(first_piece, last_piece):
            return dot(result[first_piece * tokens : last_piece * tokens, :], weight_ref[...], NT)

        if count == 4:
            far = share(2, 4)
            first_out[c, 0] = far[tokens : tokens + span].astype(BF16)
            first_out[c, 1] = far[tokens + span :].astype(BF16)
            first(c, 0).start()
            first(c, 1).start()
            side[1] = far[:tokens]
            near = share(0, 2)
            side[0] = near[tokens:]
        else:
            for r in direct_peers:
                second_out[c, r - 1] = share(r, r + 1).astype(BF16)
            near = share(0, 1)
        sum_ref[pl.ds(pl.multiple_of(c * tokens, tokens), tokens), :] = near[:tokens]

    save(chunks - 1).wait()
    depth, third = left.shape[1], product.shape[1]
    tiles = length // depth
    rounds = chunks * tiles

    def load(n, side_index):
        c, k = lax.rem(n, rounds) // tiles, lax.rem(n, tiles)
        span_rows = pl.ds(pl.multiple_of(k * depth, depth), depth)
        slot = lax.rem(n, 2)
        if side_index == 0:
            source, target = rows_ref.at[c, span_rows], left.at[slot]
        else:
            lanes = pl.ds(pl.multiple_of(n // rounds * third, third), third)
            source, target = out_ref.at[c, span_rows, lanes], right.at[slot]
        return pltpu.make_async_copy(source, target, tile_sems.at[slot, side_index])

    def save_product(part):
        lanes = pl.ds(pl.multiple_of(part * third, third), third)
        return pltpu.make_async_copy(rounded_product, product_ref.at[:, lanes], product_sem.at[0])

    for side_index in range(2):
        load(0, side_index).start()

    @pl.loop(0, 3 * rounds)
    def _(n):
        slot = lax.rem(n, 2)
        part = n // rounds
        lanes = pl.ds(pl.multiple_of(part * third, third), third)
        for side_index in range(2):
            load(n, side_index).wait()

        @pl.when(n < 3 * rounds - 1)
        def _():
            for side_index in range(2):
                load(n + 1, side_index).start()

        @pl.when(n == rounds)
        def _():
            send_sums(chunks - 1)

        term = dot(left[slot], right[slot], TN)
        column_sum = jnp.sum(right[slot].astype(F32), 0, keepdims=True)

        @pl.when(lax.rem(n, rounds) == 0)
        def _():
            product[...] = term
            bias_ref[:, lanes] = column_sum

        @pl.when(lax.rem(n, rounds) != 0)
        def _():
            product[...] += term
            bias_ref[:, lanes] += column_sum

        @pl.when(lax.rem(n, rounds) == rounds - 1)
        def _():
            when(part >= 1, lambda: save_product(part - 1).wait())
            rounded_product[...] = product[...].astype(BF16)
            save_product(part).start()

    for c in range(chunks):
        total = sum_ref[c * tokens : (c + 1) * tokens, :]
        for r in direct_peers:
            second(c, r).wait_recv()
            total = total + second_in[c, r - 1].astype(F32)
        sum_ref[c * tokens : (c + 1) * tokens, :] = total
        for r in direct_peers:
            second(c, r).wait_send()
        if count == 4:
            first(c, 0).wait_send()
            first(c, 1).wait_send()
        for r in range(1, count):
            inward(c, r).wait_send()
    save_product(2).wait()


def call_backward(order, place, qkv, grads, lse, weight, rows, count, heads):
    chunks, length, columns = qkv.shape
    width = weight.shape[0]
    pairs, tokens = columns // (3 * LANES), length // count
    sides = 2 if count == 4 else count - 1
    return pl.pallas_call(
        functools.partial(backward_kernel, count, tokens // 2, heads % 2 == 1),
        in_specs=[SMEM, SMEM, FAR, FAR, VMEM, VMEM, FAR],
        out_specs=[FAR, VMEM, FAR, VMEM],
        out_shape=[
            jax.ShapeDtypeStruct((chunks, length, columns), BF16),
            jax.ShapeDtypeStruct((chunks * tokens, width), F32),
            jax.ShapeDtypeStruct((width, columns), BF16),
            jax.ShapeDtypeStruct((1, columns), F32),
        ],
        scratch_shapes=[
            pltpu.VMEM((chunks, count, tokens, pairs * LANES), BF16),
            pltpu.VMEM((2, length, columns), BF16),
            pltpu.VMEM((length, columns), BF16),
        ]
        + [pltpu.VMEM((length, LANES), BF16)] * 5
        + [pltpu.VMEM((LANES, length), F32)] * 2
        + [
            pltpu.VMEM((chunks, 2, tokens // 2, width), BF16),
            pltpu.VMEM((chunks, 2, tokens // 2, width), BF16),
            pltpu.VMEM((2, tokens, width), F32),
            pltpu.VMEM((chunks, sides, tokens, width), BF16),
            pltpu.VMEM((chunks, sides, tokens, width), BF16),
        ]
        + [pltpu.SemaphoreType.DMA((chunks, count))] * 2
        + [pltpu.SemaphoreType.DMA((chunks, 2))] * 2
        + [pltpu.SemaphoreType.DMA((chunks, sides))] * 2
        + [
            pltpu.SemaphoreType.DMA((3, chunks)),
            pltpu.VMEM((2, 2 * tokens, width), BF16),
            pltpu.VMEM((2, 2 * tokens, columns // 3), BF16),
            pltpu.VMEM((width, columns // 3), F32),
            pltpu.VMEM((width, columns // 3), BF16),
            pltpu.SemaphoreType.DMA((2, 2)),
            pltpu.SemaphoreType.DMA((1,)),
        ],
        compiler_params=pltpu.CompilerParams(
            collective_id=3, has_side_effects=True, vmem_limit_bytes=60 * MIB
        ),
        cost_estimate=pl.CostEstimate(
            flops=chunks * (2 * length * width * columns + heads * length * length * 8 * 256),
            bytes_accessed=80 * MIB,
            transcendentals=chunks * heads * length * length,
        ),
        name="attend_backward",
    )(order, place, qkv, grads, lse, weight, rows)


def gelu_pair(u):
    scale = 0.7978845608028654
    square = u * u
    inner = jnp.tanh(u * (scale + scale * 0.044715 * square))
    half = 0.5 + 0.5 * inner
    slope = half + u * (half * (1.0 - inner)) * (scale + scale * 0.134145 * square)
    return u * half, slope


def load_block(stays, whole_ref, other_ref, weight, sem, start):
    if start:
        when(stays, lambda: pltpu.make_async_copy(whole_ref, weight, sem).start())
        when(jnp.logical_not(stays), lambda: pltpu.make_async_copy(other_ref, weight, sem).start())
    else:
        pltpu.make_async_copy(whole_ref, weight, sem).wait()


def hidden_kernel(
    count, masks, own_ref, whole_ref, other_ref, bias_ref, block_ref, rows_ref, value_ref, slope_ref, moved_ref,
    rows, staged, weight, group_send, group_recv, local_sems, save_sems, weight_sem, block_sems,
):
    stays = block_stays(count)
    chunks, pieces, tokens, width = rows.shape

    def keep(c):
        return pltpu.make_async_copy(own_ref.at[pl.ds(c * tokens, tokens)], rows.at[c, 0], local_sems.at[0, c])

    def save_rows(c):
        return pltpu.make_async_copy(rows.at[c], rows_ref.at[c], local_sems.at[1, c])

    def grouped(c, d):
        origin, bit = group_route(d)
        source = own_ref.at[pl.ds(c * tokens, tokens)] if origin == 0 else rows.at[c, origin]
        return remote(count, source, rows.at[c, d], group_send.at[c, d], group_recv.at[c, d], masks[bit])

    def save(n, part):
        c, i = n // pieces, n % pieces
        p = (i % 2) * 2 + i // 2
        target = value_ref.at[p, c] if part == 0 else slope_ref.at[c, p]
        return pltpu.make_async_copy(staged.at[n % 2, part], target, save_sems.at[n % 2, part])

    load_block(stays, whole_ref, other_ref, weight, weight_sem.at[0], True)
    for c in range(chunks):
        keep(c).start()
    meet(count, masks + (count // 2,))
    for c in range(chunks):
        grouped(c, 1).start()
    for c in range(chunks):
        grouped(c, 2).start()
    when(stays, lambda: pass_block(count, block_ref, moved_ref, block_sems).start())
    load_block(stays, whole_ref, other_ref, weight, weight_sem.at[0], False)

    @pl.loop(0, chunks)
    def _(c):
        keep(c).wait()

        @pl.loop(0, pieces)
        def _(i):
            p = (i % 2) * 2 + i // 2
            step = c * pieces + i

            @pl.when(i == 1)
            def _():
                grouped(c, 2).wait_recv()

            @pl.when(i == 2)
            def _():
                grouped(c, 1).wait_recv()
                grouped(c, 3).start()

            @pl.when(i == 3)
            def _():
                grouped(c, 3).wait_recv()
                save_rows(c).start()

            value, slope = gelu_pair(dot(rows[c, p], weight[...]) + bias_ref[...])

            @pl.when(step >= 2)
            def _():
                for part in range(2):
                    save(step - 2, part).wait()

            staged[step % 2, 0] = value.astype(BF16)
            staged[step % 2, 1] = slope.astype(BF16)
            for part in range(2):
                save(step, part).start()

    for c in range(chunks):
        save_rows(c).wait()
        for d in range(1, pieces):
            grouped(c, d).wait_send()
    for step in range(chunks * pieces - 2, chunks * pieces):
        for part in range(2):
            save(step, part).wait()
    when(stays, lambda: pass_block(count, block_ref, moved_ref, block_sems).wait_send())
    when(jnp.logical_not(stays), lambda: pass_block(count, block_ref, moved_ref, block_sems).wait_recv())


def call_hidden(own, whole, other, bias, block, chunks, count, masks):
    width, hidden = whole.shape
    tokens, pieces = own.shape[0] // chunks, 1 << len(masks)
    return pl.pallas_call(
        functools.partial(hidden_kernel, count, masks),
        in_specs=[FAR, FAR, FAR, VMEM, FAR],
        out_specs=[FAR] * 4,
        out_shape=[
            jax.ShapeDtypeStruct((chunks, pieces, tokens, width), BF16),
            jax.ShapeDtypeStruct((pieces, chunks, tokens, hidden), BF16),
            jax.ShapeDtypeStruct((chunks, pieces, tokens, hidden), BF16),
            jax.ShapeDtypeStruct(block.shape, BF16),
        ],
        scratch_shapes=[
            pltpu.VMEM((chunks, pieces, tokens, width), BF16),
            pltpu.VMEM((2, 2, tokens, hidden), BF16),
            pltpu.VMEM((width, hidden), BF16),
            pltpu.SemaphoreType.DMA((chunks, pieces)),
            pltpu.SemaphoreType.DMA((chunks, pieces)),
            pltpu.SemaphoreType.DMA((2, chunks)),
            pltpu.SemaphoreType.DMA((2, 2)),
            pltpu.SemaphoreType.DMA((1,)),
            pltpu.SemaphoreType.DMA((2,)),
        ],
        compiler_params=pltpu.CompilerParams(
            collective_id=4, has_side_effects=True, vmem_limit_bytes=44 * MIB
        ),
        cost_estimate=pl.CostEstimate(
            flops=2 * chunks * pieces * tokens * width * hidden, bytes_accessed=100 * MIB, transcendentals=0
        ),
        name="hidden_forward",
    )(own, whole, other, bias, block)


def group_kernel(count, masks, backward, *refs):
    if backward:
        grad_ref, slope_ref, *blocks, part_ref, other_ref, sum_ref, out_ref, bias_ref, staged, contract = refs[:13]
        sources = (grad_ref, slope_ref)
        targets = (contract, refs[13])
        scratch = refs[13:]
    else:
        value_ref, *blocks, residual_ref, bias_ref, part_ref, other_ref, sum_ref = refs[:8]
        sources = (value_ref,)
        targets = (refs[8],)
        scratch = refs[8:]
    weight, loaded, partial, from_core, over, from_side = scratch[:6]
    core_send, core_recv, side_send, side_recv, cargo_sems, load_sems, save_sems, weight_sems, held = scratch[6:]
    chunks, tokens, _ = over.shape
    steps = 4 * chunks
    high = count // 2
    stays = block_stays(count)

    def place(step):
        return lax.rem(step, 2 * chunks) // 2, 3 - step // (2 * chunks) - 2 * lax.rem(step, 2)

    def load(step, part):
        c, p = place(step)
        slot = lax.rem(step, 2)
        source = sources[part].at[p, c] if part == 0 else sources[part].at[c, p]
        return pltpu.make_async_copy(source, loaded.at[slot, part], load_sems.at[slot, part])

    def save(step):
        c, p = place(step)
        slot = lax.rem(step, 2)
        return pltpu.make_async_copy(staged.at[slot], out_ref.at[c, p], save_sems.at[slot])

    def to_core(c, p):
        return remote(
            count, partial.at[c, p], from_core.at[c, p - 2], core_send.at[c, p - 2], core_recv.at[c, p - 2], masks[1]
        )

    def to_side(c):
        return remote(count, over.at[c], from_side.at[c], side_send.at[c], side_recv.at[c], masks[0])

    def put_sum(value):
        bias_ref[...] = value

    def cargo():
        return remote(count, part_ref, other_ref, cargo_sems.at[0], cargo_sems.at[1], count + high)

    def take_part():
        return pltpu.make_async_copy(part_ref, held, cargo_sems.at[0])

    def keep_part():
        return pltpu.make_async_copy(held, other_ref, cargo_sems.at[1])

    def load_blocks(start):
        for n, target in enumerate(targets):
            load_block(stays, blocks[2 * n], blocks[2 * n + 1], target, weight_sems.at[n], start)

    load_blocks(True)
    for part in range(len(sources)):
        load(0, part).start()
    meet(count, masks + (count + high,))
    when(stays, lambda: take_part().start())
    when(jnp.logical_not(stays), lambda: cargo().start())
    load_blocks(False)
    when(stays, lambda: take_part().wait())
    when(stays, lambda: keep_part().start())

    @pl.loop(0, steps)
    def _(step):
        c, p = place(step)
        slot = lax.rem(step, 2)
        for part in range(len(sources)):
            load(step, part).wait()

        @pl.when(step < steps - 1)
        def _():
            for part in range(len(sources)):
                load(step + 1, part).start()

        @pl.when((slot == 0) & (step >= 2) & (step <= 2 * chunks))
        def _():
            before = step // 2 - 1
            to_core(before, 3).wait_recv()
            over[before] = (partial[before, 1].astype(F32) + from_core[before, 1].astype(F32)).astype(BF16)
            to_side(before).start()

        if backward:
            hidden = dot(loaded[slot, 0], contract[...]) * loaded[slot, 1].astype(F32)
            hidden = hidden.astype(BF16)

            @pl.when(step >= 2)
            def _():
                save(step - 2).wait()

            staged[slot] = hidden
            save(step).start()
            column_sum = jnp.sum(hidden.astype(F32), 0, keepdims=True)
            when(step == 0, lambda: put_sum(column_sum))
            when(step > 0, lambda: put_sum(bias_ref[...] + column_sum))
        else:
            hidden = loaded[slot, 0]
        partial[c, p] = dot(hidden, weight[...], NT).astype(BF16)

        @pl.when(p >= 2)
        def _():
            to_core(c, p).start()

    for c in range(chunks):
        to_core(c, 2).wait_recv()
        to_side(c).wait_recv()
        total = partial[c, 0].astype(F32) + from_core[c, 0].astype(F32) + from_side[c].astype(F32)
        mine = slice(c * tokens, (c + 1) * tokens)
        if backward:
            sum_ref[mine, :] = total
        else:
            sum_ref[mine, :] = (residual_ref[mine, :] + total + bias_ref[...]).astype(BF16)
        to_core(c, 2).wait_send()
        to_core(c, 3).wait_send()
        to_side(c).wait_send()
    if backward:
        for step in range(steps - 2, steps):
            save(step).wait()

    when(stays, lambda: keep_part().wait())
    when(jnp.logical_not(stays), lambda: cargo().wait())


def call_group(count, masks, backward, tiles, blocks, rest, part):
    pieces, chunks, tokens, width = tiles[0].shape
    outs = [
        jax.ShapeDtypeStruct(part.shape, BF16),
        jax.ShapeDtypeStruct((chunks * tokens, width), F32 if backward else BF16),
    ]
    scratch = [
        pltpu.VMEM((width, width), BF16),
        pltpu.VMEM((2, len(tiles), tokens, width), BF16),
        pltpu.VMEM((chunks, pieces, tokens, width), BF16),
        pltpu.VMEM((chunks, 2, tokens, width), BF16),
        pltpu.VMEM((chunks, tokens, width), BF16),
        pltpu.VMEM((chunks, tokens, width), BF16),
        pltpu.SemaphoreType.DMA((chunks, 2)),
        pltpu.SemaphoreType.DMA((chunks, 2)),
        pltpu.SemaphoreType.DMA((chunks,)),
        pltpu.SemaphoreType.DMA((chunks,)),
        pltpu.SemaphoreType.DMA((2,)),
        pltpu.SemaphoreType.DMA((2, len(tiles))),
        pltpu.SemaphoreType.DMA((2,)),
        pltpu.SemaphoreType.DMA((2,)),
        pltpu.VMEM(part.shape, BF16),
    ]
    if backward:
        outs.append(jax.ShapeDtypeStruct((chunks, pieces, tokens, width), BF16))
        outs.append(jax.ShapeDtypeStruct((1, width), F32))
        scratch = [pltpu.VMEM((2, tokens, width), BF16), pltpu.VMEM((width, width), BF16)] + scratch
    return pl.pallas_call(
        functools.partial(group_kernel, count, masks, backward),
        in_specs=[FAR] * (len(tiles) + len(blocks)) + [VMEM] * len(rest) + [FAR],
        out_specs=[FAR, VMEM] + ([FAR, VMEM] if backward else []),
        out_shape=outs,
        scratch_shapes=scratch,
        compiler_params=pltpu.CompilerParams(
            collective_id=5 if backward else 6, has_side_effects=True, vmem_limit_bytes=56 * MIB
        ),
        cost_estimate=pl.CostEstimate(
            flops=(4 if backward else 2) * chunks * pieces * tokens * width * width,
            bytes_accessed=160 * MIB,
            transcendentals=0,
        ),
        name="group_backward" if backward else "group_forward",
    )(*tiles, *blocks, *rest, part)


def statistics(values):
    centred = values - jnp.mean(values, -1, keepdims=True)
    spread = jnp.mean(centred * centred, -1, keepdims=True)
    inverse = lax.rsqrt(spread + epsilon)
    return centred * inverse, inverse


def norm_forward(values, gain, shift):
    return (statistics(values)[0] * gain + shift).astype(BF16)


def norm_backward(values, gain, grad):
    normal, inverse = statistics(values)
    scaled = grad * gain
    spread = jnp.mean(scaled * normal, -1, keepdims=True)
    result = inverse * (scaled - jnp.mean(scaled, -1, keepdims=True) - normal * spread)
    return result, jnp.sum(grad * normal, 0), jnp.sum(grad, 0)


def body(
    seq_count,
    tp_count,
    tokens,
    positions,
    ln1_gain,
    ln1_bias,
    query_key_value_weight,
    qv_bias,
    attention_output_weight,
    attention_output_bias,
    ln2_gain,
    ln2_bias,
    expand_weight,
    expand_bias,
    contract_weight,
    contract_bias,
    cotangent,
):
    devices = seq_count * tp_count
    both = ("seq", "tp")
    t = lax.axis_index("tp")
    core = lax.axis_index("seq") % 2
    core_bit = tp_count
    tp_bits = [1 << k for k in range(tp_count.bit_length() - 1)]
    high = tp_bits[-1]
    ff_bits = tp_bits[:-1] + [core_bit]
    chunks, rows, width = tokens.shape
    span = rows // 2
    group_heads = -(-HEADS // tp_count)
    group = group_heads * HEAD
    pairs = -(-group_heads // 2)
    padded = pairs * LANES
    hidden = expand_weight.shape[1]
    peers = t ^ jnp.arange(tp_count)

    def swap(value, mask):
        return lax.ppermute(value, both, [(i, i ^ mask) for i in range(devices)])

    def after(value, *earlier):
        return lax.optimization_barrier((value, *earlier))[0]

    def choose(pieces, index):
        result = pieces[0]
        for n in range(1, len(pieces)):
            result = jnp.where(index == n, pieces[n], result)
        return result

    def gather_ff(value):
        pieces = [value]
        for bit in ff_bits:
            pieces += [swap(piece, bit) for piece in pieces]
        return pieces

    def sum_ff(pieces):
        while len(pieces) > 1:
            half = len(pieces) // 2
            bit = ff_bits[half.bit_length() - 1]
            pieces = [
                piece + swap(other, bit) for piece, other in zip(pieces[:half], pieces[half:], strict=True)
            ]
        return pieces[0]

    def sum_all(value):
        for k in range(devices.bit_length() - 1):
            value = value + swap(value, 1 << k)
        return value

    columns = query_key_value_weight.shape[1]
    feature = lax.broadcasted_iota(jnp.int32, (1, padded), 1)

    def shard_columns(owner, holder):
        found = []
        for part in range(3):
            column = part * width + holder * group + feature - columns * owner
            valid = (feature < group) & (holder * group + feature < width)
            found.append(jnp.where(valid & (column >= 0) & (column < columns), column, -1))
        return found

    def to_block(packed):
        parts = []
        for part in range(3):
            chosen = jnp.zeros_like(packed[0])
            for r in range(tp_count):
                chosen = jnp.where(shard_columns(t ^ r, t)[part] >= 0, packed[r], chosen)
            parts.append(chosen.reshape(-1, pairs, 1, LANES))
        return jnp.concatenate(parts, 2).reshape(-1, 3 * padded)

    def from_block(value):
        value = value.reshape(-1, pairs, 3, LANES)
        packed = []
        for r in range(tp_count):
            chosen = jnp.zeros((value.shape[0], padded), value.dtype)
            for part in range(3):
                here = shard_columns(t ^ r, t)[part] >= 0
                chosen = jnp.where(here, value[:, :, part].reshape(-1, padded), chosen)
            packed.append(chosen)
        return packed

    shard_index = lax.broadcasted_iota(jnp.int32, (columns, 1), 0)
    pick = []
    for r in range(tp_count):
        first, second, third = shard_columns(t, t ^ r)
        pick.append((shard_index == jnp.maximum(jnp.maximum(first, second), third)).astype(BF16))
    pick = jnp.concatenate(pick, 1)
    packed = dot(query_key_value_weight, pick).astype(BF16)
    packed = [packed[:, r * padded : (r + 1) * padded] for r in range(tp_count)]
    packed = [packed[0]] + [swap(packed[r], r) for r in range(1, tp_count)]

    flat = tokens.reshape(-1, width)
    gain_one, shift_one = ln1_gain.astype(F32), ln1_bias.astype(F32)
    gain_two, shift_two = ln2_gain.astype(F32), ln2_bias.astype(F32)
    normal_own = norm_forward(flat.astype(F32), gain_one, shift_one)
    packed[-1] = after(packed[-1], normal_own)
    qkv_rows = to_block(packed)
    qkv_weight = lax.all_gather(qkv_rows, "seq", axis=0, tiled=True)

    def head_columns(vector):
        whole = jnp.pad(vector, (0, tp_count * group - width))
        mine = lax.dynamic_slice_in_dim(whole, t * group, group)
        return jnp.pad(mine, (0, padded - group)).reshape(pairs, LANES)

    query_bias, value_bias = head_columns(qv_bias[0]), head_columns(qv_bias[1])
    qkv_bias = jnp.stack([query_bias, jnp.zeros_like(query_bias), value_bias], 1).reshape(-1)

    place = positions.reshape(chunks, tp_count, 2, span)[:, :, 0, 0] // span
    place = jnp.take(place, peers, axis=1)
    turned = (place >= tp_count).astype(jnp.int32)
    pair = jnp.minimum(place, 2 * tp_count - 1 - place)
    holds = pair[:, None, :] == jnp.arange(tp_count)[None, :, None]
    holder = jnp.sum(jnp.where(holds, jnp.arange(tp_count), 0), 2)
    orders = jnp.concatenate([holder, jnp.sum(jnp.where(holds, turned[:, None, :], 0), 2)], 1).astype(jnp.int32)
    places = jnp.concatenate([pair, turned], 1).astype(jnp.int32)
    masks = tuple(ff_bits)
    members = 1 << len(masks)

    stays = core == t // high
    block = t % high + core * high
    send = [
        (s * tp_count + i, s * tp_count + (i ^ high))
        for s in range(seq_count)
        for i in range(tp_count)
        if s % 2 == i // high
    ]

    def gather_seq(shard):
        return lax.all_gather(shard, "seq", axis=0, tiled=True)

    def take_block(whole):
        return lax.ppermute(whole, both, send)

    def give_block(partial):
        return lax.ppermute(partial, both, [(b, a) for a, b in send])

    def keep_block(partial, other):
        return jnp.where(stays, partial.astype(F32) + other, 0.0).astype(BF16)

    def sum_seq(partial):
        return after(lax.psum_scatter(partial, "seq", scatter_dimension=0, tiled=True))

    shards = [attention_output_weight] + [swap(attention_output_weight, r) for r in range(1, tp_count)]
    out_row = jnp.concatenate([choose(shards, t ^ a) for a in range(tp_count)], 1)
    normal_one = gather_rows(after(normal_own, out_row, qkv_rows), chunks, tp_count)
    expand_whole = gather_seq(expand_weight)
    contract_whole = gather_seq(after(contract_weight.T, normal_one))
    hidden_bias = lax.dynamic_slice_in_dim(expand_bias, block * hidden, hidden).astype(F32)

    out_weight = gather_seq(after(out_row, normal_one))

    qkv, heads_out, lse, output_rows, expand_other = call_forward(
        orders,
        places,
        normal_one,
        qkv_weight,
        qkv_bias.astype(F32).reshape(1, -1),
        cotangent.reshape(-1, width),
        expand_whole,
        tp_count,
        group_heads,
        masks,
    )
    pieces = [heads_out[r, :, :group] for r in range(tp_count)]
    mixed = jnp.concatenate([choose(pieces, t ^ a) for a in range(tp_count)], 1)[:, :width]
    residual = flat.astype(F32) + dot(mixed, out_weight) + attention_output_bias
    normal = norm_forward(residual, gain_two, shift_two)

    def second_norm_back(norm_grad):
        from_norm, gain_two_grad, shift_two_grad = norm_backward(residual, gain_two, norm_grad)
        resid_grad = cotangent.reshape(-1, width).astype(F32) + from_norm
        branch = resid_grad.astype(BF16)
        head_grad = dot(branch, out_weight, NT).astype(BF16)
        head_grad = jnp.pad(head_grad, ((0, 0), (0, tp_count * group - width)))
        pieces = [head_grad[:, a * group : (a + 1) * group] for a in range(tp_count)]
        pieces = [jnp.pad(choose(pieces, t ^ r), ((0, 0), (0, padded - group))) for r in range(tp_count)]
        out_part = dot(mixed, branch, TN).astype(BF16)
        out_grad = sum_seq(out_part)
        return gain_two_grad, shift_two_grad, resid_grad, branch, jnp.stack(pieces), out_grad

    flat_rows = output_rows.reshape(-1, width)
    if tp_count == 4:
        normal_two, value, slope, contract_other = call_hidden(
            normal,
            expand_whole,
            expand_other,
            hidden_bias.reshape(1, -1),
            contract_whole,
            chunks,
            tp_count,
            masks,
        )
        value = value.reshape(-1, hidden)
        contract_grad = dot(flat_rows, value, TN).astype(BF16)
        contract_grad, norm_grad, hidden_grad, hidden_bias_grad = call_group(
            tp_count,
            masks,
            True,
            [output_rows, slope],
            [contract_whole, contract_other, expand_whole, expand_other],
            [],
            contract_grad,
        )
        proj_weight_grad = sum_seq(contract_grad)
        normal_two, hidden_grad = normal_two.reshape(-1, width), hidden_grad.reshape(-1, hidden)
        expand_grad = dot(normal_two, after(hidden_grad, contract_grad), TN).astype(BF16)
        from_second = second_norm_back(norm_grad)

        def group_forward(expand_grad):
            return call_group(
                tp_count,
                masks,
                False,
                [value.reshape(members, chunks, rows, hidden)],
                [contract_whole, contract_other],
                [residual, contract_bias.astype(F32).reshape(1, -1)],
                expand_grad,
            )

    else:
        expand = jnp.where(stays, expand_whole, expand_other)
        contract = jnp.where(stays, contract_whole, take_block(contract_whole))
        normal_two = jnp.concatenate(gather_ff(normal), 0)
        value, slope = gelu_pair(dot(normal_two, expand) + hidden_bias)
        value = value.astype(BF16)
        contract_grad = dot(flat_rows, value, TN).astype(BF16)
        hidden_grad = (dot(flat_rows, contract) * slope).astype(BF16)
        partial = dot(hidden_grad, expand, NT).astype(BF16).reshape(members, -1, width)
        hidden_bias_grad = jnp.sum(hidden_grad, 0, dtype=F32)
        from_second = second_norm_back(sum_ff([partial[d] for d in range(members)]).astype(F32))
        proj_weight_grad = sum_seq(keep_block(contract_grad, give_block(contract_grad)))
        expand_grad = dot(normal_two, hidden_grad, TN).astype(BF16)

        def group_forward(expand_grad):
            members_value = value.reshape(members, -1, hidden)
            feed = [dot(members_value[d], contract, NT).astype(BF16) for d in range(members)]
            kept = keep_block(expand_grad, give_block(expand_grad))
            return kept, (residual + sum_ff(feed) + contract_bias).astype(BF16)


    gain_two_grad, shift_two_grad, resid_grad, branch, head_grads, out_grad = from_second
    _, one_grad, qkv_grad, qkv_bias_grad = call_backward(
        orders,
        places,
        after(qkv, expand_grad),
        head_grads,
        lse,
        qkv_weight,
        normal_one,
        tp_count,
        group_heads,
    )
    qkv_grad = after(qkv_grad, proj_weight_grad, out_grad)
    out_grad = [out_grad[:, a * (width // tp_count) : (a + 1) * (width // tp_count)] for a in range(tp_count)]
    out_weight_grad = choose(out_grad, t).astype(F32)
    for r in range(1, tp_count):
        out_weight_grad = out_weight_grad + swap(choose(out_grad, t ^ r), r)


    summed = lax.psum_scatter(qkv_grad, "seq", scatter_dimension=0, tiled=True)
    expand_grad, layer_out = group_forward(after(expand_grad, qkv_grad))
    expand_grad = after(expand_grad, summed)
    fc_weight_grad = sum_seq(expand_grad)

    packed = from_block(after(summed, expand_grad))
    one_grad = after(one_grad, packed[-1])
    packed = [packed[0]] + [swap(packed[r], r) for r in range(1, tp_count)]
    qkv_weight_grad = dot(jnp.concatenate(packed, 1), pick, NT)
    from_norm, gain_one_grad, shift_one_grad = norm_backward(flat.astype(F32), gain_one, one_grad)
    input_grad = (resid_grad + from_norm).astype(BF16).reshape(tokens.shape)
    qkv_bias_grad = qkv_bias_grad.reshape(pairs, 3, LANES)

    def whole_bias(part):
        mine = qkv_bias_grad[:, part].reshape(-1)[:group]
        whole = jnp.zeros((tp_count * group,), F32)
        return lax.dynamic_update_slice_in_dim(whole, mine, t * group, 0)[:width]

    hidden_whole = lax.dynamic_update_slice_in_dim(
        jnp.zeros(expand_bias.shape, F32), hidden_bias_grad.reshape(-1), block * hidden, 0
    )
    out_bias_part = jnp.sum(branch, 0, dtype=F32)
    proj_bias_part = jnp.sum(cotangent, axis=(0, 1), dtype=F32)
    vector = sum_all(
        jnp.concatenate(
            [
                gain_two_grad,
                shift_two_grad,
                out_bias_part,
                proj_bias_part,
                gain_one_grad,
                shift_one_grad,
                whole_bias(0),
                whole_bias(2),
                hidden_whole,
            ]
        )
    )
    def part(vector, index):
        return vector[index * width : (index + 1) * width]

    return (
        layer_out.reshape(tokens.shape),
        input_grad,
        part(vector, 4),
        part(vector, 5),
        qkv_weight_grad,
        vector[6 * width : 8 * width].reshape(2, width),
        out_weight_grad,
        part(vector, 2),
        part(vector, 0),
        part(vector, 1),
        fc_weight_grad.astype(F32),
        vector[8 * width :],
        proj_weight_grad.astype(F32).T,
        part(vector, 3),
    )


def solution(mesh):
    in_specs = (
        P("seq", "tp", None),
        P("seq", None),
        P(),
        P(),
        P("seq", "tp"),
        P(),
        P("seq", "tp"),
        P(),
        P(),
        P(),
        P("seq", "tp"),
        P(),
        P("tp", "seq"),
        P(),
        P("seq", "tp", None),
    )
    out_specs = (
        P("seq", "tp", None),
        P("seq", "tp", None),
        P(),
        P(),
        P("seq", "tp"),
        P(),
        P("seq", "tp"),
        P(),
        P(),
        P(),
        P("seq", "tp"),
        P(),
        P("tp", "seq"),
        P(),
    )
    placed = functools.partial(body, mesh.shape["seq"], mesh.shape["tp"])
    return jax.shard_map(placed, mesh=mesh, in_specs=in_specs, out_specs=out_specs, check_vma=False)
```

```python
import functools
import jax
import jax.numpy as jnp
from jax import lax
from jax.experimental import pallas as pl
from jax.experimental.pallas import tpu as pltpu
from jax.sharding import PartitionSpec as P

HEADS = 25
HEAD = 64
LANES = 128
TILE = 256
epsilon = 1e-05
F32 = jnp.float32
BF16 = jnp.bfloat16
NN = (((1,), (0,)), ((), ()))
NT = (((1,), (1,)), ((), ()))
TN = (((0,), (0,)), ((), ()))
MIB = 2**20
VMEM = pl.BlockSpec(memory_space=pltpu.VMEM)
SMEM = pl.BlockSpec(memory_space=pltpu.SMEM)
FAR = pl.BlockSpec(memory_space=pl.ANY)


def dot(left, right, dims=NN):
    return lax.dot_general(left, right, dims, preferred_element_type=F32)


def peer_id(count, mask):
    if mask < count:
        return {"tp": lax.axis_index("tp") ^ mask}
    if mask == count:
        return {"seq": lax.axis_index("seq") ^ 1}
    return {"seq": lax.axis_index("seq") ^ 1, "tp": lax.axis_index("tp") ^ (mask - count)}


def meet(count, masks):
    barrier = pltpu.get_barrier_semaphore()
    for mask in masks:
        pl.semaphore_signal(barrier, inc=1, device_id=peer_id(count, mask), device_id_type=pl.DeviceIdType.MESH)
    pl.semaphore_wait(barrier, len(masks))


def remote(count, source, target, send, recv, mask):
    return pltpu.make_async_remote_copy(
        src_ref=source,
        dst_ref=target,
        send_sem=send,
        recv_sem=recv,
        device_id=peer_id(count, mask),
        device_id_type=pl.DeviceIdType.MESH,
    )


def block_stays(count):
    return lax.rem(lax.axis_index("seq"), 2) == lax.axis_index("tp") // (count // 2)


def pass_block(count, source, target, sems):
    return remote(count, source, target, sems.at[0], sems.at[1], count // 2)


def when(condition, action):
    pl.when(condition)(action)


def gather_kernel(count, tokens, own_ref, rows_ref, send_sems, recv_sems, local_sems):
    chunks = rows_ref.shape[0]
    span = tokens // 2
    direct_peers = (1, 2) if count == 4 else tuple(range(1, count))
    meet(count, direct_peers)

    def own(c):
        return pltpu.make_async_copy(
            own_ref.at[pl.ds(c * tokens, tokens)], rows_ref.at[c, pl.ds(0, tokens)], local_sems.at[c]
        )

    def direct(c, r):
        return remote(
            count,
            own_ref.at[pl.ds(c * tokens, tokens)],
            rows_ref.at[c, pl.ds(r * tokens, tokens)],
            send_sems.at[c, r],
            recv_sems.at[c, r],
            r,
        )

    def passed(c, half):
        start = (tokens, 2 * tokens + span)[half]
        return remote(
            count,
            rows_ref.at[c, pl.ds(start, span)],
            rows_ref.at[c, pl.ds(3 * tokens + half * span, span)],
            send_sems.at[c, 3 * half],
            recv_sems.at[c, 3 * half],
            2 - half,
        )

    for c in range(chunks):
        own(c).start()
        for r in direct_peers:
            direct(c, r).start()
    for c in range(chunks):
        for r in direct_peers:
            direct(c, r).wait_recv()
        if count == 4:
            passed(c, 0).start()
            passed(c, 1).start()
    for c in range(chunks):
        own(c).wait()
        for r in direct_peers:
            direct(c, r).wait_send()
        if count == 4:
            passed(c, 0).wait()
            passed(c, 1).wait()


def gather_rows(own, chunks, count):
    tokens = own.shape[0] // chunks
    return pl.pallas_call(
        functools.partial(gather_kernel, count, tokens),
        in_specs=[FAR],
        out_specs=FAR,
        out_shape=jax.ShapeDtypeStruct((chunks, tokens * count, own.shape[1]), BF16),
        scratch_shapes=[pltpu.SemaphoreType.DMA((chunks, count))] * 2 + [pltpu.SemaphoreType.DMA((chunks,))],
        compiler_params=pltpu.CompilerParams(collective_id=1, has_side_effects=True),
        cost_estimate=pl.CostEstimate(flops=0, bytes_accessed=120 * MIB, transcendentals=0),
        name="gather_rows",
    )(own)


def pick_one(index, options):
    result = options(0)
    for n in range(1, index[1]):
        result = lax.select(index[0] == n, options(n), result)
    return result


def to_places(count, span, holder, turned, source, target):
    for p in range(count):
        piece = pick_one((holder(p), count), source)
        first, second = piece[:span], piece[span:]
        swap = turned(p) == 1
        high = 2 * count - 1 - p
        target[p * span : (p + 1) * span, :] = lax.select(swap, second, first)
        target[high * span : (high + 1) * span, :] = lax.select(swap, first, second)


def from_places(count, span, pair, turned, source, store):
    for r in range(count):
        low = pick_one((pair(r), count), lambda p: source[p * span : (p + 1) * span, :])
        high = pick_one(
            (pair(r), count),
            lambda p: source[(2 * count - 1 - p) * span : (2 * count - p) * span, :],
        )
        swap = turned(r) == 1
        store(r, 0, lax.select(swap, high, low))
        store(r, 1, lax.select(swap, low, high))


def group_route(d):
    bit = d.bit_length() - 1
    return d - (1 << bit), bit


def forward_kernel(
    count,
    span,
    odd,
    masks,
    order_ref,
    place_ref,
    rows_ref,
    weight_ref,
    bias_ref,
    grad_ref,
    block_ref,
    qkv_ref,
    mixed_ref,
    lse_ref,
    group_ref,
    other_ref,
    rows,
    projected,
    outgoing,
    queries,
    keys,
    values,
    mixed,
    out_send,
    out_recv,
    group_send,
    group_recv,
    local_sems,
    block_sems,
):
    stays = block_stays(count)
    chunks, length, _ = rows.shape
    pairs = weight_ref.shape[1] // (3 * LANES)
    tokens = 2 * span
    pieces = 1 << len(masks)

    def load_rows(c):
        return pltpu.make_async_copy(rows_ref.at[c], rows.at[c], local_sems.at[0, c])

    def save_qkv(c):
        return pltpu.make_async_copy(projected.at[c % 2], qkv_ref.at[c], local_sems.at[1, c])

    def keep(c):
        return pltpu.make_async_copy(
            outgoing.at[c, 0], mixed_ref.at[0, pl.ds(c * tokens, tokens)], local_sems.at[2, c]
        )

    def keep_grad(c):
        return pltpu.make_async_copy(
            grad_ref.at[pl.ds(c * tokens, tokens)], group_ref.at[0, c], local_sems.at[3, c]
        )

    def outward(c, r):
        return remote(
            count,
            outgoing.at[c, r],
            mixed_ref.at[r, pl.ds(c * tokens, tokens)],
            out_send.at[c, r],
            out_recv.at[c, r],
            r,
        )

    def grouped(c, d):
        origin, bit = group_route(d)
        source = grad_ref.at[pl.ds(c * tokens, tokens)] if origin == 0 else group_ref.at[origin, c]
        return remote(
            count, source, group_ref.at[d, c], group_send.at[c, d], group_recv.at[c, d], masks[bit]
        )

    for c in range(chunks):
        load_rows(c).start()
    meet(count, tuple(range(1, count)) + (count,))
    when(stays, lambda: pass_block(count, block_ref, other_ref, block_sems).start())
    for c in range(chunks):
        keep_grad(c).start()
        for d in range(1, pieces):
            if group_route(d)[0] == 0:
                grouped(c, d).start()

    @pl.loop(0, chunks)
    def _(c):
        load_rows(c).wait()

        @pl.when(c >= 2)
        def _():
            save_qkv(c - 2).wait()

        @pl.loop(0, pairs)
        def _(j):
            columns = pl.ds(pl.multiple_of(j * 3 * LANES, LANES), 3 * LANES)
            block = (dot(rows[c], weight_ref[:, columns]) + bias_ref[:, columns]).astype(BF16)
            projected[c % 2, :, columns] = block
            for part, target in enumerate((queries, keys, values)):
                to_places(
                    count,
                    span,
                    lambda p: order_ref[c, p],
                    lambda p: order_ref[c, count + p],
                    lambda r: block[r * tokens : (r + 1) * tokens, part * LANES : (part + 1) * LANES],
                    target,
                )

            def one_head(head):
                lane = lax.broadcasted_iota(jnp.int32, (TILE, LANES), 1)
                mine = (lane // HEAD) == head
                for first in range(0, length, TILE):
                    last = first + TILE
                    query = jnp.where(mine, queries[first:last, :] * BF16(HEAD**-0.5), BF16(0))
                    scores = dot(query, keys[0:last, :], NT)
                    row = lax.broadcasted_iota(jnp.int32, (TILE, TILE), 0)
                    column = lax.broadcasted_iota(jnp.int32, (TILE, TILE), 1)
                    corner = jnp.where(column <= row, scores[:, first:last], -1e30)
                    scores = corner if first == 0 else jnp.concatenate([scores[:, :first], corner], axis=1)
                    row_max = jnp.max(scores, 1, keepdims=True)
                    weights = jnp.exp(scores - row_max)
                    total = jnp.sum(weights, 1, keepdims=True)
                    part = dot(weights.astype(BF16), values[0:last, :]) / total
                    lse_ref[c, j, head, first:last] = (row_max + jnp.log(total))[:, 0]
                    if head == 0:
                        mixed[first:last, :] = jnp.where(mine, part, 0.0).astype(BF16)
                    else:
                        mixed[first:last, :] = jnp.where(mine, part.astype(BF16), mixed[first:last, :])

            one_head(0)
            if odd:
                pl.when(j < pairs - 1)(lambda: one_head(1))
            else:
                one_head(1)
            lanes = pl.ds(pl.multiple_of(j * LANES, LANES), LANES)

            def put(r, half, value):
                outgoing[c, r, half * span : (half + 1) * span, lanes] = value

            from_places(
                count, span, lambda r: place_ref[c, r], lambda r: place_ref[c, count + r], mixed, put
            )

        save_qkv(c).start()
        keep(c).start()
        for r in range(1, count):
            outward(c, r).start()

    for c in range(chunks):
        keep_grad(c).wait()
    for d in range(1, pieces):
        origin = group_route(d)[0]
        for c in range(chunks):
            if origin != 0:
                grouped(c, d).start()
        for c in range(chunks):
            grouped(c, d).wait()
    for c in range(chunks):
        keep(c).wait()
        for r in range(1, count):
            outward(c, r).wait()
    for c in range(max(chunks - 2, 0), chunks):
        save_qkv(c).wait()
    when(stays, lambda: pass_block(count, block_ref, other_ref, block_sems).wait_send())
    when(jnp.logical_not(stays), lambda: pass_block(count, block_ref, other_ref, block_sems).wait_recv())


def call_forward(order, place, rows, weight, bias, grad, block, count, heads, masks):
    chunks, length, width = rows.shape
    columns = weight.shape[1]
    pairs, tokens, pieces = columns // (3 * LANES), length // count, 1 << len(masks)
    return pl.pallas_call(
        functools.partial(forward_kernel, count, tokens // 2, heads % 2 == 1, masks),
        in_specs=[SMEM, SMEM, FAR, VMEM, VMEM, FAR, FAR],
        out_specs=[FAR, FAR, VMEM, FAR, FAR],
        out_shape=[
            jax.ShapeDtypeStruct((chunks, length, columns), BF16),
            jax.ShapeDtypeStruct((count, chunks * tokens, pairs * LANES), BF16),
            jax.ShapeDtypeStruct((chunks, pairs, 2, length), F32),
            jax.ShapeDtypeStruct((pieces, chunks, tokens, width), BF16),
            jax.ShapeDtypeStruct(block.shape, BF16),
        ],
        scratch_shapes=[
            pltpu.VMEM((chunks, length, width), BF16),
            pltpu.VMEM((2, length, columns), BF16),
            pltpu.VMEM((chunks, count, tokens, pairs * LANES), BF16),
        ]
        + [pltpu.VMEM((length, LANES), BF16)] * 4
        + [pltpu.SemaphoreType.DMA((chunks, count))] * 2
        + [pltpu.SemaphoreType.DMA((chunks, pieces))] * 2
        + [pltpu.SemaphoreType.DMA((4, chunks)), pltpu.SemaphoreType.DMA((2,))],
        compiler_params=pltpu.CompilerParams(
            collective_id=2, has_side_effects=True, vmem_limit_bytes=52 * MIB
        ),
        cost_estimate=pl.CostEstimate(
            flops=chunks * (2 * length * width * columns + heads * length * length * 5 * 256),
            bytes_accessed=80 * MIB,
            transcendentals=chunks * heads * length * length,
        ),
        name="attend_forward",
    )(order, place, rows, weight, bias, grad, block)


def backward_kernel(
    count,
    span,
    odd,
    order_ref,
    place_ref,
    qkv_ref,
    grad_ref,
    lse_ref,
    weight_ref,
    rows_ref,
    out_ref,
    sum_ref,
    product_ref,
    bias_ref,
    arrived,
    block,
    result,
    queries,
    keys,
    values,
    grads,
    query_grad,
    key_sum,
    value_sum,
    first_out,
    first_in,
    side,
    second_out,
    second_in,
    head_send,
    head_recv,
    first_send,
    first_recv,
    second_send,
    second_recv,
    local_sems,
    left,
    right,
    product,
    rounded_product,
    tile_sems,
    product_sem,
):
    chunks, length = out_ref.shape[:2]
    pairs = weight_ref.shape[1] // (3 * LANES)
    tokens = 2 * span

    def load_qkv(c):
        return pltpu.make_async_copy(qkv_ref.at[c], block.at[c % 2], local_sems.at[0, c])

    def load_own(c):
        return pltpu.make_async_copy(
            grad_ref.at[0, pl.ds(c * tokens, tokens)], arrived.at[c, 0], local_sems.at[1, c]
        )

    def save(c):
        return pltpu.make_async_copy(result, out_ref.at[c], local_sems.at[2, c])

    def inward(c, r):
        return remote(
            count,
            grad_ref.at[r, pl.ds(c * tokens, tokens)],
            arrived.at[c, r],
            head_send.at[c, r],
            head_recv.at[c, r],
            r,
        )

    def first(c, half):
        return remote(
            count,
            first_out.at[c, half],
            first_in.at[c, half],
            first_send.at[c, half],
            first_recv.at[c, half],
            2 - half,
        )

    def second(c, r):
        return remote(
            count,
            second_out.at[c, r - 1],
            second_in.at[c, r - 1],
            second_send.at[c, r - 1],
            second_recv.at[c, r - 1],
            r,
        )

    direct_peers = (1, 2) if count == 4 else tuple(range(1, count))

    def send_sums(c):
        if count == 4:
            first(c, 0).wait_recv()
            first(c, 1).wait_recv()
            second_out[c, 0, 0:span] = (side[0, 0:span] + first_in[c, 0].astype(F32)).astype(BF16)
            second_out[c, 0, span:tokens] = side[0, span:tokens].astype(BF16)
            second_out[c, 1, 0:span] = side[1, 0:span].astype(BF16)
            second_out[c, 1, span:tokens] = (side[1, span:tokens] + first_in[c, 1].astype(F32)).astype(
                BF16
            )
        for r in direct_peers:
            second(c, r).start()

    load_qkv(0).start()
    meet(count, tuple(range(1, count)))
    for c in range(chunks):
        load_own(c).start()
        for r in range(1, count):
            inward(c, r).start()

    @pl.loop(0, chunks)
    def _(c):
        load_qkv(c).wait()

        @pl.when(c < chunks - 1)
        def _():
            load_qkv(c + 1).start()

        load_own(c).wait()
        for r in range(1, count):
            inward(c, r).wait_recv()

        @pl.when(c >= 1)
        def _():
            save(c - 1).wait()

        @pl.loop(0, pairs)
        def _(j):
            @pl.when((j == pairs - 1) & (c >= 1))
            def _():
                send_sums(c - 1)

            def place(source, target):
                to_places(
                    count,
                    span,
                    lambda p: order_ref[c, p],
                    lambda p: order_ref[c, count + p],
                    source,
                    target,
                )

            for part, target in enumerate((queries, keys, values)):
                lanes = pl.ds(pl.multiple_of(j * 3 * LANES + part * LANES, LANES), LANES)
                place(lambda r: block[c % 2, r * tokens : (r + 1) * tokens, lanes], target)
            lanes = pl.ds(pl.multiple_of(j * LANES, LANES), LANES)
            place(lambda r: arrived[c, r, :, lanes], grads)

            def one_head(head):
                lane = lax.broadcasted_iota(jnp.int32, (TILE, LANES), 1)
                mine = (lane // HEAD) == head
                for first_row in reversed(range(0, length, TILE)):
                    last = first_row + TILE
                    query = jnp.where(mine, queries[first_row:last, :] * BF16(HEAD**-0.5), BF16(0))
                    grad = jnp.where(mine, grads[first_row:last, :], BF16(0))
                    scores = dot(query, keys[0:last, :], NT)
                    row = lax.broadcasted_iota(jnp.int32, (TILE, TILE), 0)
                    column = lax.broadcasted_iota(jnp.int32, (TILE, TILE), 1)
                    corner = jnp.where(column <= row, scores[:, first_row:last], -1e30)
                    scores = (
                        corner if first_row == 0 else jnp.concatenate([scores[:, :first_row], corner], axis=1)
                    )
                    weights = jnp.exp(scores - lse_ref[c, j, head, first_row:last][:, None])
                    prob_grad = dot(grad, values[0:last, :], NT)
                    product = weights * prob_grad
                    inner = jnp.sum(product, 1, keepdims=True)
                    score_grad = (product - weights * inner).astype(BF16)
                    rounded = weights.astype(BF16)
                    part = (dot(score_grad, keys[0:last, :]) * HEAD**-0.5).astype(BF16)
                    key_part = dot(query, score_grad, TN)
                    value_part = dot(grad, rounded, TN)
                    if head == 0 and last == length:
                        key_sum[...] = key_part
                        value_sum[...] = value_part
                    else:
                        key_sum[:, 0:last] += key_part
                        value_sum[:, 0:last] += value_part
                    if head == 0:
                        query_grad[first_row:last, :] = jnp.where(mine, part, BF16(0))
                    else:
                        query_grad[first_row:last, :] = jnp.where(mine, part, query_grad[first_row:last, :])

            one_head(0)
            if odd:
                pl.when(j < pairs - 1)(lambda: one_head(1))
            else:
                one_head(1)
            keys[...] = key_sum[...].T.astype(BF16)
            values[...] = value_sum[...].T.astype(BF16)
            for part, source in enumerate((query_grad, keys, values)):
                lanes = pl.ds(pl.multiple_of(j * 3 * LANES + part * LANES, LANES), LANES)

                def put(r, half, value):
                    start = r * tokens + half * span
                    result[start : start + span, lanes] = value

                from_places(
                    count, span, lambda r: place_ref[c, r], lambda r: place_ref[c, count + r], source, put
                )

        save(c).start()

        def share(first_piece, last_piece):
            return dot(result[first_piece * tokens : last_piece * tokens, :], weight_ref[...], NT)

        if count == 4:
            far = share(2, 4)
            first_out[c, 0] = far[tokens : tokens + span].astype(BF16)
            first_out[c, 1] = far[tokens + span :].astype(BF16)
            first(c, 0).start()
            first(c, 1).start()
            side[1] = far[:tokens]
            near = share(0, 2)
            side[0] = near[tokens:]
        else:
            for r in direct_peers:
                second_out[c, r - 1] = share(r, r + 1).astype(BF16)
            near = share(0, 1)
        sum_ref[pl.ds(pl.multiple_of(c * tokens, tokens), tokens), :] = near[:tokens]

    save(chunks - 1).wait()
    depth, third = left.shape[1], product.shape[1]
    tiles = length // depth
    rounds = chunks * tiles

    def load(n, side_index):
        c, k = lax.rem(n, rounds) // tiles, lax.rem(n, tiles)
        span_rows = pl.ds(pl.multiple_of(k * depth, depth), depth)
        slot = lax.rem(n, 2)
        if side_index == 0:
            source, target = rows_ref.at[c, span_rows], left.at[slot]
        else:
            lanes = pl.ds(pl.multiple_of(n // rounds * third, third), third)
            source, target = out_ref.at[c, span_rows, lanes], right.at[slot]
        return pltpu.make_async_copy(source, target, tile_sems.at[slot, side_index])

    def save_product(part):
        lanes = pl.ds(pl.multiple_of(part * third, third), third)
        return pltpu.make_async_copy(rounded_product, product_ref.at[:, lanes], product_sem.at[0])

    for side_index in range(2):
        load(0, side_index).start()

    @pl.loop(0, 3 * rounds)
    def _(n):
        slot = lax.rem(n, 2)
        part = n // rounds
        lanes = pl.ds(pl.multiple_of(part * third, third), third)
        for side_index in range(2):
            load(n, side_index).wait()

        @pl.when(n < 3 * rounds - 1)
        def _():
            for side_index in range(2):
                load(n + 1, side_index).start()

        @pl.when(n == rounds)
        def _():
            send_sums(chunks - 1)

        term = dot(left[slot], right[slot], TN)
        column_sum = jnp.sum(right[slot].astype(F32), 0, keepdims=True)

        @pl.when(lax.rem(n, rounds) == 0)
        def _():
            product[...] = term
            bias_ref[:, lanes] = column_sum

        @pl.when(lax.rem(n, rounds) != 0)
        def _():
            product[...] += term
            bias_ref[:, lanes] += column_sum

        @pl.when(lax.rem(n, rounds) == rounds - 1)
        def _():
            when(part >= 1, lambda: save_product(part - 1).wait())
            rounded_product[...] = product[...].astype(BF16)
            save_product(part).start()

    for c in range(chunks):
        total = sum_ref[c * tokens : (c + 1) * tokens, :]
        for r in direct_peers:
            second(c, r).wait_recv()
            total = total + second_in[c, r - 1].astype(F32)
        sum_ref[c * tokens : (c + 1) * tokens, :] = total
        for r in direct_peers:
            second(c, r).wait_send()
        if count == 4:
            first(c, 0).wait_send()
            first(c, 1).wait_send()
        for r in range(1, count):
            inward(c, r).wait_send()
    save_product(2).wait()


def call_backward(order, place, qkv, grads, lse, weight, rows, count, heads):
    chunks, length, columns = qkv.shape
    width = weight.shape[0]
    pairs, tokens = columns // (3 * LANES), length // count
    sides = 2 if count == 4 else count - 1
    return pl.pallas_call(
        functools.partial(backward_kernel, count, tokens // 2, heads % 2 == 1),
        in_specs=[SMEM, SMEM, FAR, FAR, VMEM, VMEM, FAR],
        out_specs=[FAR, VMEM, FAR, VMEM],
        out_shape=[
            jax.ShapeDtypeStruct((chunks, length, columns), BF16),
            jax.ShapeDtypeStruct((chunks * tokens, width), F32),
            jax.ShapeDtypeStruct((width, columns), BF16),
            jax.ShapeDtypeStruct((1, columns), F32),
        ],
        scratch_shapes=[
            pltpu.VMEM((chunks, count, tokens, pairs * LANES), BF16),
            pltpu.VMEM((2, length, columns), BF16),
            pltpu.VMEM((length, columns), BF16),
        ]
        + [pltpu.VMEM((length, LANES), BF16)] * 5
        + [pltpu.VMEM((LANES, length), F32)] * 2
        + [
            pltpu.VMEM((chunks, 2, tokens // 2, width), BF16),
            pltpu.VMEM((chunks, 2, tokens // 2, width), BF16),
            pltpu.VMEM((2, tokens, width), F32),
            pltpu.VMEM((chunks, sides, tokens, width), BF16),
            pltpu.VMEM((chunks, sides, tokens, width), BF16),
        ]
        + [pltpu.SemaphoreType.DMA((chunks, count))] * 2
        + [pltpu.SemaphoreType.DMA((chunks, 2))] * 2
        + [pltpu.SemaphoreType.DMA((chunks, sides))] * 2
        + [
            pltpu.SemaphoreType.DMA((3, chunks)),
            pltpu.VMEM((2, 2 * tokens, width), BF16),
            pltpu.VMEM((2, 2 * tokens, columns // 3), BF16),
            pltpu.VMEM((width, columns // 3), F32),
            pltpu.VMEM((width, columns // 3), BF16),
            pltpu.SemaphoreType.DMA((2, 2)),
            pltpu.SemaphoreType.DMA((1,)),
        ],
        compiler_params=pltpu.CompilerParams(
            collective_id=3, has_side_effects=True, vmem_limit_bytes=60 * MIB
        ),
        cost_estimate=pl.CostEstimate(
            flops=chunks * (2 * length * width * columns + heads * length * length * 8 * 256),
            bytes_accessed=80 * MIB,
            transcendentals=chunks * heads * length * length,
        ),
        name="attend_backward",
    )(order, place, qkv, grads, lse, weight, rows)


def gelu_pair(u):
    scale = 0.7978845608028654
    square = u * u
    inner = jnp.tanh(u * (scale + scale * 0.044715 * square))
    half = 0.5 + 0.5 * inner
    slope = half + u * (half * (1.0 - inner)) * (scale + scale * 0.134145 * square)
    return u * half, slope


def load_block(stays, whole_ref, other_ref, weight, sem, start):
    if start:
        when(stays, lambda: pltpu.make_async_copy(whole_ref, weight, sem).start())
        when(jnp.logical_not(stays), lambda: pltpu.make_async_copy(other_ref, weight, sem).start())
    else:
        pltpu.make_async_copy(whole_ref, weight, sem).wait()


def hidden_kernel(
    count, masks, own_ref, whole_ref, other_ref, bias_ref, block_ref, rows_ref, value_ref, slope_ref, moved_ref,
    rows, staged, weight, group_send, group_recv, local_sems, save_sems, weight_sem, block_sems,
):
    stays = block_stays(count)
    chunks, pieces, tokens, width = rows.shape

    def keep(c):
        return pltpu.make_async_copy(own_ref.at[pl.ds(c * tokens, tokens)], rows.at[c, 0], local_sems.at[0, c])

    def save_rows(c):
        return pltpu.make_async_copy(rows.at[c], rows_ref.at[c], local_sems.at[1, c])

    def grouped(c, d):
        origin, bit = group_route(d)
        source = own_ref.at[pl.ds(c * tokens, tokens)] if origin == 0 else rows.at[c, origin]
        return remote(count, source, rows.at[c, d], group_send.at[c, d], group_recv.at[c, d], masks[bit])

    def save(n, part):
        c, i = n // pieces, n % pieces
        p = (i % 2) * 2 + i // 2
        target = value_ref.at[p, c] if part == 0 else slope_ref.at[c, p]
        return pltpu.make_async_copy(staged.at[n % 2, part], target, save_sems.at[n % 2, part])

    load_block(stays, whole_ref, other_ref, weight, weight_sem.at[0], True)
    for c in range(chunks):
        keep(c).start()
    meet(count, masks + (count // 2,))
    for c in range(chunks):
        grouped(c, 1).start()
    for c in range(chunks):
        grouped(c, 2).start()
    when(stays, lambda: pass_block(count, block_ref, moved_ref, block_sems).start())
    load_block(stays, whole_ref, other_ref, weight, weight_sem.at[0], False)

    @pl.loop(0, chunks)
    def _(c):
        keep(c).wait()

        @pl.loop(0, pieces)
        def _(i):
            p = (i % 2) * 2 + i // 2
            step = c * pieces + i

            @pl.when(i == 1)
            def _():
                grouped(c, 2).wait_recv()

            @pl.when(i == 2)
            def _():
                grouped(c, 1).wait_recv()
                grouped(c, 3).start()

            @pl.when(i == 3)
            def _():
                grouped(c, 3).wait_recv()
                save_rows(c).start()

            value, slope = gelu_pair(dot(rows[c, p], weight[...]) + bias_ref[...])

            @pl.when(step >= 2)
            def _():
                for part in range(2):
                    save(step - 2, part).wait()

            staged[step % 2, 0] = value.astype(BF16)
            staged[step % 2, 1] = slope.astype(BF16)
            for part in range(2):
                save(step, part).start()

    for c in range(chunks):
        save_rows(c).wait()
        for d in range(1, pieces):
            grouped(c, d).wait_send()
    for step in range(chunks * pieces - 2, chunks * pieces):
        for part in range(2):
            save(step, part).wait()
    when(stays, lambda: pass_block(count, block_ref, moved_ref, block_sems).wait_send())
    when(jnp.logical_not(stays), lambda: pass_block(count, block_ref, moved_ref, block_sems).wait_recv())


def call_hidden(own, whole, other, bias, block, chunks, count, masks):
    width, hidden = whole.shape
    tokens, pieces = own.shape[0] // chunks, 1 << len(masks)
    return pl.pallas_call(
        functools.partial(hidden_kernel, count, masks),
        in_specs=[FAR, FAR, FAR, VMEM, FAR],
        out_specs=[FAR] * 4,
        out_shape=[
            jax.ShapeDtypeStruct((chunks, pieces, tokens, width), BF16),
            jax.ShapeDtypeStruct((pieces, chunks, tokens, hidden), BF16),
            jax.ShapeDtypeStruct((chunks, pieces, tokens, hidden), BF16),
            jax.ShapeDtypeStruct(block.shape, BF16),
        ],
        scratch_shapes=[
            pltpu.VMEM((chunks, pieces, tokens, width), BF16),
            pltpu.VMEM((2, 2, tokens, hidden), BF16),
            pltpu.VMEM((width, hidden), BF16),
            pltpu.SemaphoreType.DMA((chunks, pieces)),
            pltpu.SemaphoreType.DMA((chunks, pieces)),
            pltpu.SemaphoreType.DMA((2, chunks)),
            pltpu.SemaphoreType.DMA((2, 2)),
            pltpu.SemaphoreType.DMA((1,)),
            pltpu.SemaphoreType.DMA((2,)),
        ],
        compiler_params=pltpu.CompilerParams(
            collective_id=4, has_side_effects=True, vmem_limit_bytes=44 * MIB
        ),
        cost_estimate=pl.CostEstimate(
            flops=2 * chunks * pieces * tokens * width * hidden, bytes_accessed=100 * MIB, transcendentals=0
        ),
        name="hidden_forward",
    )(own, whole, other, bias, block)


def group_kernel(count, masks, backward, *refs):
    if backward:
        grad_ref, slope_ref, *blocks, part_ref, other_ref, sum_ref, out_ref, bias_ref, staged, contract = refs[:13]
        sources = (grad_ref, slope_ref)
        targets = (contract, refs[13])
        scratch = refs[13:]
    else:
        value_ref, *blocks, residual_ref, bias_ref, part_ref, other_ref, sum_ref = refs[:8]
        sources = (value_ref,)
        targets = (refs[8],)
        scratch = refs[8:]
    weight, loaded, partial, from_core, over, from_side = scratch[:6]
    core_send, core_recv, side_send, side_recv, cargo_sems, load_sems, save_sems, weight_sems, held = scratch[6:]
    chunks, tokens, _ = over.shape
    steps = 4 * chunks
    high = count // 2
    stays = block_stays(count)

    def place(step):
        return lax.rem(step, 2 * chunks) // 2, 3 - step // (2 * chunks) - 2 * lax.rem(step, 2)

    def load(step, part):
        c, p = place(step)
        slot = lax.rem(step, 2)
        source = sources[part].at[p, c] if part == 0 else sources[part].at[c, p]
        return pltpu.make_async_copy(source, loaded.at[slot, part], load_sems.at[slot, part])

    def save(step):
        c, p = place(step)
        slot = lax.rem(step, 2)
        return pltpu.make_async_copy(staged.at[slot], out_ref.at[c, p], save_sems.at[slot])

    def to_core(c, p):
        return remote(
            count, partial.at[c, p], from_core.at[c, p - 2], core_send.at[c, p - 2], core_recv.at[c, p - 2], masks[1]
        )

    def to_side(c):
        return remote(count, over.at[c], from_side.at[c], side_send.at[c], side_recv.at[c], masks[0])

    def put_sum(value):
        bias_ref[...] = value

    def cargo():
        return remote(count, part_ref, other_ref, cargo_sems.at[0], cargo_sems.at[1], count + high)

    def take_part():
        return pltpu.make_async_copy(part_ref, held, cargo_sems.at[0])

    def keep_part():
        return pltpu.make_async_copy(held, other_ref, cargo_sems.at[1])

    def load_blocks(start):
        for n, target in enumerate(targets):
            load_block(stays, blocks[2 * n], blocks[2 * n + 1], target, weight_sems.at[n], start)

    load_blocks(True)
    for part in range(len(sources)):
        load(0, part).start()
    meet(count, masks + (count + high,))
    when(stays, lambda: take_part().start())
    when(jnp.logical_not(stays), lambda: cargo().start())
    load_blocks(False)
    when(stays, lambda: take_part().wait())
    when(stays, lambda: keep_part().start())

    @pl.loop(0, steps)
    def _(step):
        c, p = place(step)
        slot = lax.rem(step, 2)
        for part in range(len(sources)):
            load(step, part).wait()

        @pl.when(step < steps - 1)
        def _():
            for part in range(len(sources)):
                load(step + 1, part).start()

        @pl.when((slot == 0) & (step >= 2) & (step <= 2 * chunks))
        def _():
            before = step // 2 - 1
            to_core(before, 3).wait_recv()
            over[before] = (partial[before, 1].astype(F32) + from_core[before, 1].astype(F32)).astype(BF16)
            to_side(before).start()

        if backward:
            hidden = dot(loaded[slot, 0], contract[...]) * loaded[slot, 1].astype(F32)
            hidden = hidden.astype(BF16)

            @pl.when(step >= 2)
            def _():
                save(step - 2).wait()

            staged[slot] = hidden
            save(step).start()
            column_sum = jnp.sum(hidden.astype(F32), 0, keepdims=True)
            when(step == 0, lambda: put_sum(column_sum))
            when(step > 0, lambda: put_sum(bias_ref[...] + column_sum))
        else:
            hidden = loaded[slot, 0]
        partial[c, p] = dot(hidden, weight[...], NT).astype(BF16)

        @pl.when(p >= 2)
        def _():
            to_core(c, p).start()

    for c in range(chunks):
        to_core(c, 2).wait_recv()
        to_side(c).wait_recv()
        total = partial[c, 0].astype(F32) + from_core[c, 0].astype(F32) + from_side[c].astype(F32)
        mine = slice(c * tokens, (c + 1) * tokens)
        if backward:
            sum_ref[mine, :] = total
        else:
            sum_ref[mine, :] = (residual_ref[mine, :] + total + bias_ref[...]).astype(BF16)
        to_core(c, 2).wait_send()
        to_core(c, 3).wait_send()
        to_side(c).wait_send()
    if backward:
        for step in range(steps - 2, steps):
            save(step).wait()

    when(stays, lambda: keep_part().wait())
    when(jnp.logical_not(stays), lambda: cargo().wait())


def call_group(count, masks, backward, tiles, blocks, rest, part):
    pieces, chunks, tokens, width = tiles[0].shape
    outs = [
        jax.ShapeDtypeStruct(part.shape, BF16),
        jax.ShapeDtypeStruct((chunks * tokens, width), F32 if backward else BF16),
    ]
    scratch = [
        pltpu.VMEM((width, width), BF16),
        pltpu.VMEM((2, len(tiles), tokens, width), BF16),
        pltpu.VMEM((chunks, pieces, tokens, width), BF16),
        pltpu.VMEM((chunks, 2, tokens, width), BF16),
        pltpu.VMEM((chunks, tokens, width), BF16),
        pltpu.VMEM((chunks, tokens, width), BF16),
        pltpu.SemaphoreType.DMA((chunks, 2)),
        pltpu.SemaphoreType.DMA((chunks, 2)),
        pltpu.SemaphoreType.DMA((chunks,)),
        pltpu.SemaphoreType.DMA((chunks,)),
        pltpu.SemaphoreType.DMA((2,)),
        pltpu.SemaphoreType.DMA((2, len(tiles))),
        pltpu.SemaphoreType.DMA((2,)),
        pltpu.SemaphoreType.DMA((2,)),
        pltpu.VMEM(part.shape, BF16),
    ]
    if backward:
        outs.append(jax.ShapeDtypeStruct((chunks, pieces, tokens, width), BF16))
        outs.append(jax.ShapeDtypeStruct((1, width), F32))
        scratch = [pltpu.VMEM((2, tokens, width), BF16), pltpu.VMEM((width, width), BF16)] + scratch
    return pl.pallas_call(
        functools.partial(group_kernel, count, masks, backward),
        in_specs=[FAR] * (len(tiles) + len(blocks)) + [VMEM] * len(rest) + [FAR],
        out_specs=[FAR, VMEM] + ([FAR, VMEM] if backward else []),
        out_shape=outs,
        scratch_shapes=scratch,
        compiler_params=pltpu.CompilerParams(
            collective_id=5 if backward else 6, has_side_effects=True, vmem_limit_bytes=56 * MIB
        ),
        cost_estimate=pl.CostEstimate(
            flops=(4 if backward else 2) * chunks * pieces * tokens * width * width,
            bytes_accessed=160 * MIB,
            transcendentals=0,
        ),
        name="group_backward" if backward else "group_forward",
    )(*tiles, *blocks, *rest, part)


def statistics(values):
    centred = values - jnp.mean(values, -1, keepdims=True)
    spread = jnp.mean(centred * centred, -1, keepdims=True)
    inverse = lax.rsqrt(spread + epsilon)
    return centred * inverse, inverse


def norm_forward(values, gain, shift):
    return (statistics(values)[0] * gain + shift).astype(BF16)


def norm_backward(values, gain, grad):
    normal, inverse = statistics(values)
    scaled = grad * gain
    spread = jnp.mean(scaled * normal, -1, keepdims=True)
    result = inverse * (scaled - jnp.mean(scaled, -1, keepdims=True) - normal * spread)
    return result, jnp.sum(grad * normal, 0), jnp.sum(grad, 0)


def body(
    seq_count,
    tp_count,
    tokens,
    positions,
    ln1_gain,
    ln1_bias,
    query_key_value_weight,
    qv_bias,
    attention_output_weight,
    attention_output_bias,
    ln2_gain,
    ln2_bias,
    expand_weight,
    expand_bias,
    contract_weight,
    contract_bias,
    cotangent,
):
    devices = seq_count * tp_count
    both = ("seq", "tp")
    t = lax.axis_index("tp")
    core = lax.axis_index("seq") % 2
    core_bit = tp_count
    tp_bits = [1 << k for k in range(tp_count.bit_length() - 1)]
    high = tp_bits[-1]
    ff_bits = tp_bits[:-1] + [core_bit]
    chunks, rows, width = tokens.shape
    span = rows // 2
    group_heads = -(-HEADS // tp_count)
    group = group_heads * HEAD
    pairs = -(-group_heads // 2)
    padded = pairs * LANES
    hidden = expand_weight.shape[1]
    peers = t ^ jnp.arange(tp_count)

    def swap(value, mask):
        return lax.ppermute(value, both, [(i, i ^ mask) for i in range(devices)])

    def after(value, *earlier):
        return lax.optimization_barrier((value, *earlier))[0]

    def choose(pieces, index):
        result = pieces[0]
        for n in range(1, len(pieces)):
            result = jnp.where(index == n, pieces[n], result)
        return result

    def gather_ff(value):
        pieces = [value]
        for bit in ff_bits:
            pieces += [swap(piece, bit) for piece in pieces]
        return pieces

    def sum_ff(pieces):
        while len(pieces) > 1:
            half = len(pieces) // 2
            bit = ff_bits[half.bit_length() - 1]
            pieces = [
                piece + swap(other, bit) for piece, other in zip(pieces[:half], pieces[half:], strict=True)
            ]
        return pieces[0]

    def sum_all(value):
        for k in range(devices.bit_length() - 1):
            value = value + swap(value, 1 << k)
        return value

    columns = query_key_value_weight.shape[1]
    feature = lax.broadcasted_iota(jnp.int32, (1, padded), 1)

    def shard_columns(owner, holder):
        found = []
        for part in range(3):
            column = part * width + holder * group + feature - columns * owner
            valid = (feature < group) & (holder * group + feature < width)
            found.append(jnp.where(valid & (column >= 0) & (column < columns), column, -1))
        return found

    def to_block(packed):
        parts = []
        for part in range(3):
            chosen = jnp.zeros_like(packed[0])
            for r in range(tp_count):
                chosen = jnp.where(shard_columns(t ^ r, t)[part] >= 0, packed[r], chosen)
            parts.append(chosen.reshape(-1, pairs, 1, LANES))
        return jnp.concatenate(parts, 2).reshape(-1, 3 * padded)

    def from_block(value):
        value = value.reshape(-1, pairs, 3, LANES)
        packed = []
        for r in range(tp_count):
            chosen = jnp.zeros((value.shape[0], padded), value.dtype)
            for part in range(3):
                here = shard_columns(t ^ r, t)[part] >= 0
                chosen = jnp.where(here, value[:, :, part].reshape(-1, padded), chosen)
            packed.append(chosen)
        return packed

    shard_index = lax.broadcasted_iota(jnp.int32, (columns, 1), 0)
    pick = []
    for r in range(tp_count):
        first, second, third = shard_columns(t, t ^ r)
        pick.append((shard_index == jnp.maximum(jnp.maximum(first, second), third)).astype(BF16))
    pick = jnp.concatenate(pick, 1)
    packed = dot(query_key_value_weight, pick).astype(BF16)
    packed = [packed[:, r * padded : (r + 1) * padded] for r in range(tp_count)]
    packed = [packed[0]] + [swap(packed[r], r) for r in range(1, tp_count)]

    flat = tokens.reshape(-1, width)
    gain_one, shift_one = ln1_gain.astype(F32), ln1_bias.astype(F32)
    gain_two, shift_two = ln2_gain.astype(F32), ln2_bias.astype(F32)
    normal_own = norm_forward(flat.astype(F32), gain_one, shift_one)
    packed[-1] = after(packed[-1], normal_own)
    qkv_rows = to_block(packed)
    qkv_weight = lax.all_gather(qkv_rows, "seq", axis=0, tiled=True)

    def head_columns(vector):
        whole = jnp.pad(vector, (0, tp_count * group - width))
        mine = lax.dynamic_slice_in_dim(whole, t * group, group)
        return jnp.pad(mine, (0, padded - group)).reshape(pairs, LANES)

    query_bias, value_bias = head_columns(qv_bias[0]), head_columns(qv_bias[1])
    qkv_bias = jnp.stack([query_bias, jnp.zeros_like(query_bias), value_bias], 1).reshape(-1)

    place = positions.reshape(chunks, tp_count, 2, span)[:, :, 0, 0] // span
    place = jnp.take(place, peers, axis=1)
    turned = (place >= tp_count).astype(jnp.int32)
    pair = jnp.minimum(place, 2 * tp_count - 1 - place)
    holds = pair[:, None, :] == jnp.arange(tp_count)[None, :, None]
    holder = jnp.sum(jnp.where(holds, jnp.arange(tp_count), 0), 2)
    orders = jnp.concatenate([holder, jnp.sum(jnp.where(holds, turned[:, None, :], 0), 2)], 1).astype(jnp.int32)
    places = jnp.concatenate([pair, turned], 1).astype(jnp.int32)
    masks = tuple(ff_bits)
    members = 1 << len(masks)

    stays = core == t // high
    block = t % high + core * high
    send = [
        (s * tp_count + i, s * tp_count + (i ^ high))
        for s in range(seq_count)
        for i in range(tp_count)
        if s % 2 == i // high
    ]

    def gather_seq(shard):
        return lax.all_gather(shard, "seq", axis=0, tiled=True)

    def take_block(whole):
        return lax.ppermute(whole, both, send)

    def give_block(partial):
        return lax.ppermute(partial, both, [(b, a) for a, b in send])

    def keep_block(partial, other):
        return jnp.where(stays, partial.astype(F32) + other, 0.0).astype(BF16)

    def sum_seq(partial):
        return after(lax.psum_scatter(partial, "seq", scatter_dimension=0, tiled=True))

    shards = [attention_output_weight] + [swap(attention_output_weight, r) for r in range(1, tp_count)]
    out_row = jnp.concatenate([choose(shards, t ^ a) for a in range(tp_count)], 1)
    normal_one = gather_rows(after(normal_own, out_row, qkv_rows), chunks, tp_count)
    expand_whole = gather_seq(expand_weight)
    contract_whole = gather_seq(after(contract_weight.T, normal_one))
    hidden_bias = lax.dynamic_slice_in_dim(expand_bias, block * hidden, hidden).astype(F32)

    out_weight = gather_seq(after(out_row, normal_one))

    qkv, heads_out, lse, output_rows, expand_other = call_forward(
        orders,
        places,
        normal_one,
        qkv_weight,
        qkv_bias.astype(F32).reshape(1, -1),
        cotangent.reshape(-1, width),
        expand_whole,
        tp_count,
        group_heads,
        masks,
    )
    pieces = [heads_out[r, :, :group] for r in range(tp_count)]
    mixed = jnp.concatenate([choose(pieces, t ^ a) for a in range(tp_count)], 1)[:, :width]
    residual = flat.astype(F32) + dot(mixed, out_weight) + attention_output_bias
    normal = norm_forward(residual, gain_two, shift_two)

    def second_norm_back(norm_grad):
        from_norm, gain_two_grad, shift_two_grad = norm_backward(residual, gain_two, norm_grad)
        resid_grad = cotangent.reshape(-1, width).astype(F32) + from_norm
        branch = resid_grad.astype(BF16)
        head_grad = dot(branch, out_weight, NT).astype(BF16)
        head_grad = jnp.pad(head_grad, ((0, 0), (0, tp_count * group - width)))
        pieces = [head_grad[:, a * group : (a + 1) * group] for a in range(tp_count)]
        pieces = [jnp.pad(choose(pieces, t ^ r), ((0, 0), (0, padded - group))) for r in range(tp_count)]
        out_part = dot(mixed, branch, TN).astype(BF16)
        out_grad = sum_seq(out_part)
        return gain_two_grad, shift_two_grad, resid_grad, branch, jnp.stack(pieces), out_grad

    flat_rows = output_rows.reshape(-1, width)
    if tp_count == 4:
        normal_two, value, slope, contract_other = call_hidden(
            normal,
            expand_whole,
            expand_other,
            hidden_bias.reshape(1, -1),
            contract_whole,
            chunks,
            tp_count,
            masks,
        )
        value = value.reshape(-1, hidden)
        contract_grad = dot(flat_rows, value, TN).astype(BF16)
        contract_grad, norm_grad, hidden_grad, hidden_bias_grad = call_group(
            tp_count,
            masks,
            True,
            [output_rows, slope],
            [contract_whole, contract_other, expand_whole, expand_other],
            [],
            contract_grad,
        )
        proj_weight_grad = sum_seq(contract_grad)
        normal_two, hidden_grad = normal_two.reshape(-1, width), hidden_grad.reshape(-1, hidden)
        from_second = second_norm_back(norm_grad)
        late_grad = after(hidden_grad, contract_grad, from_second[4])
        expand_grad = dot(normal_two, late_grad, TN).astype(BF16)

        def group_forward(expand_grad):
            return call_group(
                tp_count,
                masks,
                False,
                [value.reshape(members, chunks, rows, hidden)],
                [contract_whole, contract_other],
                [residual, contract_bias.astype(F32).reshape(1, -1)],
                expand_grad,
            )

    else:
        expand = jnp.where(stays, expand_whole, expand_other)
        contract = jnp.where(stays, contract_whole, take_block(contract_whole))
        normal_two = jnp.concatenate(gather_ff(normal), 0)
        value, slope = gelu_pair(dot(normal_two, expand) + hidden_bias)
        value = value.astype(BF16)
        contract_grad = dot(flat_rows, value, TN).astype(BF16)
        hidden_grad = (dot(flat_rows, contract) * slope).astype(BF16)
        partial = dot(hidden_grad, expand, NT).astype(BF16).reshape(members, -1, width)
        hidden_bias_grad = jnp.sum(hidden_grad, 0, dtype=F32)
        from_second = second_norm_back(sum_ff([partial[d] for d in range(members)]).astype(F32))
        proj_weight_grad = sum_seq(keep_block(contract_grad, give_block(contract_grad)))
        expand_grad = dot(normal_two, hidden_grad, TN).astype(BF16)

        def group_forward(expand_grad):
            members_value = value.reshape(members, -1, hidden)
            feed = [dot(members_value[d], contract, NT).astype(BF16) for d in range(members)]
            kept = keep_block(expand_grad, give_block(expand_grad))
            return kept, (residual + sum_ff(feed) + contract_bias).astype(BF16)


    gain_two_grad, shift_two_grad, resid_grad, branch, head_grads, out_grad = from_second
    _, one_grad, qkv_grad, qkv_bias_grad = call_backward(
        orders,
        places,
        after(qkv, expand_grad),
        head_grads,
        lse,
        qkv_weight,
        normal_one,
        tp_count,
        group_heads,
    )
    qkv_grad = after(qkv_grad, proj_weight_grad, out_grad)
    out_grad = [out_grad[:, a * (width // tp_count) : (a + 1) * (width // tp_count)] for a in range(tp_count)]
    out_weight_grad = choose(out_grad, t).astype(F32)
    for r in range(1, tp_count):
        out_weight_grad = out_weight_grad + swap(choose(out_grad, t ^ r), r)


    summed = lax.psum_scatter(qkv_grad, "seq", scatter_dimension=0, tiled=True)
    expand_grad, layer_out = group_forward(after(expand_grad, qkv_grad))
    expand_grad = after(expand_grad, summed)
    fc_weight_grad = sum_seq(expand_grad)

    packed = from_block(after(summed, expand_grad))
    one_grad = after(one_grad, packed[-1])
    packed = [packed[0]] + [swap(packed[r], r) for r in range(1, tp_count)]
    qkv_weight_grad = dot(jnp.concatenate(packed, 1), pick, NT)
    from_norm, gain_one_grad, shift_one_grad = norm_backward(flat.astype(F32), gain_one, one_grad)
    input_grad = (resid_grad + from_norm).astype(BF16).reshape(tokens.shape)
    qkv_bias_grad = qkv_bias_grad.reshape(pairs, 3, LANES)

    def whole_bias(part):
        mine = qkv_bias_grad[:, part].reshape(-1)[:group]
        whole = jnp.zeros((tp_count * group,), F32)
        return lax.dynamic_update_slice_in_dim(whole, mine, t * group, 0)[:width]

    hidden_whole = lax.dynamic_update_slice_in_dim(
        jnp.zeros(expand_bias.shape, F32), hidden_bias_grad.reshape(-1), block * hidden, 0
    )
    out_bias_part = jnp.sum(branch, 0, dtype=F32)
    proj_bias_part = jnp.sum(cotangent, axis=(0, 1), dtype=F32)
    vector = sum_all(
        jnp.concatenate(
            [
                gain_two_grad,
                shift_two_grad,
                out_bias_part,
                proj_bias_part,
                gain_one_grad,
                shift_one_grad,
                whole_bias(0),
                whole_bias(2),
                hidden_whole,
            ]
        )
    )
    def part(vector, index):
        return vector[index * width : (index + 1) * width]

    return (
        layer_out.reshape(tokens.shape),
        input_grad,
        part(vector, 4),
        part(vector, 5),
        qkv_weight_grad,
        vector[6 * width : 8 * width].reshape(2, width),
        out_weight_grad,
        part(vector, 2),
        part(vector, 0),
        part(vector, 1),
        fc_weight_grad.astype(F32),
        vector[8 * width :],
        proj_weight_grad.astype(F32).T,
        part(vector, 3),
    )


def solution(mesh):
    in_specs = (
        P("seq", "tp", None),
        P("seq", None),
        P(),
        P(),
        P("seq", "tp"),
        P(),
        P("seq", "tp"),
        P(),
        P(),
        P(),
        P("seq", "tp"),
        P(),
        P("tp", "seq"),
        P(),
        P("seq", "tp", None),
    )
    out_specs = (
        P("seq", "tp", None),
        P("seq", "tp", None),
        P(),
        P(),
        P("seq", "tp"),
        P(),
        P("seq", "tp"),
        P(),
        P(),
        P(),
        P("seq", "tp"),
        P(),
        P("tp", "seq"),
        P(),
    )
    placed = functools.partial(body, mesh.shape["seq"], mesh.shape["tp"])
    return jax.shard_map(placed, mesh=mesh, in_specs=in_specs, out_specs=out_specs, check_vma=False)
```
